32 devices in a mesh: layer: 4 (over y, x), row: 2 (over core), col: 4 (over z).
Axes of the slice: x: 2, y: 2, z: 4, core: 2. Of those that a mesh axis runs over, the one named last changes fastest.
Arguments:
- left_values: bfloat16 [4096, 4, 1024], P('row', 'layer', 'col'), may hold values from -22 to 22
- left_pattern: int32 [16, 4, 4], P('row', 'layer', 'col'), may hold values from 0 to 1, as said below
- right_values: bfloat16 [4096, 4, 1024], P(('layer', 'row'), None, 'col'), may hold values from -6 to 6
- right_pattern: int32 [16, 4, 4], P(('layer', 'row'), None, 'col'), may hold values from 0 to 1, as said below
Outputs:
- expanded: bfloat16 [4096, 4, 1024], P('row', 'layer', 'col')
The draws below stay inside these ranges and needn't reach their ends.
Inputs may be any that keep to these rules, and one draw needn't show every extreme that they name: `left_pattern`: 1 marks a stored tile, 0 an absent one. `right_pattern`: 1 marks a stored tile, 0 an absent one.
All inputs are finite; a program needn't handle non-finite values.
Results may differ from the reference program's by a relative error of at most 0.001.
Values may be sent and summed in bfloat16 or wider, within the bound.
No kernel may reach another device: no remote copies, remote signals or barrier semaphores. Data moves between devices by JAX's collectives and lax.ppermute only.
A program may use at most 64 MiB of HBM per device.

```python
import math
import jax
import jax.numpy as jnp

TILE = 256
N = 4096
N_LAYER = 4


def tile_pattern(key_base):
    tile_rows = N // TILE
    tile_cols = N // (N_LAYER * TILE)
    key_one, key_two = jax.random.split(key_base)
    density = jax.random.randint(key_one, (tile_rows, 1, 1), 20, 91)
    draws_int = jax.random.randint(key_two, (tile_rows, N_LAYER, tile_cols), 0, 100)
    return jnp.where(draws_int < density, 1, 0).astype(jnp.int32)


def draw_left_pattern(key, part):
    return tile_pattern(jax.random.fold_in(key, 11))


def draw_right_pattern(key, part):
    return tile_pattern(jax.random.fold_in(key, 23))


def draw_left_values(key, part):
    key_one, key_two = jax.random.split(jax.random.fold_in(key, 37), 2)
    shape_full = (N, N_LAYER, N // N_LAYER)
    position = jnp.arange(N, dtype=jnp.float32) / (N - 1)
    row_ramp = jnp.sqrt(1.0 + 2.0 * position)[:, None, None]
    spread = jnp.exp(jax.random.uniform(key_one, (N, 1, 1), jnp.float32) * math.log(math.sqrt(10.0)))
    sample = jnp.clip(jax.random.normal(key_two, shape_full, jnp.float32), -4.0, 4.0)
    return (sample * row_ramp * spread).astype(jnp.bfloat16)


def block_scale(stream_key, shape, shards, least, high):
    level = 1.0
    for dim, shards_of in shards:
        draws = jax.random.uniform(jax.random.fold_in(jax.random.fold_in(stream_key, 6), dim), (shards_of,), jnp.float32, least / len(shards), high / len(shards))
        level = level * jnp.repeat(jnp.exp(draws), shape[dim] // shards_of).reshape((-1,) + (1,) * (len(shape) - 1 - dim))
    return level


def noise(stream_key, extent, scale, bound, shards=(), held_as=jnp.bfloat16):
    loudness = block_scale(stream_key, extent, shards, -0.22, 0.18) if shards else 1.0
    result = jax.random.normal(stream_key, extent, jnp.float32) * scale * loudness
    return jnp.minimum(jnp.maximum(result, -bound), bound).astype(held_as)


def setup_inputs(seed: int = 0) -> dict:
    keys = jax.random.split(jax.random.key(seed), 5)
    return {
        "left_values": draw_left_values(jax.random.fold_in(keys[4], 71), 0),
        "left_pattern": draw_left_pattern(jax.random.fold_in(keys[4], 71), 0),
        "right_values": noise(keys[2], (N, N_LAYER, N // N_LAYER), 1.0, 6.0, ((0, 8), (2, 4))),
        "right_pattern": draw_right_pattern(jax.random.fold_in(keys[4], 71), 0),
    }


def expand_tiles(values, pattern):
    tile_rows, layers, tile_cols = pattern.shape
    tile_size = values.shape[0] // tile_rows
    blocks = values.reshape(tile_rows, tile_size, layers, tile_cols, tile_size)
    blocks = blocks * pattern[:, None, :, :, None].astype(values.dtype)
    return blocks.reshape(values.shape)


def reference(left_values, left_pattern, right_values, right_pattern):
    left_full = expand_tiles(left_values, left_pattern).reshape(N, N)
    right_full = expand_tiles(right_values, right_pattern).reshape(N, N)
    product = jnp.dot(left_full, right_full, preferred_element_type=jnp.float32)
    squared = product * product
    colmean = jnp.mean(squared, axis=0, keepdims=True)
    expanded = (squared / (colmean + 1e-6)).astype(jnp.bfloat16)
    return expanded.reshape(N, N_LAYER, N // N_LAYER)
```

```python
import functools

import jax
import jax.numpy as jnp
from jax import lax
from jax.experimental import pallas as pl
from jax.experimental.pallas import tpu as pltpu
from jax.sharding import PartitionSpec as P

TILE = 256
CHUNKS = 4
SCALE_ROWS = 16
CODE = 64.0
TOP = 32767.0
LEAST = 2.0**-100
VMEM = pl.BlockSpec(memory_space=pltpu.VMEM)
PARAMS = pltpu.CompilerParams(vmem_limit_bytes=40 * 1024 * 1024)


def partial_kernel(n_sources, n_layers, where, *refs):
    lefts = refs[:n_sources]
    right_ref, mine_ref, sent_ref = refs[n_sources:]
    rows = lefts[0].shape[0]
    for step in range(n_layers):
        layer = where[0] ^ step
        total = jnp.zeros((rows, right_ref.shape[3]), jnp.float32)
        for source in range(n_sources):
            start = pl.multiple_of(where[2 + 2 * source], TILE)
            total += jnp.dot(
                lefts[source][...],
                right_ref[where[1 + 2 * source], layer, pl.ds(start, TILE), :],
                preferred_element_type=jnp.float32,
            )
        if step == 0:
            mine_ref[...] = total
            continue
        top = jnp.maximum(jnp.max(jnp.abs(total), axis=0, keepdims=True), LEAST)
        code = jnp.ceil(jnp.log2(top) * CODE + 0.01)
        unit = jnp.exp2(code / -CODE) * TOP
        fixed = jnp.round(total * unit).astype(jnp.int32)
        sent_ref[step - 1, :rows, :] = fixed.astype(jnp.int16)
        codes = jnp.broadcast_to(code.astype(jnp.int32), (SCALE_ROWS, code.shape[1]))
        sent_ref[step - 1, rows:, :] = codes.astype(jnp.int16)


def partial_products(where, lefts, right, n_layers):
    rows, columns = lefts[0].shape[0], right.shape[3]
    return pl.pallas_call(
        functools.partial(partial_kernel, len(lefts), n_layers),
        out_shape=(
            jax.ShapeDtypeStruct((rows, columns), jnp.float32),
            jax.ShapeDtypeStruct((n_layers - 1, rows + SCALE_ROWS, columns), jnp.int16),
        ),
        in_specs=[pl.BlockSpec(memory_space=pltpu.SMEM)] + [VMEM] * (len(lefts) + 1),
        out_specs=(VMEM, VMEM),
        compiler_params=PARAMS,
        cost_estimate=pl.CostEstimate(
            flops=2 * rows * len(lefts) * TILE * columns * n_layers,
            bytes_accessed=right.size * 2 + rows * columns * 14,
            transcendentals=0,
        ),
    )(where, *lefts, right)


def combine_kernel(n_received, mine_ref, *refs):
    received, (squared_ref, sum_ref) = refs[:n_received], refs[n_received:]
    total = mine_ref[...]
    rows = total.shape[0]
    for block in received:
        code = block[rows:, :].astype(jnp.int32)[:1].astype(jnp.float32)
        unit = jnp.exp2(code / CODE) * (1.0 / TOP)
        total += block[:rows, :].astype(jnp.int32).astype(jnp.float32) * unit
    squared = total * total
    squared_ref[...] = squared
    sum_ref[...] = jnp.sum(squared, axis=0, keepdims=True)


def combine(mine, received):
    return pl.pallas_call(
        functools.partial(combine_kernel, len(received)),
        out_shape=(
            jax.ShapeDtypeStruct(mine.shape, jnp.float32),
            jax.ShapeDtypeStruct((1, mine.shape[1]), jnp.float32),
        ),
        in_specs=[VMEM] * (1 + len(received)),
        out_specs=(VMEM, VMEM),
        compiler_params=PARAMS,
        cost_estimate=pl.CostEstimate(
            flops=8 * mine.size, bytes_accessed=mine.size * 14, transcendentals=0
        ),
    )(mine, *received)


def normalise_kernel(n_chunks, rows_total, column_ref, *refs):
    chunks, out_ref = refs[:n_chunks], refs[n_chunks]
    rows = chunks[0].shape[0]
    colmean = column_ref[...] / rows_total
    for i, chunk in enumerate(chunks):
        out_ref[i * rows : (i + 1) * rows, :] = (
            chunk[...] / (colmean + 1e-06)
        ).astype(jnp.bfloat16)


def normalise(column, chunks, rows_total):
    rows, columns = chunks[0].shape
    return pl.pallas_call(
        functools.partial(normalise_kernel, len(chunks), rows_total),
        out_shape=jax.ShapeDtypeStruct((rows * len(chunks), columns), jnp.bfloat16),
        in_specs=[VMEM] * (1 + len(chunks)),
        out_specs=VMEM,
        compiler_params=PARAMS,
        cost_estimate=pl.CostEstimate(
            flops=4 * rows * columns * len(chunks),
            bytes_accessed=6 * rows * columns * len(chunks),
            transcendentals=0,
        ),
    )(column, *chunks)


def expand_tiles(values, pattern):
    tile_rows, layers, tile_cols = pattern.shape
    tile_size = values.shape[0] // tile_rows
    blocks = values.reshape(tile_rows, tile_size, layers, tile_cols, tile_size)
    blocks = blocks * pattern[:, None, :, :, None].astype(values.dtype)
    return blocks.reshape(values.shape)


def shift(x, axis, by):
    n = lax.axis_size(axis)
    return lax.ppermute(x, axis, [(i, (i + by) % n) for i in range(n)])


def per_device(left_values, left_pattern, right_values, right_pattern):
    n_layers, n_rows, n_cols = (lax.axis_size(a) for a in ("layer", "row", "col"))
    layer, row, col = (lax.axis_index(a) for a in ("layer", "row", "col"))
    rows_local, _, columns_local = left_values.shape
    inner_piece = right_values.shape[0]
    rows = rows_local // CHUNKS

    left_block = expand_tiles(left_values, left_pattern).reshape(rows_local, columns_local)
    lefts = []
    for i in range(CHUNKS):
        ring = [left_block[i * rows : (i + 1) * rows]]
        for _ in range(n_cols - 1):
            ring.append(shift(ring[-1], "col", 1))
        lefts.append(ring)

    right_block = expand_tiles(right_values, right_pattern).transpose(1, 0, 2)
    pieces = [right_block]
    for i in range(1, n_rows):
        pieces.append(shift(right_block, "row", i))
    right = jnp.stack(pieces)

    where = [layer]
    for source in range(n_cols):
        inner = (col - source + n_cols) % n_cols * columns_local
        where += [(row - inner // inner_piece + n_rows) % n_rows, inner % inner_piece]
    where = jnp.stack(where).astype(jnp.int32)

    squares, sums = [], []
    for ring in lefts:
        mine, sent = partial_products(where, ring, right, n_layers)
        received = [
            lax.ppermute(sent[j - 1], "layer", [(i, i ^ j) for i in range(n_layers)])
            for j in range(1, n_layers)
        ]
        squared, column = combine(mine, received)
        squares.append(squared)
        sums.append(column)
    column = lax.psum(functools.reduce(jnp.add, sums), "row")
    out = normalise(column, squares, rows_local * n_rows)
    return out.reshape(rows_local, 1, columns_local)


def solution(mesh):
    return jax.shard_map(
        per_device,
        mesh=mesh,
        in_specs=(
            P("row", "layer", "col"),
            P("row", "layer", "col"),
            P(("layer", "row"), None, "col"),
            P(("layer", "row"), None, "col"),
        ),
        out_specs=P("row", "layer", "col"),
        check_vma=False,
    )
```

```python
import functools

import jax
import jax.numpy as jnp
from jax import lax
from jax.experimental import pallas as pl
from jax.experimental.pallas import tpu as pltpu
from jax.sharding import PartitionSpec as P

TILE = 256
SIXTEENTHS = (4, 5, 4, 3)
SCALE_ROWS = 16
CODE = 64.0
TOP = 32767.0
LEAST = 2.0**-100
VMEM = pl.BlockSpec(memory_space=pltpu.VMEM)
PARAMS = pltpu.CompilerParams(vmem_limit_bytes=40 * 1024 * 1024)


def gated_mask_kernel(first, pattern_ref, left_ref, *refs):
    tile = (first + pl.program_id(0)) * left_ref.shape[0] // TILE
    refs[-1][...] = left_ref[...] * pattern_ref[tile].astype(jnp.float32).astype(left_ref.dtype)


def gated_mask(left, pattern, at, size, after):
    columns = left.shape[1]
    block = left.shape[0] // sum(SIXTEENTHS)
    first = at // block
    return pl.pallas_call(
        functools.partial(gated_mask_kernel, first),
        grid=(size // block,),
        out_shape=jax.ShapeDtypeStruct((size, columns), left.dtype),
        in_specs=[
            pl.BlockSpec(memory_space=pltpu.SMEM),
            pl.BlockSpec((block, columns), lambda i: (first + i, 0)),
        ]
        + [pl.BlockSpec(memory_space=pl.ANY)] * len(after),
        out_specs=pl.BlockSpec((block, columns), lambda i: (i, 0)),
        compiler_params=PARAMS,
        cost_estimate=pl.CostEstimate(
            flops=size * columns, bytes_accessed=4 * size * columns, transcendentals=0
        ),
    )(pattern, left, *after)


def gate_kernel(x_ref, after_ref, out_ref):
    out_ref[...] = x_ref[...]


def gate(x, after):
    return pl.pallas_call(
        gate_kernel,
        out_shape=jax.ShapeDtypeStruct(x.shape, x.dtype),
        in_specs=[VMEM, pl.BlockSpec(memory_space=pl.ANY)],
        out_specs=VMEM,
    )(x, after)


def partial_kernel(n_sources, n_layers, where, *refs):
    lefts = refs[:n_sources]
    right_ref, mine_ref, *sent_refs = refs[n_sources:]
    rows = lefts[0].shape[0]
    for step in range(n_layers):
        layer = where[0] ^ step
        total = jnp.zeros((rows, right_ref.shape[3]), jnp.float32)
        for source in range(n_sources):
            start = pl.multiple_of(where[2 + 2 * source], TILE)
            total += jnp.dot(
                lefts[source][...],
                right_ref[where[1 + 2 * source], layer, pl.ds(start, TILE), :],
                preferred_element_type=jnp.float32,
            )
        if step == 0:
            mine_ref[...] = total
            continue
        top = jnp.maximum(jnp.max(jnp.abs(total), axis=0, keepdims=True), LEAST)
        code = jnp.ceil(jnp.log2(top) * CODE + 0.01)
        unit = jnp.exp2(code / -CODE) * TOP
        fixed = jnp.round(total * unit).astype(jnp.int32)
        sent_refs[step - 1][:rows, :] = fixed.astype(jnp.int16)
        codes = jnp.broadcast_to(code.astype(jnp.int32), (SCALE_ROWS, code.shape[1]))
        sent_refs[step - 1][rows:, :] = codes.astype(jnp.int16)


def partial_products(where, lefts, right, n_layers):
    rows, columns = lefts[0].shape[0], right.shape[3]
    return pl.pallas_call(
        functools.partial(partial_kernel, len(lefts), n_layers),
        out_shape=[jax.ShapeDtypeStruct((rows, columns), jnp.float32)]
        + [jax.ShapeDtypeStruct((rows + SCALE_ROWS, columns), jnp.int16)] * (n_layers - 1),
        in_specs=[pl.BlockSpec(memory_space=pltpu.SMEM)] + [VMEM] * (len(lefts) + 1),
        out_specs=[VMEM] * n_layers,
        compiler_params=PARAMS,
        cost_estimate=pl.CostEstimate(
            flops=2 * rows * len(lefts) * TILE * columns * n_layers,
            bytes_accessed=right.size * 2 + rows * columns * 14,
            transcendentals=0,
        ),
    )(where, *lefts, right)


def combine_kernel(n_received, mine_ref, *refs):
    received, (before_ref, squared_ref, sum_ref) = refs[:n_received], refs[n_received:]
    total = mine_ref[...]
    rows = total.shape[0]
    for block in received:
        code = block[rows:, :].astype(jnp.int32)[:1].astype(jnp.float32)
        unit = jnp.exp2(code / CODE) * (1.0 / TOP)
        total += block[:rows, :].astype(jnp.int32).astype(jnp.float32) * unit
    squared = total * total
    squared_ref[...] = squared
    sum_ref[...] = before_ref[...] + jnp.sum(squared, axis=0, keepdims=True)


def combine(mine, received, before):
    return pl.pallas_call(
        functools.partial(combine_kernel, len(received)),
        out_shape=(
            jax.ShapeDtypeStruct(mine.shape, jnp.float32),
            jax.ShapeDtypeStruct((1, mine.shape[1]), jnp.float32),
        ),
        in_specs=[VMEM] * (2 + len(received)),
        out_specs=(VMEM, VMEM),
        compiler_params=PARAMS,
        cost_estimate=pl.CostEstimate(
            flops=8 * mine.size, bytes_accessed=mine.size * 14, transcendentals=0
        ),
    )(mine, *received, before)


def normalise_kernel(n_chunks, rows_total, column_ref, *refs):
    chunks, out_ref = refs[:n_chunks], refs[n_chunks]
    colmean = column_ref[...] / rows_total
    at = 0
    for chunk in chunks:
        rows = chunk.shape[0]
        out_ref[at : at + rows, :] = (chunk[...] / (colmean + 1e-06)).astype(jnp.bfloat16)
        at += rows


def normalise(column, chunks, rows_total):
    rows, columns = sum(chunk.shape[0] for chunk in chunks), chunks[0].shape[1]
    return pl.pallas_call(
        functools.partial(normalise_kernel, len(chunks), rows_total),
        out_shape=jax.ShapeDtypeStruct((rows, columns), jnp.bfloat16),
        in_specs=[VMEM] * (1 + len(chunks)),
        out_specs=VMEM,
        compiler_params=PARAMS,
        cost_estimate=pl.CostEstimate(
            flops=4 * rows * columns,
            bytes_accessed=6 * rows * columns,
            transcendentals=0,
        ),
    )(column, *chunks)


def expand_tiles(values, pattern):
    tile_rows, layers, tile_cols = pattern.shape
    tile_size = values.shape[0] // tile_rows
    blocks = values.reshape(tile_rows, tile_size, layers, tile_cols, tile_size)
    blocks = blocks * pattern[:, None, :, :, None].astype(values.dtype)
    return blocks.reshape(values.shape)


def shift(x, axis, by):
    n = lax.axis_size(axis)
    return lax.ppermute(x, axis, [(i, (i + by) % n) for i in range(n)])


def per_device(left_values, left_pattern, right_values, right_pattern):
    n_layers, n_rows, n_cols = (lax.axis_size(a) for a in ("layer", "row", "col"))
    layer, row, col = (lax.axis_index(a) for a in ("layer", "row", "col"))
    rows_local, _, columns_local = left_values.shape
    inner_piece = right_values.shape[0]
    sizes = [rows_local * part // 16 for part in SIXTEENTHS]
    starts = [sum(sizes[:i]) for i in range(len(sizes))]

    left = left_values.reshape(rows_local, columns_local)
    pattern = left_pattern.reshape(-1)
    rings = []
    for i, (at, size) in enumerate(zip(starts, sizes)):
        ring = [gated_mask(left, pattern, at, size, [rings[i - 2][-1]] if i > 1 else [])]
        for _ in range(n_cols - 1):
            ring.append(shift(ring[-1], "col", 1))
        rings.append(ring)

    right_pattern = gate(right_pattern, rings[1][0])
    right_block = expand_tiles(right_values, right_pattern).transpose(1, 0, 2)
    pieces = [right_block]
    for i in range(1, n_rows):
        pieces.append(shift(right_block, "row", i))
    right = jnp.stack(pieces)

    where = [layer]
    for source in range(n_cols):
        inner = (col - source + n_cols) % n_cols * columns_local
        where += [(row - inner // inner_piece + n_rows) % n_rows, inner % inner_piece]
    where = jnp.stack(where).astype(jnp.int32)

    squares = []
    column = jnp.zeros((1, columns_local), jnp.float32)
    for ring in rings:
        mine, *sent = partial_products(where, ring, right, n_layers)
        received = [
            lax.ppermute(sent[j - 1], "layer", [(i, i ^ j) for i in range(n_layers)])
            for j in range(1, n_layers)
        ]
        squared, column = combine(mine, received, column)
        squares.append(squared)
    column = lax.psum(column, "row")
    out = normalise(column, squares, rows_local * n_rows)
    return out.reshape(rows_local, 1, columns_local)


def solution(mesh):
    return jax.shard_map(
        per_device,
        mesh=mesh,
        in_specs=(
            P("row", "layer", "col"),
            P("row", "layer", "col"),
            P(("layer", "row"), None, "col"),
            P(("layer", "row"), None, "col"),
        ),
        out_specs=P("row", "layer", "col"),
        check_vma=False,
    )
```

```python
import functools

import jax
import jax.numpy as jnp
from jax import lax
from jax.experimental import pallas as pl
from jax.experimental.pallas import tpu as pltpu
from jax.sharding import PartitionSpec as P

TILE = 256
SIXTEENTHS = (4, 5, 4, 3)
SCALE_ROWS = 16
CODE = 64.0
TOP = 32767.0
LEAST = 2.0**-100
VMEM = pl.BlockSpec(memory_space=pltpu.VMEM)
PARAMS = pltpu.CompilerParams(vmem_limit_bytes=40 * 1024 * 1024)


def gated_mask_kernel(first, pattern_ref, left_ref, *refs):
    tile = (first + pl.program_id(0)) * left_ref.shape[0] // TILE
    refs[-1][...] = left_ref[...] * pattern_ref[tile].astype(jnp.float32).astype(left_ref.dtype)


def gated_mask(left, pattern, at, size, after):
    columns = left.shape[1]
    block = left.shape[0] // sum(SIXTEENTHS)
    first = at // block
    return pl.pallas_call(
        functools.partial(gated_mask_kernel, first),
        grid=(size // block,),
        out_shape=jax.ShapeDtypeStruct((size, columns), left.dtype),
        in_specs=[
            pl.BlockSpec(memory_space=pltpu.SMEM),
            pl.BlockSpec((block, columns), lambda i: (first + i, 0)),
        ]
        + [pl.BlockSpec(memory_space=pl.ANY)] * len(after),
        out_specs=pl.BlockSpec((block, columns), lambda i: (i, 0)),
        compiler_params=PARAMS,
        cost_estimate=pl.CostEstimate(
            flops=size * columns, bytes_accessed=4 * size * columns, transcendentals=0
        ),
    )(pattern, left, *after)


def gate_kernel(x_ref, after_ref, out_ref):
    out_ref[...] = x_ref[...]


def gate(x, after):
    return pl.pallas_call(
        gate_kernel,
        out_shape=jax.ShapeDtypeStruct(x.shape, x.dtype),
        in_specs=[VMEM, pl.BlockSpec(memory_space=pl.ANY)],
        out_specs=VMEM,
    )(x, after)


def partial_kernel(n_sources, n_layers, where, *refs):
    left_ref, right_ref, mine_ref, *sent_refs = refs
    rows = left_ref.shape[1]
    for step in range(n_layers):
        layer = where[0] ^ step
        total = jnp.zeros((rows, right_ref.shape[3]), jnp.float32)
        for source in range(n_sources):
            start = pl.multiple_of(where[2 + 2 * source], TILE)
            total += jnp.dot(
                left_ref[source],
                right_ref[where[1 + 2 * source], layer, pl.ds(start, TILE), :],
                preferred_element_type=jnp.float32,
            )
        if step == 0:
            mine_ref[...] = total
            continue
        top = jnp.maximum(jnp.max(jnp.abs(total), axis=0, keepdims=True), LEAST)
        code = jnp.ceil(jnp.log2(top) * CODE + 0.01)
        unit = jnp.exp2(code / -CODE) * TOP
        fixed = jnp.round(total * unit).astype(jnp.int32)
        sent_refs[step - 1][:rows, :] = fixed.astype(jnp.int16)
        codes = jnp.broadcast_to(code.astype(jnp.int32), (SCALE_ROWS, code.shape[1]))
        sent_refs[step - 1][rows:, :] = codes.astype(jnp.int16)


def partial_products(where, left, right, n_layers):
    n_sources, rows, columns = left.shape[0], left.shape[1], right.shape[3]
    return pl.pallas_call(
        functools.partial(partial_kernel, n_sources, n_layers),
        out_shape=[jax.ShapeDtypeStruct((rows, columns), jnp.float32)]
        + [jax.ShapeDtypeStruct((rows + SCALE_ROWS, columns), jnp.int16)] * (n_layers - 1),
        in_specs=[pl.BlockSpec(memory_space=pltpu.SMEM)] + [VMEM] * 2,
        out_specs=[VMEM] * n_layers,
        compiler_params=PARAMS,
        cost_estimate=pl.CostEstimate(
            flops=2 * rows * n_sources * TILE * columns * n_layers,
            bytes_accessed=right.size * 2 + rows * columns * 14,
            transcendentals=0,
        ),
    )(where, left, right)


def combine_kernel(n_received, mine_ref, *refs):
    received, (before_ref, squared_ref, sum_ref) = refs[:n_received], refs[n_received:]
    total = mine_ref[...]
    rows = total.shape[0]
    for block in received:
        code = block[rows:, :].astype(jnp.int32)[:1].astype(jnp.float32)
        unit = jnp.exp2(code / CODE) * (1.0 / TOP)
        total += block[:rows, :].astype(jnp.int32).astype(jnp.float32) * unit
    squared = total * total
    squared_ref[...] = squared
    sum_ref[...] = before_ref[...] + jnp.sum(squared, axis=0, keepdims=True)


def combine(mine, received, before):
    return pl.pallas_call(
        functools.partial(combine_kernel, len(received)),
        out_shape=(
            jax.ShapeDtypeStruct(mine.shape, jnp.float32),
            jax.ShapeDtypeStruct((1, mine.shape[1]), jnp.float32),
        ),
        in_specs=[VMEM] * (2 + len(received)),
        out_specs=(VMEM, VMEM),
        compiler_params=PARAMS,
        cost_estimate=pl.CostEstimate(
            flops=8 * mine.size, bytes_accessed=mine.size * 14, transcendentals=0
        ),
    )(mine, *received, before)


def normalise_kernel(n_chunks, rows_total, column_ref, *refs):
    chunks, out_ref = refs[:n_chunks], refs[n_chunks]
    colmean = column_ref[...] / rows_total
    at = 0
    for chunk in chunks:
        rows = chunk.shape[0]
        out_ref[at : at + rows, :] = (chunk[...] / (colmean + 1e-06)).astype(jnp.bfloat16)
        at += rows


def normalise(column, chunks, rows_total):
    rows, columns = sum(chunk.shape[0] for chunk in chunks), chunks[0].shape[1]
    return pl.pallas_call(
        functools.partial(normalise_kernel, len(chunks), rows_total),
        out_shape=jax.ShapeDtypeStruct((rows, columns), jnp.bfloat16),
        in_specs=[VMEM] * (1 + len(chunks)),
        out_specs=VMEM,
        compiler_params=PARAMS,
        cost_estimate=pl.CostEstimate(
            flops=4 * rows * columns,
            bytes_accessed=6 * rows * columns,
            transcendentals=0,
        ),
    )(column, *chunks)


def expand_tiles(values, pattern):
    tile_rows, layers, tile_cols = pattern.shape
    tile_size = values.shape[0] // tile_rows
    blocks = values.reshape(tile_rows, tile_size, layers, tile_cols, tile_size)
    blocks = blocks * pattern[:, None, :, :, None].astype(values.dtype)
    return blocks.reshape(values.shape)


def shift(x, axis, by):
    n = lax.axis_size(axis)
    return lax.ppermute(x, axis, [(i, (i + by) % n) for i in range(n)])


def per_device(left_values, left_pattern, right_values, right_pattern):
    n_layers, n_rows, n_cols = (lax.axis_size(a) for a in ("layer", "row", "col"))
    layer, row = lax.axis_index("layer"), lax.axis_index("row")
    rows_local, _, columns_local = left_values.shape
    inner_piece = right_values.shape[0]
    sizes = [rows_local * part // 16 for part in SIXTEENTHS]
    starts = [sum(sizes[:i]) for i in range(len(sizes))]

    left = left_values.reshape(rows_local, columns_local)
    pattern = left_pattern.reshape(-1)
    masked = [gated_mask(left, pattern, at, size, []) for at, size in zip(starts, sizes)]
    rings = [lax.all_gather(block, "col") for block in masked]

    right_pattern = gate(right_pattern, masked[0])
    right_block = expand_tiles(right_values, right_pattern).transpose(1, 0, 2)
    pieces = [right_block]
    for i in range(1, n_rows):
        pieces.append(shift(right_block, "row", i))
    right = jnp.stack(pieces)

    where = [layer]
    for source in range(n_cols):
        inner = source * columns_local
        where += [(row - inner // inner_piece + n_rows) % n_rows, inner % inner_piece]
    where = jnp.stack(where).astype(jnp.int32)

    squares = []
    column = jnp.zeros((1, columns_local), jnp.float32)
    for ring in rings:
        mine, *sent = partial_products(where, ring, right, n_layers)
        received = [
            lax.ppermute(sent[j - 1], "layer", [(i, i ^ j) for i in range(n_layers)])
            for j in range(1, n_layers)
        ]
        squared, column = combine(mine, received, column)
        squares.append(squared)
    column = lax.psum(column, "row")
    out = normalise(column, squares, rows_local * n_rows)
    return out.reshape(rows_local, 1, columns_local)


def solution(mesh):
    return jax.shard_map(
        per_device,
        mesh=mesh,
        in_specs=(
            P("row", "layer", "col"),
            P("row", "layer", "col"),
            P(("layer", "row"), None, "col"),
            P(("layer", "row"), None, "col"),
        ),
        out_specs=P("row", "layer", "col"),
        check_vma=False,
    )
```

```python
import functools
import math

import jax
import jax.numpy as jnp
from jax import lax
from jax.experimental import pallas as pl
from jax.experimental.pallas import tpu as pltpu
from jax.sharding import PartitionSpec as P

TILE = 256
SIXTEENTHS = (5, 5, 3, 3)
SCALE_ROWS = 16
CODE = 64.0
TOP = 32767.0
LEAST = 2.0**-100
VMEM = pl.BlockSpec(memory_space=pltpu.VMEM)
PARAMS = pltpu.CompilerParams(vmem_limit_bytes=40 * 1024 * 1024)


def load_kernel(at, pattern_ref, left_ref, *refs):
    out_ref = refs[-1]
    size = out_ref.shape[0]
    step = math.gcd(TILE, math.gcd(at, size))
    for i in range(0, size, step):
        entry = pattern_ref[(at + i) // TILE].astype(jnp.float32).astype(out_ref.dtype)
        out_ref[i : i + step, :] = left_ref[at + i : at + i + step, :] * entry


def load(left, pattern, at, size, after):
    columns = left.shape[1]
    return pl.pallas_call(
        functools.partial(load_kernel, at),
        out_shape=jax.ShapeDtypeStruct((size, columns), left.dtype),
        in_specs=[pl.BlockSpec(memory_space=pltpu.SMEM), VMEM]
        + [pl.BlockSpec(memory_space=pl.ANY)] * len(after),
        out_specs=VMEM,
        compiler_params=PARAMS,
        cost_estimate=pl.CostEstimate(
            flops=size * columns, bytes_accessed=4 * size * columns, transcendentals=0
        ),
    )(pattern, left, *after)


def gate_kernel(x_ref, after_ref, out_ref):
    out_ref[...] = x_ref[...]


def gate(x, after):
    return pl.pallas_call(
        gate_kernel,
        out_shape=jax.ShapeDtypeStruct(x.shape, x.dtype),
        in_specs=[VMEM, pl.BlockSpec(memory_space=pl.ANY)],
        out_specs=VMEM,
    )(x, after)


def put_fixed(ref, at, total):
    rows, columns = total.shape
    top = jnp.maximum(jnp.max(jnp.abs(total), axis=0, keepdims=True), LEAST)
    code = jnp.ceil(jnp.log2(top) * CODE + 0.01)
    fixed = jnp.round(total * (jnp.exp2(code / -CODE) * TOP)).astype(jnp.int32)
    ref[at : at + rows, :] = fixed.astype(jnp.int16)
    codes = jnp.broadcast_to(code.astype(jnp.int32), (SCALE_ROWS, columns))
    ref[at + rows : at + rows + SCALE_ROWS, :] = codes.astype(jnp.int16)


def get_fixed(ref, at, rows):
    code = ref[at + rows : at + rows + SCALE_ROWS, :].astype(jnp.int32)[:1].astype(jnp.float32)
    unit = jnp.exp2(code / CODE) * (1.0 / TOP)
    return ref[at : at + rows, :].astype(jnp.int32).astype(jnp.float32) * unit


def partial_kernel(n_sources, kept, sent, where, *refs):
    lefts, right_ref, outs = refs[:n_sources], refs[n_sources], refs[n_sources + 1 :]
    rows, columns = lefts[0].shape[0], right_ref.shape[3]

    def product(k):
        total = jnp.zeros((rows, columns), jnp.float32)
        for source in range(n_sources):
            start = pl.multiple_of(where[2 + 2 * source], TILE)
            total += jnp.dot(
                lefts[source][...],
                right_ref[where[1 + 2 * source], where[0] ^ k, pl.ds(start, TILE), :],
                preferred_element_type=jnp.float32,
            )
        return total

    for out, ks in zip(outs[len(kept) :], sent):
        for i, k in enumerate(ks):
            put_fixed(out, i * (rows + SCALE_ROWS), product(k))
    for out, k in zip(outs, kept):
        out[...] = product(k)


def partial_products(where, lefts, right, kept, sent):
    rows, columns = lefts[0].shape[0], right.shape[3]
    n_products = len(kept) + sum(len(ks) for ks in sent)
    outs = [jax.ShapeDtypeStruct((rows, columns), jnp.float32)] * len(kept)
    outs += [
        jax.ShapeDtypeStruct((len(ks) * (rows + SCALE_ROWS), columns), jnp.int16) for ks in sent
    ]
    out = pl.pallas_call(
        functools.partial(partial_kernel, len(lefts), kept, sent),
        out_shape=outs,
        in_specs=[pl.BlockSpec(memory_space=pltpu.SMEM)] + [VMEM] * (len(lefts) + 1),
        out_specs=[VMEM] * len(outs),
        compiler_params=PARAMS,
        cost_estimate=pl.CostEstimate(
            flops=2 * rows * len(lefts) * TILE * columns * n_products,
            bytes_accessed=right.size * 2 + rows * columns * 14,
            transcendentals=0,
        ),
    )(where, *lefts, right)
    return out[: len(kept)], out[len(kept) :]


def pass_on_kernel(kept_ref, received_ref, after_ref, out_ref):
    rows = kept_ref.shape[0]
    total = kept_ref[...] + get_fixed(received_ref, rows + SCALE_ROWS, rows)
    put_fixed(out_ref, 0, total)


def pass_on(kept, received, after):
    rows, columns = kept.shape
    return pl.pallas_call(
        pass_on_kernel,
        out_shape=jax.ShapeDtypeStruct((rows + SCALE_ROWS, columns), jnp.int16),
        in_specs=[VMEM, VMEM, pl.BlockSpec(memory_space=pl.ANY)],
        out_specs=VMEM,
        compiler_params=PARAMS,
        cost_estimate=pl.CostEstimate(
            flops=10 * kept.size, bytes_accessed=8 * kept.size, transcendentals=0
        ),
    )(kept, received, after)


def combine_kernel(n_received, kept_ref, *refs):
    received, (before_ref, squared_ref, sum_ref) = refs[:n_received], refs[n_received:]
    total = kept_ref[...]
    for block in received:
        total += get_fixed(block, 0, total.shape[0])
    squared = total * total
    squared_ref[...] = squared
    sum_ref[...] = before_ref[...] + jnp.sum(squared, axis=0, keepdims=True)


def combine(kept, received, before):
    return pl.pallas_call(
        functools.partial(combine_kernel, len(received)),
        out_shape=(
            jax.ShapeDtypeStruct(kept.shape, jnp.float32),
            jax.ShapeDtypeStruct((1, kept.shape[1]), jnp.float32),
        ),
        in_specs=[VMEM] * (2 + len(received)),
        out_specs=(VMEM, VMEM),
        compiler_params=PARAMS,
        cost_estimate=pl.CostEstimate(
            flops=8 * kept.size, bytes_accessed=kept.size * 14, transcendentals=0
        ),
    )(kept, *received, before)


def normalise_kernel(n_chunks, rows_total, column_ref, *refs):
    chunks, out_ref = refs[:n_chunks], refs[n_chunks]
    colmean = column_ref[...] / rows_total
    at = 0
    for chunk in chunks:
        rows = chunk.shape[0]
        out_ref[at : at + rows, :] = (chunk[...] / (colmean + 1e-06)).astype(jnp.bfloat16)
        at += rows


def normalise(column, chunks, rows_total):
    rows, columns = sum(chunk.shape[0] for chunk in chunks), chunks[0].shape[1]
    return pl.pallas_call(
        functools.partial(normalise_kernel, len(chunks), rows_total),
        out_shape=jax.ShapeDtypeStruct((rows, columns), jnp.bfloat16),
        in_specs=[VMEM] * (1 + len(chunks)),
        out_specs=VMEM,
        compiler_params=PARAMS,
        cost_estimate=pl.CostEstimate(
            flops=4 * rows * columns,
            bytes_accessed=6 * rows * columns,
            transcendentals=0,
        ),
    )(column, *chunks)


def expand_tiles(values, pattern):
    tile_rows, layers, tile_cols = pattern.shape
    tile_size = values.shape[0] // tile_rows
    blocks = values.reshape(tile_rows, tile_size, layers, tile_cols, tile_size)
    blocks = blocks * pattern[:, None, :, :, None].astype(values.dtype)
    return blocks.reshape(values.shape)


def shift(x, axis, by):
    n = lax.axis_size(axis)
    return lax.ppermute(x, axis, [(i, (i + by) % n) for i in range(n)])


def swap(x, bits):
    return lax.ppermute(x, "layer", [(i, i ^ bits) for i in range(4)])


def per_device(left_values, left_pattern, right_values, right_pattern):
    n_rows, n_cols = lax.axis_size("row"), lax.axis_size("col")
    layer, row, col = (lax.axis_index(a) for a in ("layer", "row", "col"))
    rows_local, _, columns_local = left_values.shape
    inner_piece = right_values.shape[0]
    sizes = [rows_local * part // sum(SIXTEENTHS) for part in SIXTEENTHS]

    left = left_values.reshape(rows_local, columns_local)
    pattern = left_pattern.reshape(-1)
    starts = [sum(sizes[:i]) for i in range(len(sizes))]
    chunks = []
    for i, (at, size) in enumerate(zip(starts, sizes)):
        ring = [load(left, pattern, at, size, [chunks[i - 2][-1]] if i > 1 else [chunk[0] for chunk in chunks])]
        for _ in range(n_cols - 1):
            ring.append(shift(ring[-1], "col", 1))
        chunks.append(ring)

    right_pattern = gate(right_pattern, chunks[1][0])
    right_block = expand_tiles(right_values, right_pattern).transpose(1, 0, 2)
    pieces = [right_block]
    for i in range(1, n_rows):
        pieces.append(shift(right_block, "row", i))
    right = jnp.stack(pieces)

    where = [layer]
    for source in range(n_cols):
        inner = (col - source + n_cols) % n_cols * columns_local
        where += [(row - inner // inner_piece + n_rows) % n_rows, inner % inner_piece]
    where = jnp.stack(where).astype(jnp.int32)

    sums = []
    for i, chunk in enumerate(chunks):
        if i + 1 < len(chunks):
            first, second = (1, 2) if i % 2 == 0 else (2, 1)
            kept, sent = partial_products(where, chunk, right, (0, second), ((first, 3),))
            sums.append((kept, swap(sent[0], first), second))
        else:
            kept, sent = partial_products(where, chunk, right, (0,), ((1,), (2,), (3,)))
            sums.append((kept, [swap(x, k + 1) for k, x in enumerate(sent)], 0))

    squares = []
    column = jnp.zeros((1, columns_local), jnp.float32)
    for i, (kept, received, second) in enumerate(sums):
        if second:
            after = chunks[i + 2][0] if i + 2 < len(chunks) else sums[-1][0][0]
            received = [received, swap(pass_on(kept[1], received, after), second)]
        squared, column = combine(kept[0], received, column)
        squares.append(squared)
    column = lax.psum(column, "row")
    out = normalise(column, squares, rows_local * n_rows)
    return out.reshape(rows_local, 1, columns_local)


def solution(mesh):
    return jax.shard_map(
        per_device,
        mesh=mesh,
        in_specs=(
            P("row", "layer", "col"),
            P("row", "layer", "col"),
            P(("layer", "row"), None, "col"),
            P(("layer", "row"), None, "col"),
        ),
        out_specs=P("row", "layer", "col"),
        check_vma=False,
    )
```

```python
import functools
import math

import jax
import jax.numpy as jnp
from jax import lax
from jax.experimental import pallas as pl
from jax.experimental.layout import Layout, with_layout_constraint
from jax.experimental.pallas import tpu as pltpu
from jax.sharding import PartitionSpec as P

TILE = 256
SIXTEENTHS = (4, 5, 4, 3)
SCALE_ROWS = 16
CODE = 64.0
TOP = 32767.0
LEAST = 2.0**-100
VMEM = pl.BlockSpec(memory_space=pltpu.VMEM)
PARAMS = pltpu.CompilerParams(vmem_limit_bytes=40 * 1024 * 1024)


def load_kernel(at, pattern_ref, left_ref, *refs):
    out_ref = refs[-1]
    size = out_ref.shape[0]
    step = math.gcd(TILE, math.gcd(at, size))
    for i in range(0, size, step):
        entry = pattern_ref[(at + i) // TILE].astype(jnp.float32).astype(out_ref.dtype)
        out_ref[i : i + step, :] = left_ref[at + i : at + i + step, :] * entry


def load(left, pattern, at, size, after):
    columns = left.shape[1]
    return pl.pallas_call(
        functools.partial(load_kernel, at),
        out_shape=jax.ShapeDtypeStruct((size, columns), left.dtype),
        in_specs=[pl.BlockSpec(memory_space=pltpu.SMEM), VMEM]
        + [pl.BlockSpec(memory_space=pl.ANY)] * len(after),
        out_specs=VMEM,
        compiler_params=PARAMS,
        cost_estimate=pl.CostEstimate(
            flops=size * columns, bytes_accessed=4 * size * columns, transcendentals=0
        ),
    )(pattern, left, *after)


def put_fixed(ref, at, total):
    rows, columns = total.shape
    top = jnp.maximum(jnp.max(jnp.abs(total), axis=0, keepdims=True), LEAST)
    code = jnp.ceil(jnp.log2(top) * CODE + 0.01)
    fixed = jnp.round(total * (jnp.exp2(code / -CODE) * TOP)).astype(jnp.int32)
    ref[at : at + rows, :] = fixed.astype(jnp.int16)
    codes = jnp.broadcast_to(code.astype(jnp.int32), (SCALE_ROWS, columns))
    ref[at + rows : at + rows + SCALE_ROWS, :] = codes.astype(jnp.int16)


def get_fixed(ref, at, rows):
    code = ref[at + rows : at + rows + SCALE_ROWS, :].astype(jnp.int32)[:1].astype(jnp.float32)
    unit = jnp.exp2(code / CODE) * (1.0 / TOP)
    return ref[at : at + rows, :].astype(jnp.int32).astype(jnp.float32) * unit


def partial_kernel(n_sources, n_pieces, kept, sent, where, *refs):
    lefts, pieces = refs[:n_sources], refs[n_sources : n_sources + n_pieces]
    outs = refs[-len(kept) - len(sent) :]
    rows, columns = lefts[0].shape[0], pieces[0].shape[2]

    def right(source, layer):
        start = pl.multiple_of(where[2 + 2 * source], TILE)
        tile = pieces[0][layer, pl.ds(start, TILE), :]
        for i in range(1, n_pieces):
            here = where[1 + 2 * source] == i
            tile = jnp.where(here, pieces[i][layer, pl.ds(start, TILE), :], tile)
        return tile

    def product(k):
        total = jnp.zeros((rows, columns), jnp.float32)
        for source in range(n_sources):
            total += jnp.dot(
                lefts[source][...],
                right(source, where[0] ^ k),
                preferred_element_type=jnp.float32,
            )
        return total

    for out, ks in zip(outs[len(kept) :], sent):
        for i, k in enumerate(ks):
            put_fixed(out, i * (rows + SCALE_ROWS), product(k))
    for out, k in zip(outs, kept):
        out[...] = product(k)


def partial_products(where, lefts, pieces, after, kept, sent):
    rows, columns = lefts[0].shape[0], pieces[0].shape[2]
    n_products = len(kept) + sum(len(ks) for ks in sent)
    outs = [jax.ShapeDtypeStruct((rows, columns), jnp.float32)] * len(kept)
    outs += [
        jax.ShapeDtypeStruct((len(ks) * (rows + SCALE_ROWS), columns), jnp.int16) for ks in sent
    ]
    out = pl.pallas_call(
        functools.partial(partial_kernel, len(lefts), len(pieces), kept, sent),
        out_shape=outs,
        in_specs=[pl.BlockSpec(memory_space=pltpu.SMEM)]
        + [VMEM] * (len(lefts) + len(pieces))
        + [pl.BlockSpec(memory_space=pl.ANY)] * len(after),
        out_specs=[VMEM] * len(outs),
        compiler_params=PARAMS,
        cost_estimate=pl.CostEstimate(
            flops=2 * rows * len(lefts) * TILE * columns * n_products,
            bytes_accessed=len(pieces) * pieces[0].size * 2 + rows * columns * 14,
            transcendentals=0,
        ),
    )(where, *lefts, *pieces, *after)
    return out[: len(kept)], out[len(kept) :]


def pass_on_kernel(kept_ref, received_ref, after_ref, out_ref):
    rows = kept_ref.shape[0]
    total = kept_ref[...] + get_fixed(received_ref, rows + SCALE_ROWS, rows)
    put_fixed(out_ref, 0, total)


def pass_on(kept, received, after):
    rows, columns = kept.shape
    return pl.pallas_call(
        pass_on_kernel,
        out_shape=jax.ShapeDtypeStruct((rows + SCALE_ROWS, columns), jnp.int16),
        in_specs=[VMEM, VMEM, pl.BlockSpec(memory_space=pl.ANY)],
        out_specs=VMEM,
        compiler_params=PARAMS,
        cost_estimate=pl.CostEstimate(
            flops=10 * kept.size, bytes_accessed=8 * kept.size, transcendentals=0
        ),
    )(kept, received, after)


def combine_kernel(n_received, kept_ref, *refs):
    received, (before_ref, squared_ref, sum_ref) = refs[:n_received], refs[n_received:]
    total = kept_ref[...]
    for block in received:
        total += get_fixed(block, 0, total.shape[0])
    squared = total * total
    squared_ref[...] = squared
    sum_ref[...] = before_ref[...] + jnp.sum(squared, axis=0, keepdims=True)


def combine(kept, received, before):
    return pl.pallas_call(
        functools.partial(combine_kernel, len(received)),
        out_shape=(
            jax.ShapeDtypeStruct(kept.shape, jnp.float32),
            jax.ShapeDtypeStruct((1, kept.shape[1]), jnp.float32),
        ),
        in_specs=[VMEM] * (2 + len(received)),
        out_specs=(VMEM, VMEM),
        compiler_params=PARAMS,
        cost_estimate=pl.CostEstimate(
            flops=8 * kept.size, bytes_accessed=kept.size * 14, transcendentals=0
        ),
    )(kept, *received, before)


def normalise_kernel(n_chunks, rows_total, column_ref, *refs):
    chunks, out_ref = refs[:n_chunks], refs[n_chunks]
    colmean = column_ref[...] / rows_total
    at = 0
    for chunk in chunks:
        rows = chunk.shape[0]
        out_ref[at : at + rows, :] = (chunk[...] / (colmean + 1e-06)).astype(jnp.bfloat16)
        at += rows


def normalise(column, chunks, rows_total):
    rows, columns = sum(chunk.shape[0] for chunk in chunks), chunks[0].shape[1]
    return pl.pallas_call(
        functools.partial(normalise_kernel, len(chunks), rows_total),
        out_shape=jax.ShapeDtypeStruct((rows, columns), jnp.bfloat16),
        in_specs=[VMEM] * (1 + len(chunks)),
        out_specs=VMEM,
        compiler_params=PARAMS,
        cost_estimate=pl.CostEstimate(
            flops=4 * rows * columns,
            bytes_accessed=6 * rows * columns,
            transcendentals=0,
        ),
    )(column, *chunks)


def expand_tiles(values, pattern):
    tile_rows, layers, tile_cols = pattern.shape
    tile_size = values.shape[0] // tile_rows
    blocks = values.reshape(tile_rows, tile_size, layers, tile_cols, tile_size)
    blocks = blocks * pattern[:, None, :, :, None].astype(values.dtype)
    return blocks.reshape(values.shape)


def shift(x, axis, by):
    n = lax.axis_size(axis)
    return lax.ppermute(x, axis, [(i, (i + by) % n) for i in range(n)])


def as_it_lies(x):
    return with_layout_constraint(x, Layout(tuple(range(x.ndim))))


def swap(x, bits):
    return lax.ppermute(x, "layer", [(i, i ^ bits) for i in range(4)])


def per_device(left_values, left_pattern, right_values, right_pattern):
    n_rows, n_cols = lax.axis_size("row"), lax.axis_size("col")
    layer, row, col = (lax.axis_index(a) for a in ("layer", "row", "col"))
    rows_local, _, columns_local = left_values.shape
    inner_piece = right_values.shape[0]
    sizes = [rows_local * part // sum(SIXTEENTHS) for part in SIXTEENTHS]

    left = left_values.reshape(rows_local, columns_local)
    pattern = left_pattern.reshape(-1)
    where = [layer]
    for source in range(n_cols):
        inner = (col - source + n_cols) % n_cols * columns_local
        where += [(row - inner // inner_piece + n_rows) % n_rows, inner % inner_piece]
    where = jnp.stack(where).astype(jnp.int32)

    starts = [sum(sizes[:i]) for i in range(len(sizes))]
    rings, kept, received, last = [], [], [], []

    def open_ring(i):
        after = [rings[0][-1]] if i == 2 else []
        ring = [load(left, pattern, starts[i], sizes[i], after + last)]
        for _ in range(n_cols - 1):
            ring.append(shift(ring[-1], "col", 1))
        rings.append(ring)
        last[:] = [ring[0]]

    def sum_ring(i):
        if i + 1 < len(sizes):
            ks, sent_ks = (0, second(i)), ((3 - second(i), 3),)
        else:
            ks, sent_ks = (0,), ((1,), (2,), (3,))
        mine, sent = partial_products(where, rings[i], pieces, last, ks, sent_ks)
        kept.append(mine)
        received.append([swap(x, k[0]) for x, k in zip(sent, sent_ks)])
        last[:] = [mine[0]]

    def second(i):
        return 2 - i % 2

    def send_on(i):
        block = pass_on(kept[i][1], received[i][0], last[0])
        received[i].append(swap(block, second(i)))
        last[:] = [block]

    pieces = []
    for i in range(n_rows):
        values, tiles = right_values, right_pattern
        if i:
            values, tiles = as_it_lies(shift(values, "row", i)), shift(tiles, "row", i)
        pieces.append(expand_tiles(values, tiles).transpose(1, 0, 2))

    open_ring(0)
    open_ring(1)
    last += pieces
    for i in range(len(sizes)):
        if i + 2 < len(sizes):
            open_ring(i + 2)
        sum_ring(i)
        if i > 0:
            send_on(i - 1)

    squares = []
    column = jnp.zeros((1, columns_local), jnp.float32)
    for mine, blocks in zip(kept, received):
        squared, column = combine(mine[0], blocks, column)
        squares.append(squared)
    column = lax.psum(column, "row")
    out = normalise(column, squares, rows_local * n_rows)
    return out.reshape(rows_local, 1, columns_local)


def solution(mesh):
    return jax.shard_map(
        per_device,
        mesh=mesh,
        in_specs=(
            P("row", "layer", "col"),
            P("row", "layer", "col"),
            P(("layer", "row"), None, "col"),
            P(("layer", "row"), None, "col"),
        ),
        out_specs=P("row", "layer", "col"),
        check_vma=False,
    )
```

```python
import functools
import math

import jax
import jax.numpy as jnp
from jax import lax
from jax.experimental import pallas as pl
from jax.experimental.layout import Layout, with_layout_constraint
from jax.experimental.pallas import tpu as pltpu
from jax.sharding import PartitionSpec as P

TILE = 256
SIXTEENTHS = (4, 4, 3, 3, 2)
SCALE_ROWS = 16
CODE = 64.0
TOP = 32767.0
LEAST = 2.0**-100
VMEM = pl.BlockSpec(memory_space=pltpu.VMEM)
PARAMS = pltpu.CompilerParams(vmem_limit_bytes=40 * 1024 * 1024)


def load_kernel(at, size, moving, pattern_ref, left_ref, *refs):
    outs = refs[-len(moving) :]
    for arrived, out, parts in zip(refs, outs, moving):
        done = 0
        for first, rows in parts:
            out[done : done + rows, :] = arrived[first : first + rows, :]
            done += rows
        step = math.gcd(TILE, math.gcd(at, size))
        for i in range(0, size, step):
            entry = pattern_ref[(at + i) // TILE].astype(jnp.float32).astype(out.dtype)
            block = left_ref[at + i : at + i + step, :] * entry
            out[done + i : done + i + step, :] = block


def load(left, pattern, at, size, arrived, moving, after):
    columns = left.shape[1]
    totals = [size + sum(rows for _, rows in parts) for parts in moving]
    return pl.pallas_call(
        functools.partial(load_kernel, at, size, moving),
        out_shape=[jax.ShapeDtypeStruct((total, columns), left.dtype) for total in totals],
        in_specs=[pl.BlockSpec(memory_space=pltpu.SMEM), VMEM]
        + [VMEM if parts else pl.BlockSpec(memory_space=pl.ANY) for parts in moving]
        + [pl.BlockSpec(memory_space=pl.ANY)] * len(after),
        out_specs=[VMEM] * len(moving),
        compiler_params=PARAMS,
        cost_estimate=pl.CostEstimate(
            flops=sum(totals) * columns,
            bytes_accessed=4 * sum(totals) * columns,
            transcendentals=0,
        ),
    )(pattern, left, *arrived, *after)


def put_fixed(ref, at, total):
    rows, columns = total.shape
    top = jnp.maximum(jnp.max(jnp.abs(total), axis=0, keepdims=True), LEAST)
    code = jnp.ceil(jnp.log2(top) * CODE + 0.01)
    fixed = jnp.round(total * (jnp.exp2(code / -CODE) * TOP)).astype(jnp.int32)
    ref[at : at + rows, :] = fixed.astype(jnp.int16)
    codes = jnp.broadcast_to(code.astype(jnp.int32), (SCALE_ROWS, columns))
    ref[at + rows : at + rows + SCALE_ROWS, :] = codes.astype(jnp.int16)


def get_fixed(ref, at, rows):
    code = ref[at + rows : at + rows + SCALE_ROWS, :].astype(jnp.int32)[:1].astype(jnp.float32)
    unit = jnp.exp2(code / CODE) * (1.0 / TOP)
    return ref[at : at + rows, :].astype(jnp.int32).astype(jnp.float32) * unit


def partial_kernel(rows, firsts, n_pieces, kept, sent, where, *refs):
    n_sources = len(firsts)
    lefts, pieces = refs[:n_sources], refs[n_sources : n_sources + n_pieces]
    outs = refs[-len(kept) - len(sent) :]
    columns = pieces[0].shape[2]

    def right(source, layer):
        start = pl.multiple_of(where[2 + 2 * source], TILE)
        tile = pieces[0][layer, pl.ds(start, TILE), :]
        for i in range(1, n_pieces):
            here = where[1 + 2 * source] == i
            tile = jnp.where(here, pieces[i][layer, pl.ds(start, TILE), :], tile)
        return tile

    def product(k):
        total = jnp.zeros((rows, columns), jnp.float32)
        for source in range(n_sources):
            total += jnp.dot(
                lefts[source][firsts[source] : firsts[source] + rows, :],
                right(source, where[0] ^ k),
                preferred_element_type=jnp.float32,
            )
        return total

    for out, ks in zip(outs[len(kept) :], sent):
        for i, k in enumerate(ks):
            put_fixed(out, i * (rows + SCALE_ROWS), product(k))
    for out, k in zip(outs, kept):
        out[...] = product(k)


def partial_products(where, lefts, rows, pieces, after, kept, sent):
    columns = pieces[0].shape[2]
    firsts = tuple(first for _, first in lefts)
    n_products = len(kept) + sum(len(ks) for ks in sent)
    outs = [jax.ShapeDtypeStruct((rows, columns), jnp.float32)] * len(kept)
    outs += [
        jax.ShapeDtypeStruct((len(ks) * (rows + SCALE_ROWS), columns), jnp.int16) for ks in sent
    ]
    out = pl.pallas_call(
        functools.partial(partial_kernel, rows, firsts, len(pieces), kept, sent),
        out_shape=outs,
        in_specs=[pl.BlockSpec(memory_space=pltpu.SMEM)]
        + [VMEM] * (len(lefts) + len(pieces))
        + [pl.BlockSpec(memory_space=pl.ANY)] * len(after),
        out_specs=[VMEM] * len(outs),
        compiler_params=PARAMS,
        cost_estimate=pl.CostEstimate(
            flops=2 * rows * len(lefts) * TILE * columns * n_products,
            bytes_accessed=len(pieces) * pieces[0].size * 2 + rows * columns * 14,
            transcendentals=0,
        ),
    )(where, *(block for block, _ in lefts), *pieces, *after)
    return out[: len(kept)], out[len(kept) :]


def pass_on_kernel(kept_ref, received_ref, after_ref, out_ref):
    rows = kept_ref.shape[0]
    total = kept_ref[...] + get_fixed(received_ref, rows + SCALE_ROWS, rows)
    put_fixed(out_ref, 0, total)


def pass_on(kept, received, after):
    rows, columns = kept.shape
    return pl.pallas_call(
        pass_on_kernel,
        out_shape=jax.ShapeDtypeStruct((rows + SCALE_ROWS, columns), jnp.int16),
        in_specs=[VMEM, VMEM, pl.BlockSpec(memory_space=pl.ANY)],
        out_specs=VMEM,
        compiler_params=PARAMS,
        cost_estimate=pl.CostEstimate(
            flops=10 * kept.size, bytes_accessed=8 * kept.size, transcendentals=0
        ),
    )(kept, received, after)


def combine_kernel(n_received, kept_ref, *refs):
    received, before_ref = refs[:n_received], refs[n_received]
    squared_ref, sum_ref = refs[-2:]
    total = kept_ref[...]
    for block in received:
        total += get_fixed(block, 0, total.shape[0])
    squared = total * total
    squared_ref[...] = squared
    sum_ref[...] = before_ref[...] + jnp.sum(squared, axis=0, keepdims=True)


def combine(kept, received, before, after):
    return pl.pallas_call(
        functools.partial(combine_kernel, len(received)),
        out_shape=(
            jax.ShapeDtypeStruct(kept.shape, jnp.float32),
            jax.ShapeDtypeStruct((1, kept.shape[1]), jnp.float32),
        ),
        in_specs=[VMEM] * (2 + len(received)) + [pl.BlockSpec(memory_space=pl.ANY)] * len(after),
        out_specs=(VMEM, VMEM),
        compiler_params=PARAMS,
        cost_estimate=pl.CostEstimate(
            flops=8 * kept.size, bytes_accessed=kept.size * 14, transcendentals=0
        ),
    )(kept, *received, before, *after)


def normalise_kernel(n_chunks, rows_total, column_ref, *refs):
    chunks, out_ref = refs[:n_chunks], refs[n_chunks]
    colmean = column_ref[...] / rows_total
    at = 0
    for chunk in chunks:
        rows = chunk.shape[0]
        out_ref[at : at + rows, :] = (chunk[...] / (colmean + 1e-06)).astype(jnp.bfloat16)
        at += rows


def normalise(column, chunks, rows_total):
    rows, columns = sum(chunk.shape[0] for chunk in chunks), chunks[0].shape[1]
    return pl.pallas_call(
        functools.partial(normalise_kernel, len(chunks), rows_total),
        out_shape=jax.ShapeDtypeStruct((rows, columns), jnp.bfloat16),
        in_specs=[VMEM] * (1 + len(chunks)),
        out_specs=VMEM,
        compiler_params=PARAMS,
        cost_estimate=pl.CostEstimate(
            flops=4 * rows * columns,
            bytes_accessed=6 * rows * columns,
            transcendentals=0,
        ),
    )(column, *chunks)


def expand_tiles(values, pattern):
    tile_rows, layers, tile_cols = pattern.shape
    tile_size = values.shape[0] // tile_rows
    blocks = values.reshape(tile_rows, tile_size, layers, tile_cols, tile_size)
    blocks = blocks * pattern[:, None, :, :, None].astype(values.dtype)
    return blocks.reshape(values.shape)


def shift(x, axis, by):
    n = lax.axis_size(axis)
    return lax.ppermute(x, axis, [(i, (i + by) % n) for i in range(n)])


def as_it_lies(x):
    return with_layout_constraint(x, Layout(tuple(range(x.ndim))))


def swap(x, bits):
    return lax.ppermute(x, "layer", [(i, i ^ bits) for i in range(4)])


def per_device(left_values, left_pattern, right_values, right_pattern):
    n_rows, n_cols = lax.axis_size("row"), lax.axis_size("col")
    layer, row, col = (lax.axis_index(a) for a in ("layer", "row", "col"))
    rows_local, _, columns_local = left_values.shape
    inner_piece = right_values.shape[0]
    sizes = [rows_local * part // sum(SIXTEENTHS) for part in SIXTEENTHS]

    left = left_values.reshape(rows_local, columns_local)
    pattern = left_pattern.reshape(-1)
    reach = (n_cols // 2, n_cols - 1 - n_cols // 2)
    where = [layer]
    for source in [0] + [-1 - i for i in range(reach[0])] + [1 + i for i in range(reach[1])]:
        inner = (col + source + n_cols) % n_cols * columns_local
        where += [(row - inner // inner_piece + n_rows) % n_rows, inner % inner_piece]
    where = jnp.stack(where).astype(jnp.int32)

    starts = [sum(sizes[:i]) for i in range(len(sizes))]
    own = []
    found = [([], []) for _ in sizes]
    kept, received, last = [], [], []

    def open_slot(slot):
        at, size = (starts[slot], sizes[slot]) if slot < len(sizes) else (0, 0)
        going = [d for d in (0, 1) if slot < len(sizes) - 1 + reach[d]]
        arrived, moving, riders = [], [], []
        for d in going:
            on = [c for c in range(min(slot, len(sizes))) if len(found[c][d]) < reach[d]]
            arrived.append(found[on[0]][d][-1][0] if on else left)
            moving.append(tuple((found[c][d][-1][1], sizes[c]) for c in on))
            riders.append(on + ([slot] if size else []))
        blocks = load(left, pattern, at, size, arrived, moving, last)
        last[:] = [blocks[0]]
        for d, block, chunks in zip(going, blocks, riders):
            got, first = shift(block, "col", 1 - 2 * d), 0
            for c in chunks:
                found[c][d].append((got, first))
                if c == slot and d == going[-1]:
                    own.append((block, first))
                first += sizes[c]

    def sum_chunk(i):
        if i + 1 < len(sizes):
            ks, sent_ks = (0, second(i)), ((3 - second(i), 3),)
        else:
            ks, sent_ks = (0,), ((1,), (2,), (3,))
        mine, sent = partial_products(
            where, [own[i], *found[i][0], *found[i][1]], sizes[i], pieces, last, ks, sent_ks
        )
        kept.append(mine)
        received.append([swap(x, k[0]) for x, k in zip(sent, sent_ks)])
        last[:] = [mine[0]]

    def second(i):
        return 2 - i % 2

    def send_on(i):
        block = pass_on(kept[i][1], received[i][0], last[0])
        received[i].append(swap(block, second(i)))
        last[:] = [block]

    pieces = []
    for i in range(n_rows):
        values, tiles = right_values, right_pattern
        if i:
            values, tiles = as_it_lies(shift(values, "row", i)), shift(tiles, "row", i)
        pieces.append(expand_tiles(values, tiles).transpose(1, 0, 2))

    squares, columns = [], [jnp.zeros((1, columns_local), jnp.float32)]

    def square(i):
        squared, column = combine(kept[i][0], received[i], columns[-1], last)
        squares.append(squared)
        columns.append(column)
        last[:] = [column]

    open_slot(0)
    open_slot(1)
    last += pieces
    for i in range(len(sizes)):
        while len(own) < len(sizes) and len(own) <= i + reach[0]:
            open_slot(len(own))
        if i + reach[0] >= len(sizes) and i + reach[0] < len(sizes) - 1 + reach[0]:
            open_slot(i + reach[0])
        sum_chunk(i)
        if i > 0:
            send_on(i - 1)
        if i > 1:
            square(i - 2)
    square(len(sizes) - 2)
    square(len(sizes) - 1)

    column = lax.psum(columns[-1], "row")
    out = normalise(column, squares, rows_local * n_rows)
    return out.reshape(rows_local, 1, columns_local)


def solution(mesh):
    return jax.shard_map(
        per_device,
        mesh=mesh,
        in_specs=(
            P("row", "layer", "col"),
            P("row", "layer", "col"),
            P(("layer", "row"), None, "col"),
            P(("layer", "row"), None, "col"),
        ),
        out_specs=P("row", "layer", "col"),
        check_vma=False,
    )
```

```python
import functools
import math

import jax
import jax.numpy as jnp
from jax import lax
from jax.experimental import pallas as pl
from jax.experimental.layout import Layout, with_layout_constraint
from jax.experimental.pallas import tpu as pltpu
from jax.sharding import PartitionSpec as P

TILE = 256
SIXTEENTHS = (3, 4, 4, 3, 2)
SCALE_ROWS = 16
CODE = 64.0
TOP = 32767.0
LEAST = 2.0**-100
VMEM = pl.BlockSpec(memory_space=pltpu.VMEM)
PARAMS = pltpu.CompilerParams(vmem_limit_bytes=16 * 1024 * 1024)


def load_kernel(at, size, parts, pattern_ref, left_ref, arrived, *refs):
    out = refs[-1]
    done = 0
    for first, rows in parts:
        out[done : done + rows, :] = arrived[first : first + rows, :]
        done += rows
    step = math.gcd(TILE, math.gcd(at, size))
    for i in range(0, size, step):
        entry = pattern_ref[(at + i) // TILE].astype(jnp.float32).astype(out.dtype)
        out[done + i : done + i + step, :] = left_ref[at + i : at + i + step, :] * entry


def load(left, pattern, at, size, arrived, parts, after):
    columns = left.shape[1]
    total = size + sum(rows for _, rows in parts)
    return pl.pallas_call(
        functools.partial(load_kernel, at, size, parts),
        out_shape=jax.ShapeDtypeStruct((total, columns), left.dtype),
        in_specs=[pl.BlockSpec(memory_space=pltpu.SMEM), VMEM]
        + [VMEM if parts else pl.BlockSpec(memory_space=pl.ANY)]
        + [pl.BlockSpec(memory_space=pl.ANY)] * len(after),
        out_specs=VMEM,
        compiler_params=PARAMS,
        cost_estimate=pl.CostEstimate(
            flops=total * columns, bytes_accessed=4 * total * columns, transcendentals=0
        ),
    )(pattern, left, arrived, *after)


def put_fixed(ref, at, total):
    rows, columns = total.shape
    top = jnp.maximum(jnp.max(jnp.abs(total), axis=0, keepdims=True), LEAST)
    code = jnp.ceil(jnp.log2(top) * CODE + 0.01)
    fixed = jnp.round(total * (jnp.exp2(code / -CODE) * TOP)).astype(jnp.int32)
    ref[at : at + rows, :] = fixed.astype(jnp.int16)
    codes = jnp.broadcast_to(code.astype(jnp.int32), (SCALE_ROWS, columns))
    ref[at + rows : at + rows + SCALE_ROWS, :] = codes.astype(jnp.int16)


def get_fixed(ref, at, rows):
    code = ref[at + rows : at + rows + SCALE_ROWS, :].astype(jnp.int32)[:1].astype(jnp.float32)
    unit = jnp.exp2(code / CODE) * (1.0 / TOP)
    return ref[at : at + rows, :].astype(jnp.int32).astype(jnp.float32) * unit


def partial_kernel(sources, n_pieces, kept, sent, where, *refs):
    n_lefts = sum(len(parts) for parts in sources)
    pieces = refs[n_lefts : n_lefts + n_pieces]
    rows = sum(part[2] for part in sources[0])
    outs = refs[-len(kept) - len(sent) :]
    columns = pieces[0].shape[2]

    def right(source, layer):
        start = pl.multiple_of(where[2 + 2 * source], TILE)
        tile = pieces[0][layer, pl.ds(start, TILE), :]
        for i in range(1, n_pieces):
            here = where[1 + 2 * source] == i
            tile = jnp.where(here, pieces[i][layer, pl.ds(start, TILE), :], tile)
        return tile

    def product(k):
        total = jnp.zeros((rows, columns), jnp.float32)
        for source, parts in enumerate(sources):
            tile = right(source, where[0] ^ k)
            terms = [
                jnp.dot(
                    refs[i][first : first + count, :], tile, preferred_element_type=jnp.float32
                )
                for i, first, count in parts
            ]
            total += terms[0] if len(terms) == 1 else jnp.concatenate(terms, axis=0)
        return total

    for out, ks in zip(outs[len(kept) :], sent):
        for i, k in enumerate(ks):
            put_fixed(out, i * (rows + SCALE_ROWS), product(k))
    for out, k in zip(outs, kept):
        out[...] = product(k)


def partial_products(where, sources, pieces, after, kept, sent):
    columns = pieces[0].shape[2]
    rows = sum(part[2] for part in sources[0])
    lefts = [array for parts in sources for array, _, _ in parts]
    numbers = iter(range(len(lefts)))
    shapes = tuple(tuple((next(numbers), *part[1:]) for part in parts) for parts in sources)
    n_products = len(kept) + sum(len(ks) for ks in sent)
    outs = [jax.ShapeDtypeStruct((rows, columns), jnp.float32)] * len(kept)
    outs += [
        jax.ShapeDtypeStruct((len(ks) * (rows + SCALE_ROWS), columns), jnp.int16) for ks in sent
    ]
    out = pl.pallas_call(
        functools.partial(partial_kernel, shapes, len(pieces), kept, sent),
        out_shape=outs,
        in_specs=[pl.BlockSpec(memory_space=pltpu.SMEM)]
        + [VMEM] * (len(lefts) + len(pieces))
        + [pl.BlockSpec(memory_space=pl.ANY)] * len(after),
        out_specs=[VMEM] * len(outs),
        compiler_params=PARAMS,
        cost_estimate=pl.CostEstimate(
            flops=2 * rows * len(sources) * TILE * columns * n_products,
            bytes_accessed=len(pieces) * pieces[0].size * 2 + rows * columns * 14,
            transcendentals=0,
        ),
    )(where, *lefts, *pieces, *after)
    return out[: len(kept)], out[len(kept) :]


def pass_on_kernel(kept_ref, received_ref, after_ref, out_ref):
    rows = kept_ref.shape[0]
    total = kept_ref[...] + get_fixed(received_ref, rows + SCALE_ROWS, rows)
    put_fixed(out_ref, 0, total)


def pass_on(kept, received, after):
    rows, columns = kept.shape
    return pl.pallas_call(
        pass_on_kernel,
        out_shape=jax.ShapeDtypeStruct((rows + SCALE_ROWS, columns), jnp.int16),
        in_specs=[VMEM, VMEM, pl.BlockSpec(memory_space=pl.ANY)],
        out_specs=VMEM,
        compiler_params=PARAMS,
        cost_estimate=pl.CostEstimate(
            flops=10 * kept.size, bytes_accessed=8 * kept.size, transcendentals=0
        ),
    )(kept, received, after)


def combine_kernel(n_received, kept_ref, *refs):
    received, before_ref = refs[:n_received], refs[n_received]
    squared_ref, sum_ref = refs[-2:]
    total = kept_ref[...]
    for block in received:
        total += get_fixed(block, 0, total.shape[0])
    squared = total * total
    squared_ref[...] = squared
    sum_ref[...] = before_ref[...] + jnp.sum(squared, axis=0, keepdims=True)


def combine(kept, received, before, after):
    return pl.pallas_call(
        functools.partial(combine_kernel, len(received)),
        out_shape=(
            jax.ShapeDtypeStruct(kept.shape, jnp.float32),
            jax.ShapeDtypeStruct((1, kept.shape[1]), jnp.float32),
        ),
        in_specs=[VMEM] * (2 + len(received)) + [pl.BlockSpec(memory_space=pl.ANY)] * len(after),
        out_specs=(VMEM, VMEM),
        compiler_params=PARAMS,
        cost_estimate=pl.CostEstimate(
            flops=8 * kept.size, bytes_accessed=kept.size * 14, transcendentals=0
        ),
    )(kept, *received, before, *after)


def normalise_kernel(n_chunks, rows_total, column_ref, *refs):
    chunks, out_ref = refs[:n_chunks], refs[n_chunks]
    colmean = column_ref[...] / rows_total
    at = 0
    for chunk in chunks:
        rows = chunk.shape[0]
        out_ref[at : at + rows, :] = (chunk[...] / (colmean + 1e-06)).astype(jnp.bfloat16)
        at += rows


def normalise(column, chunks, rows_total):
    rows, columns = sum(chunk.shape[0] for chunk in chunks), chunks[0].shape[1]
    return pl.pallas_call(
        functools.partial(normalise_kernel, len(chunks), rows_total),
        out_shape=jax.ShapeDtypeStruct((rows, columns), jnp.bfloat16),
        in_specs=[VMEM] * (1 + len(chunks)),
        out_specs=VMEM,
        compiler_params=PARAMS,
        cost_estimate=pl.CostEstimate(
            flops=4 * rows * columns,
            bytes_accessed=6 * rows * columns,
            transcendentals=0,
        ),
    )(column, *chunks)


def expand_tiles(values, pattern):
    tile_rows, layers, tile_cols = pattern.shape
    tile_size = values.shape[0] // tile_rows
    blocks = values.reshape(tile_rows, tile_size, layers, tile_cols, tile_size)
    blocks = blocks * pattern[:, None, :, :, None].astype(values.dtype)
    return blocks.reshape(values.shape)


def shift(x, axis, by):
    n = lax.axis_size(axis)
    return lax.ppermute(x, axis, [(i, (i + by) % n) for i in range(n)])


def as_it_lies(x):
    return with_layout_constraint(x, Layout(tuple(range(x.ndim))))


def swap(x, bits):
    return lax.ppermute(x, "layer", [(i, i ^ bits) for i in range(4)])


def per_device(left_values, left_pattern, right_values, right_pattern):
    n_rows, n_cols = lax.axis_size("row"), lax.axis_size("col")
    layer, row, col = (lax.axis_index(a) for a in ("layer", "row", "col"))
    rows_local, _, columns_local = left_values.shape
    inner_piece = right_values.shape[0]
    sizes = [rows_local * part // sum(SIXTEENTHS) for part in SIXTEENTHS]

    left = left_values.reshape(rows_local, columns_local)
    pattern = left_pattern.reshape(-1)
    reach = n_cols // 2
    away = list(range(1, reach))
    where = [layer]
    for source in [0] + [-i for i in away] + away + [reach]:
        inner = (col + source + n_cols) % n_cols * columns_local
        where += [(row - inner // inner_piece + n_rows) % n_rows, inner % inner_piece]
    where = jnp.stack(where).astype(jnp.int32)

    starts = [sum(sizes[:i]) for i in range(len(sizes))]
    own = []
    found = [([], []) for _ in sizes]
    kept, received, last = [], [], []

    def open_slot(slot):
        at, size = (starts[slot], sizes[slot]) if slot < len(sizes) else (0, 0)
        for d in (0, 1):
            riders = [c for c in range(min(slot, len(sizes))) if len(found[c][d]) < reach]
            parts = []
            for c in riders:
                _, first, rows = found[c][d][-1]
                if len(found[c][d]) == reach - 1:
                    first, rows = first + d * (rows // 2), rows // 2
                parts.append((first, rows))
            arrived = found[riders[0]][d][-1][0] if riders else left
            block = load(left, pattern, at, size, arrived, tuple(parts), last)
            last[:] = [block]
            got = shift(block, "col", 1 - 2 * d)
            first = 0
            for c, (_, rows) in zip(riders, parts):
                found[c][d].append((got, first, rows))
                first += rows
            if size:
                found[slot][d].append((got, first, size))
                if d == 0:
                    own.append((block, first, size))

    def sources(i):
        (*below, last_below), (*above, last_above) = found[i]
        near = [own[i]] + below + above
        return [[part] for part in near] + [[last_below, last_above]]

    def sum_chunk(i):
        if i + 1 < len(sizes):
            ks, sent_ks = (0, second(i)), ((3 - second(i), 3),)
        else:
            ks, sent_ks = (0,), ((1,), (2,), (3,))
        mine, sent = partial_products(where, sources(i), pieces, last, ks, sent_ks)
        kept.append(mine)
        received.append([swap(x, k[0]) for x, k in zip(sent, sent_ks)])
        last[:] = [mine[0]]

    def second(i):
        return 2 - i % 2

    def send_on(i):
        block = pass_on(kept[i][1], received[i][0], last[0])
        received[i].append(swap(block, second(i)))
        last[:] = [block]

    pieces = []
    for i in range(n_rows):
        values, tiles = right_values, right_pattern
        if i:
            values, tiles = as_it_lies(shift(values, "row", i)), shift(tiles, "row", i)
        pieces.append(expand_tiles(values, tiles).transpose(1, 0, 2))

    squares, columns = [], [jnp.zeros((1, columns_local), jnp.float32)]

    def square(i):
        squared, column = combine(kept[i][0], received[i], columns[-1], last)
        squares.append(squared)
        columns.append(column)
        last[:] = [column]

    opened = 0
    for i in range(len(sizes)):
        while opened < min(len(sizes) + reach - 1, i + reach + 1):
            open_slot(opened)
            opened += 1
            if opened == 2:
                last += pieces
        sum_chunk(i)
        if i > 0:
            send_on(i - 1)
        if i > 1:
            square(i - 2)
    square(len(sizes) - 2)
    square(len(sizes) - 1)

    column = lax.psum(columns[-1], "row")
    out = normalise(column, squares, rows_local * n_rows)
    return out.reshape(rows_local, 1, columns_local)


def solution(mesh):
    return jax.shard_map(
        per_device,
        mesh=mesh,
        in_specs=(
            P("row", "layer", "col"),
            P("row", "layer", "col"),
            P(("layer", "row"), None, "col"),
            P(("layer", "row"), None, "col"),
        ),
        out_specs=P("row", "layer", "col"),
        check_vma=False,
    )
```

```python
import functools
import math

import jax
import jax.numpy as jnp
from jax import lax
from jax.experimental import pallas as pl
from jax.experimental.pallas import tpu as pltpu
from jax.sharding import PartitionSpec as P

TILE = 256
SIXTEENTHS = (3, 4, 4, 3, 2)
SCALE_ROWS = 16
CODE = 64.0
TOP = 32767.0
LEAST = 2.0**-100
VMEM = pl.BlockSpec(memory_space=pltpu.VMEM)
PARAMS = pltpu.CompilerParams(vmem_limit_bytes=16 * 1024 * 1024)


def cost(flops, bytes_accessed):
    return pl.CostEstimate(flops=flops, bytes_accessed=bytes_accessed, transcendentals=0)


def load_kernel(at, size, parts, pattern_ref, left_ref, arrived, *refs):
    out = refs[-1]
    done = 0
    for first, rows in parts:
        out[done : done + rows, :] = arrived[first : first + rows, :]
        done += rows
    step = math.gcd(TILE, math.gcd(at, size))
    for i in range(0, size, step):
        entry = pattern_ref[(at + i) // TILE].astype(jnp.float32).astype(out.dtype)
        out[done + i : done + i + step, :] = left_ref[at + i : at + i + step, :] * entry


def load(left, pattern, at, size, arrived, parts, after):
    columns = left.shape[1]
    total = size + sum(rows for _, rows in parts)
    return pl.pallas_call(
        functools.partial(load_kernel, at, size, parts),
        out_shape=jax.ShapeDtypeStruct((total, columns), left.dtype),
        in_specs=[pl.BlockSpec(memory_space=pltpu.SMEM), VMEM]
        + [VMEM if parts else pl.BlockSpec(memory_space=pl.ANY)]
        + [pl.BlockSpec(memory_space=pl.ANY)] * len(after),
        out_specs=VMEM,
        compiler_params=PARAMS,
        cost_estimate=cost(total * columns, 4 * total * columns),
    )(pattern, left, arrived, *after)


def mask_right_kernel(pattern_ref, values_ref, *refs):
    out = refs[-1]
    layers, rows, _ = out.shape
    for i in range(0, rows, TILE):
        block = jnp.swapaxes(values_ref[i : i + TILE].astype(jnp.float32), 0, 1)
        for j in range(layers):
            entry = pattern_ref[i // TILE, j].astype(jnp.float32)
            out[j, i : i + TILE, :] = (block[j] * entry).astype(out.dtype)


def mask_right(pattern, values, after):
    rows, layers, columns = values.shape
    return pl.pallas_call(
        mask_right_kernel,
        out_shape=jax.ShapeDtypeStruct((layers, rows, columns), values.dtype),
        in_specs=[pl.BlockSpec(memory_space=pltpu.SMEM), VMEM]
        + [pl.BlockSpec(memory_space=pl.ANY)] * len(after),
        out_specs=VMEM,
        compiler_params=PARAMS,
        cost_estimate=cost(values.size, 4 * values.size),
    )(pattern.reshape(rows // TILE, layers), values, *after)


def put_fixed(ref, at, total):
    rows, columns = total.shape
    top = jnp.maximum(jnp.max(jnp.abs(total), axis=0, keepdims=True), LEAST)
    code = jnp.ceil(jnp.log2(top) * CODE + 0.01)
    fixed = jnp.round(total * (jnp.exp2(code / -CODE) * TOP)).astype(jnp.int32)
    ref[at : at + rows, :] = fixed.astype(jnp.int16)
    codes = jnp.broadcast_to(code.astype(jnp.int32), (SCALE_ROWS, columns))
    ref[at + rows : at + rows + SCALE_ROWS, :] = codes.astype(jnp.int16)


def get_fixed(ref, at, rows):
    code = ref[at + rows : at + rows + SCALE_ROWS, :].astype(jnp.int32)[:1].astype(jnp.float32)
    unit = jnp.exp2(code / CODE) * (1.0 / TOP)
    return ref[at : at + rows, :].astype(jnp.int32).astype(jnp.float32) * unit


def partial_kernel(sources, n_pieces, kept, sent, where, *refs):
    n_lefts = sum(len(parts) for parts in sources)
    pieces = refs[n_lefts : n_lefts + n_pieces]
    rows = sum(part[2] for part in sources[0])
    outs = refs[-len(kept) - len(sent) :]
    columns = pieces[0].shape[2]

    def right(source, layer):
        start = pl.multiple_of(where[2 + 2 * source], TILE)
        tile = pieces[0][layer, pl.ds(start, TILE), :]
        for i in range(1, n_pieces):
            here = where[1 + 2 * source] == i
            tile = jnp.where(here, pieces[i][layer, pl.ds(start, TILE), :], tile)
        return tile

    def product(k):
        total = jnp.zeros((rows, columns), jnp.float32)
        for source, parts in enumerate(sources):
            tile = right(source, where[0] ^ k)
            terms = [
                jnp.dot(
                    refs[i][first : first + count, :], tile, preferred_element_type=jnp.float32
                )
                for i, first, count in parts
            ]
            total += terms[0] if len(terms) == 1 else jnp.concatenate(terms, axis=0)
        return total

    for out, ks in zip(outs[len(kept) :], sent):
        for i, k in enumerate(ks):
            put_fixed(out, i * (rows + SCALE_ROWS), product(k))
    for out, k in zip(outs, kept):
        out[...] = product(k)


def partial_products(where, sources, pieces, after, kept, sent):
    columns = pieces[0].shape[2]
    rows = sum(part[2] for part in sources[0])
    lefts = [array for parts in sources for array, _, _ in parts]
    numbers = iter(range(len(lefts)))
    shapes = tuple(tuple((next(numbers), *part[1:]) for part in parts) for parts in sources)
    n_products = len(kept) + sum(len(ks) for ks in sent)
    outs = [jax.ShapeDtypeStruct((rows, columns), jnp.float32)] * len(kept)
    outs += [
        jax.ShapeDtypeStruct((len(ks) * (rows + SCALE_ROWS), columns), jnp.int16) for ks in sent
    ]
    out = pl.pallas_call(
        functools.partial(partial_kernel, shapes, len(pieces), kept, sent),
        out_shape=outs,
        in_specs=[pl.BlockSpec(memory_space=pltpu.SMEM)]
        + [VMEM] * (len(lefts) + len(pieces))
        + [pl.BlockSpec(memory_space=pl.ANY)] * len(after),
        out_specs=[VMEM] * len(outs),
        compiler_params=PARAMS,
        cost_estimate=cost(
            2 * rows * len(sources) * TILE * columns * n_products,
            2 * len(pieces) * pieces[0].size + 14 * rows * columns,
        ),
    )(where, *lefts, *pieces, *after)
    return out[: len(kept)], out[len(kept) :]


def pass_on_kernel(kept_ref, received_ref, after_ref, out_ref):
    rows = kept_ref.shape[0]
    total = kept_ref[...] + get_fixed(received_ref, rows + SCALE_ROWS, rows)
    put_fixed(out_ref, 0, total)


def pass_on(kept, received, after):
    rows, columns = kept.shape
    return pl.pallas_call(
        pass_on_kernel,
        out_shape=jax.ShapeDtypeStruct((rows + SCALE_ROWS, columns), jnp.int16),
        in_specs=[VMEM, VMEM, pl.BlockSpec(memory_space=pl.ANY)],
        out_specs=VMEM,
        compiler_params=PARAMS,
        cost_estimate=cost(10 * kept.size, 8 * kept.size),
    )(kept, received, after)


def combine_kernel(n_received, kept_ref, *refs):
    received, before_ref = refs[:n_received], refs[n_received]
    squared_ref, sum_ref = refs[-2:]
    total = kept_ref[...]
    for block in received:
        total += get_fixed(block, 0, total.shape[0])
    squared = total * total
    squared_ref[...] = squared
    sum_ref[...] = before_ref[...] + jnp.sum(squared, axis=0, keepdims=True)


def combine(kept, received, before, after):
    return pl.pallas_call(
        functools.partial(combine_kernel, len(received)),
        out_shape=(
            jax.ShapeDtypeStruct(kept.shape, jnp.float32),
            jax.ShapeDtypeStruct((1, kept.shape[1]), jnp.float32),
        ),
        in_specs=[VMEM] * (2 + len(received)) + [pl.BlockSpec(memory_space=pl.ANY)] * len(after),
        out_specs=(VMEM, VMEM),
        compiler_params=PARAMS,
        cost_estimate=cost(8 * kept.size, 14 * kept.size),
    )(kept, *received, before, *after)


def normalise_kernel(n_chunks, rows_total, column_ref, *refs):
    chunks, out_ref = refs[:n_chunks], refs[n_chunks]
    colmean = column_ref[...] / rows_total
    at = 0
    for chunk in chunks:
        rows = chunk.shape[0]
        out_ref[at : at + rows, :] = (chunk[...] / (colmean + 1e-06)).astype(jnp.bfloat16)
        at += rows


def normalise(column, chunks, rows_total):
    rows, columns = sum(chunk.shape[0] for chunk in chunks), chunks[0].shape[1]
    return pl.pallas_call(
        functools.partial(normalise_kernel, len(chunks), rows_total),
        out_shape=jax.ShapeDtypeStruct((rows, columns), jnp.bfloat16),
        in_specs=[VMEM] * (1 + len(chunks)),
        out_specs=VMEM,
        compiler_params=PARAMS,
        cost_estimate=cost(4 * rows * columns, 6 * rows * columns),
    )(column, *chunks)


def shift(x, axis, by):
    n = lax.axis_size(axis)
    return lax.ppermute(x, axis, [(i, (i + by) % n) for i in range(n)])


def swap(x, bits):
    return lax.ppermute(x, "layer", [(i, i ^ bits) for i in range(4)])


def per_device(left_values, left_pattern, right_values, right_pattern):
    n_rows, n_cols = lax.axis_size("row"), lax.axis_size("col")
    layer, row, col = (lax.axis_index(a) for a in ("layer", "row", "col"))
    rows_local, _, columns_local = left_values.shape
    inner_piece = right_values.shape[0]
    sizes = [rows_local * part // sum(SIXTEENTHS) for part in SIXTEENTHS]

    left = left_values.reshape(rows_local, columns_local)
    pattern = left_pattern.reshape(-1)
    reach = n_cols // 2
    away = list(range(1, reach))
    where = [layer]
    for source in [0] + [-i for i in away] + away + [reach]:
        inner = (col + source + n_cols) % n_cols * columns_local
        where += [(row - inner // inner_piece + n_rows) % n_rows, inner % inner_piece]
    where = jnp.stack(where).astype(jnp.int32)

    starts = [sum(sizes[:i]) for i in range(len(sizes))]
    own = []
    found = [([], []) for _ in sizes]
    kept, received, last = [], [], []

    def open_slot(slot):
        at, size = (starts[slot], sizes[slot]) if slot < len(sizes) else (0, 0)
        for d in (0, 1):
            riders = [c for c in range(min(slot, len(sizes))) if len(found[c][d]) < reach]
            parts = []
            for c in riders:
                _, first, rows = found[c][d][-1]
                if len(found[c][d]) == reach - 1:
                    first, rows = first + d * (rows // 2), rows // 2
                parts.append((first, rows))
            arrived = found[riders[0]][d][-1][0] if riders else left
            block = load(left, pattern, at, size, arrived, tuple(parts), last)
            last[:] = [block]
            got = shift(block, "col", 1 - 2 * d)
            first = 0
            for c, (_, rows) in zip(riders, parts):
                found[c][d].append((got, first, rows))
                first += rows
            if size:
                found[slot][d].append((got, first, size))
                if d == 0:
                    own.append((block, first, size))

    def sources(i):
        (*below, last_below), (*above, last_above) = found[i]
        return [[part] for part in [own[i]] + below + above] + [[last_below, last_above]]

    def sum_chunk(i):
        if i + 1 < len(sizes):
            ks, sent_ks = (0, second(i)), ((3 - second(i), 3),)
        else:
            ks, sent_ks = (0,), ((1,), (2,), (3,))
        mine, sent = partial_products(where, sources(i), pieces, last, ks, sent_ks)
        kept.append(mine)
        received.append([swap(x, k[0]) for x, k in zip(sent, sent_ks)])
        last[:] = [mine[0]]

    def second(i):
        return 2 - i % 2

    def send_on(i):
        block = pass_on(kept[i][1], received[i][0], last[0])
        received[i].append(swap(block, second(i)))
        last[:] = [block]

    raw = [(right_pattern, right_values)]
    for i in range(1, n_rows):
        raw.append((shift(right_pattern, "row", i), shift(right_values, "row", i)))
    pieces = []

    squares, columns = [], [jnp.zeros((1, columns_local), jnp.float32)]

    def square(i):
        squared, column = combine(kept[i][0], received[i], columns[-1], last)
        squares.append(squared)
        columns.append(column)
        last[:] = [column]

    opened = 0
    for i in range(len(sizes)):
        while opened < min(len(sizes) + reach - 1, i + reach + 1):
            open_slot(opened)
            opened += 1
            if opened == 2:
                for tiles, values in raw:
                    pieces.append(mask_right(tiles, values, last))
                    last[:] = pieces[-1:]
        sum_chunk(i)
        if i > 0:
            send_on(i - 1)
        if 1 < i < len(sizes) - 2:
            square(i - 2)
    for i in range(len(squares), len(sizes)):
        square(i)

    column = lax.psum(columns[-1], "row")
    out = normalise(column, squares, rows_local * n_rows)
    return out.reshape(rows_local, 1, columns_local)


def solution(mesh):
    return jax.shard_map(
        per_device,
        mesh=mesh,
        in_specs=(
            P("row", "layer", "col"),
            P("row", "layer", "col"),
            P(("layer", "row"), None, "col"),
            P(("layer", "row"), None, "col"),
        ),
        out_specs=P("row", "layer", "col"),
        check_vma=False,
    )
```

```python
import functools
import math

import jax
import jax.numpy as jnp
from jax import lax
from jax.experimental import pallas as pl
from jax.experimental.pallas import tpu as pltpu
from jax.sharding import PartitionSpec as P

TILE = 256
SIXTEENTHS = (3, 4, 4, 3, 2)
SCALE_ROWS = 16
CODE = 64.0
TOP = 32767.0
LEAST = 2.0**-100
VMEM = pl.BlockSpec(memory_space=pltpu.VMEM)
PARAMS = pltpu.CompilerParams(vmem_limit_bytes=16 * 1024 * 1024)


def cost(flops, bytes_accessed):
    return pl.CostEstimate(flops=flops, bytes_accessed=bytes_accessed, transcendentals=0)


def load_kernel(at, size, parts, pattern_ref, left_ref, arrived, *refs):
    out = refs[-1]
    done = 0
    for first, rows in parts:
        out[done : done + rows, :] = arrived[first : first + rows, :]
        done += rows
    step = math.gcd(TILE, math.gcd(at, size))
    for i in range(0, size, step):
        entry = pattern_ref[(at + i) // TILE].astype(jnp.float32).astype(out.dtype)
        out[done + i : done + i + step, :] = left_ref[at + i : at + i + step, :] * entry


def load(left, pattern, at, size, arrived, parts, after):
    columns = left.shape[1]
    total = size + sum(rows for _, rows in parts)
    return pl.pallas_call(
        functools.partial(load_kernel, at, size, parts),
        out_shape=jax.ShapeDtypeStruct((total, columns), left.dtype),
        in_specs=[pl.BlockSpec(memory_space=pltpu.SMEM), VMEM]
        + [VMEM if parts else pl.BlockSpec(memory_space=pl.ANY)]
        + [pl.BlockSpec(memory_space=pl.ANY)] * len(after),
        out_specs=VMEM,
        compiler_params=PARAMS,
        cost_estimate=cost(total * columns, 4 * total * columns),
    )(pattern, left, arrived, *after)


def mask_right_kernel(pattern_ref, values_ref, *refs):
    out = refs[-1]
    layers, rows, _ = out.shape
    for i in range(0, rows, TILE):
        block = jnp.swapaxes(values_ref[i : i + TILE].astype(jnp.float32), 0, 1)
        for j in range(layers):
            entry = pattern_ref[i // TILE, j].astype(jnp.float32)
            out[j, i : i + TILE, :] = (block[j] * entry).astype(out.dtype)


def mask_right(pattern, values, after):
    rows, layers, columns = values.shape
    return pl.pallas_call(
        mask_right_kernel,
        out_shape=jax.ShapeDtypeStruct((layers, rows, columns), values.dtype),
        in_specs=[pl.BlockSpec(memory_space=pltpu.SMEM), VMEM]
        + [pl.BlockSpec(memory_space=pl.ANY)] * len(after),
        out_specs=VMEM,
        compiler_params=PARAMS,
        cost_estimate=cost(values.size, 4 * values.size),
    )(pattern.reshape(rows // TILE, layers), values, *after)


def put_fixed(ref, at, total):
    rows, columns = total.shape
    top = jnp.maximum(jnp.max(jnp.abs(total), axis=0, keepdims=True), LEAST)
    code = jnp.ceil(jnp.log2(top) * CODE + 0.01)
    fixed = jnp.round(total * (jnp.exp2(code / -CODE) * TOP)).astype(jnp.int32)
    ref[at : at + rows, :] = fixed.astype(jnp.int16)
    codes = jnp.broadcast_to(code.astype(jnp.int32), (SCALE_ROWS, columns))
    ref[at + rows : at + rows + SCALE_ROWS, :] = codes.astype(jnp.int16)


def get_fixed(ref, at, rows):
    code = ref[at + rows : at + rows + SCALE_ROWS, :].astype(jnp.int32)[:1].astype(jnp.float32)
    unit = jnp.exp2(code / CODE) * (1.0 / TOP)
    return ref[at : at + rows, :].astype(jnp.int32).astype(jnp.float32) * unit


def partial_kernel(steps, sources, n_pieces, kept, sent, *refs):
    layer, row, col = (lax.axis_index(a) for a in ("layer", "row", "col"))
    n_cols = lax.axis_size("col")
    n_lefts = sum(len(parts) for parts in sources)
    pieces = refs[n_lefts : n_lefts + n_pieces]
    rows = sum(part[2] for part in sources[0])
    outs = refs[-len(kept) - len(sent) :]
    _, piece_rows, columns = pieces[0].shape

    def right(step, k):
        inner = lax.rem(col + (step + n_cols), n_cols) * TILE
        piece = lax.rem(row - lax.div(inner, piece_rows) + n_pieces, n_pieces)
        start = pl.multiple_of(lax.rem(inner, piece_rows), TILE)
        tile = pieces[0][layer ^ k, pl.ds(start, TILE), :]
        for i in range(1, n_pieces):
            tile = jnp.where(piece == i, pieces[i][layer ^ k, pl.ds(start, TILE), :], tile)
        return tile

    def product(k):
        total = jnp.zeros((rows, columns), jnp.float32)
        for step, parts in zip(steps, sources):
            tile = right(step, k)
            terms = [
                jnp.dot(
                    refs[i][first : first + count, :], tile, preferred_element_type=jnp.float32
                )
                for i, first, count in parts
            ]
            total += terms[0] if len(terms) == 1 else jnp.concatenate(terms, axis=0)
        return total

    for out, ks in zip(outs[len(kept) :], sent):
        for i, k in enumerate(ks):
            put_fixed(out, i * (rows + SCALE_ROWS), product(k))
    for out, k in zip(outs, kept):
        out[...] = product(k)


def partial_products(steps, sources, pieces, after, kept, sent):
    columns = pieces[0].shape[2]
    rows = sum(part[2] for part in sources[0])
    lefts = [array for parts in sources for array, _, _ in parts]
    numbers = iter(range(len(lefts)))
    shapes = tuple(tuple((next(numbers), *part[1:]) for part in parts) for parts in sources)
    n_products = len(kept) + sum(len(ks) for ks in sent)
    outs = [jax.ShapeDtypeStruct((rows, columns), jnp.float32)] * len(kept)
    outs += [
        jax.ShapeDtypeStruct((len(ks) * (rows + SCALE_ROWS), columns), jnp.int16) for ks in sent
    ]
    out = pl.pallas_call(
        functools.partial(
            partial_kernel, tuple(steps), shapes, len(pieces), kept, sent
        ),
        out_shape=outs,
        in_specs=[VMEM] * (len(lefts) + len(pieces))
        + [pl.BlockSpec(memory_space=pl.ANY)] * len(after),
        out_specs=[VMEM] * len(outs),
        compiler_params=PARAMS,
        cost_estimate=cost(
            2 * rows * len(sources) * TILE * columns * n_products,
            2 * len(pieces) * pieces[0].size + 14 * rows * columns,
        ),
    )(*lefts, *pieces, *after)
    return out[: len(kept)], out[len(kept) :]


def pass_on_kernel(kept_ref, received_ref, after_ref, out_ref):
    rows = kept_ref.shape[0]
    total = kept_ref[...] + get_fixed(received_ref, rows + SCALE_ROWS, rows)
    put_fixed(out_ref, 0, total)


def pass_on(kept, received, after):
    rows, columns = kept.shape
    return pl.pallas_call(
        pass_on_kernel,
        out_shape=jax.ShapeDtypeStruct((rows + SCALE_ROWS, columns), jnp.int16),
        in_specs=[VMEM, VMEM, pl.BlockSpec(memory_space=pl.ANY)],
        out_specs=VMEM,
        compiler_params=PARAMS,
        cost_estimate=cost(10 * kept.size, 8 * kept.size),
    )(kept, received, after)


def combine_kernel(n_received, n_before, kept_ref, *refs):
    received, before = refs[:n_received], refs[n_received : n_received + n_before]
    squared_ref, sum_ref = refs[-2:]
    total = kept_ref[...]
    for block in received:
        total += get_fixed(block, 0, total.shape[0])
    squared = total * total
    squared_ref[...] = squared
    column = jnp.sum(squared, axis=0, keepdims=True)
    for ref in before:
        column += ref[...]
    sum_ref[...] = column


def combine(kept, received, before, after):
    return pl.pallas_call(
        functools.partial(combine_kernel, len(received), len(before)),
        out_shape=(
            jax.ShapeDtypeStruct(kept.shape, jnp.float32),
            jax.ShapeDtypeStruct((1, kept.shape[1]), jnp.float32),
        ),
        in_specs=[VMEM] * (1 + len(received) + len(before)) + [pl.BlockSpec(memory_space=pl.ANY)] * len(after),
        out_specs=(VMEM, VMEM),
        compiler_params=PARAMS,
        cost_estimate=cost(8 * kept.size, 14 * kept.size),
    )(kept, *received, *before, *after)


def normalise_kernel(n_chunks, rows_total, column_ref, *refs):
    chunks, out_ref = refs[:n_chunks], refs[n_chunks]
    colmean = column_ref[...] / rows_total
    at = 0
    for chunk in chunks:
        rows = chunk.shape[0]
        out_ref[at : at + rows, :] = (chunk[...] / (colmean + 1e-06)).astype(jnp.bfloat16)
        at += rows


def normalise(column, chunks, rows_total):
    rows, columns = sum(chunk.shape[0] for chunk in chunks), chunks[0].shape[1]
    return pl.pallas_call(
        functools.partial(normalise_kernel, len(chunks), rows_total),
        out_shape=jax.ShapeDtypeStruct((rows, columns), jnp.bfloat16),
        in_specs=[VMEM] * (1 + len(chunks)),
        out_specs=VMEM,
        compiler_params=PARAMS,
        cost_estimate=cost(4 * rows * columns, 6 * rows * columns),
    )(column, *chunks)


def shift(x, axis, by):
    n = lax.axis_size(axis)
    return lax.ppermute(x, axis, [(i, (i + by) % n) for i in range(n)])


def swap(x, bits):
    return lax.ppermute(x, "layer", [(i, i ^ bits) for i in range(4)])


def per_device(left_values, left_pattern, right_values, right_pattern):
    n_rows, n_cols = lax.axis_size("row"), lax.axis_size("col")
    rows_local, _, columns_local = left_values.shape
    sizes = [rows_local * part // sum(SIXTEENTHS) for part in SIXTEENTHS]

    left = left_values.reshape(rows_local, columns_local)
    pattern = left_pattern.reshape(-1)
    reach = n_cols // 2
    away = list(range(1, reach))
    steps = [0] + [-i for i in away] + away + [reach]

    starts = [sum(sizes[:i]) for i in range(len(sizes))]
    own = []
    found = [([], []) for _ in sizes]
    kept, received, last = [], [], []

    def open_slot(slot):
        at, size = (starts[slot], sizes[slot]) if slot < len(sizes) else (0, 0)
        for d in (0, 1):
            riders = [c for c in range(min(slot, len(sizes))) if len(found[c][d]) < reach]
            parts = []
            for c in riders:
                _, first, rows = found[c][d][-1]
                if len(found[c][d]) == reach - 1:
                    first, rows = first + d * (rows // 2), rows // 2
                parts.append((first, rows))
            arrived = found[riders[0]][d][-1][0] if riders else left
            block = load(left, pattern, at, size, arrived, tuple(parts), last)
            last[:] = [block]
            got = shift(block, "col", 1 - 2 * d)
            first = 0
            for c, (_, rows) in zip(riders, parts):
                found[c][d].append((got, first, rows))
                first += rows
            if size:
                found[slot][d].append((got, first, size))
                if d == 0:
                    own.append((block, first, size))

    def sources(i):
        (*below, last_below), (*above, last_above) = found[i]
        return [[part] for part in [own[i]] + below + above] + [[last_below, last_above]]

    def sum_chunk(i):
        if i + 1 < len(sizes):
            ks, sent_ks = (0, second(i)), ((3 - second(i), 3),)
        else:
            ks, sent_ks = (0,), ((1,), (2,), (3,))
        mine, sent = partial_products(steps, sources(i), pieces, last, ks, sent_ks)
        kept.append(mine)
        received.append([swap(x, k[0]) for x, k in zip(sent, sent_ks)])
        last[:] = [mine[0]]

    def second(i):
        return 2 - i % 2

    def send_on(i):
        block = pass_on(kept[i][1], received[i][0], last[0])
        received[i].append(swap(block, second(i)))
        last[:] = [block]

    raw = [(right_pattern, right_values)]
    for i in range(1, n_rows):
        raw.append((shift(right_pattern, "row", i), shift(right_values, "row", i)))
    pieces = []

    squares, columns = [], []

    def square(i):
        squared, column = combine(kept[i][0], received[i], columns[-1:], last)
        squares.append(squared)
        columns.append(column)
        last[:] = [column]

    opened = 0
    for i in range(len(sizes)):
        while opened < min(len(sizes) + reach - 1, i + reach + 1):
            open_slot(opened)
            opened += 1
            if opened == 2:
                for tiles, values in raw:
                    pieces.append(mask_right(tiles, values, last))
                    last[:] = pieces[-1:]
        sum_chunk(i)
        if i > 0:
            send_on(i - 1)
        if 1 < i < len(sizes) - 2:
            square(i - 2)
    for i in range(len(squares), len(sizes)):
        square(i)

    column = lax.psum(columns[-1], "row")
    out = normalise(column, squares, rows_local * n_rows)
    return out.reshape(rows_local, 1, columns_local)


def solution(mesh):
    return jax.shard_map(
        per_device,
        mesh=mesh,
        in_specs=(
            P("row", "layer", "col"),
            P("row", "layer", "col"),
            P(("layer", "row"), None, "col"),
            P(("layer", "row"), None, "col"),
        ),
        out_specs=P("row", "layer", "col"),
        check_vma=False,
    )
```

```python
import functools
import math

import jax
import jax.numpy as jnp
from jax import lax
from jax.experimental import pallas as pl
from jax.experimental.pallas import tpu as pltpu
from jax.sharding import PartitionSpec as P

TILE = 256
SIXTEENTHS = (3, 3, 3, 3, 1, 3)
MINUS = (3, 3, 3, 3, 1, 3)
SCALE_ROWS = 16
CODE = 64.0
TOP = 32767.0
LEAST = 2.0**-100
VMEM = pl.BlockSpec(memory_space=pltpu.VMEM)
PARAMS = pltpu.CompilerParams(vmem_limit_bytes=16 * 1024 * 1024)


def cost(flops, bytes_accessed):
    return pl.CostEstimate(flops=flops, bytes_accessed=bytes_accessed, transcendentals=0)


def load_kernel(at, size, parts, pattern_ref, left_ref, arrived, *refs):
    out = refs[-1]
    done = 0
    for first, rows in parts:
        out[done : done + rows, :] = arrived[first : first + rows, :]
        done += rows
    step = math.gcd(TILE, math.gcd(at, size))
    for i in range(0, size, step):
        entry = pattern_ref[(at + i) // TILE].astype(jnp.float32).astype(out.dtype)
        out[done + i : done + i + step, :] = left_ref[at + i : at + i + step, :] * entry


def load(left, pattern, at, size, arrived, parts, after):
    columns = left.shape[1]
    total = size + sum(rows for _, rows in parts)
    return pl.pallas_call(
        functools.partial(load_kernel, at, size, parts),
        out_shape=jax.ShapeDtypeStruct((total, columns), left.dtype),
        in_specs=[pl.BlockSpec(memory_space=pltpu.SMEM), VMEM]
        + [VMEM if parts else pl.BlockSpec(memory_space=pl.ANY)]
        + [pl.BlockSpec(memory_space=pl.ANY)] * len(after),
        out_specs=VMEM,
        compiler_params=PARAMS,
        cost_estimate=cost(total * columns, 4 * total * columns),
    )(pattern, left, arrived, *after)


def mask_right_kernel(pattern_ref, values_ref, *refs):
    out = refs[-1]
    layers, rows, _ = out.shape
    for i in range(0, rows, TILE):
        block = jnp.swapaxes(values_ref[i : i + TILE].astype(jnp.float32), 0, 1)
        for j in range(layers):
            entry = pattern_ref[i // TILE, j].astype(jnp.float32)
            out[j, i : i + TILE, :] = (block[j] * entry).astype(out.dtype)


def mask_right(pattern, values, after):
    rows, layers, columns = values.shape
    return pl.pallas_call(
        mask_right_kernel,
        out_shape=jax.ShapeDtypeStruct((layers, rows, columns), values.dtype),
        in_specs=[pl.BlockSpec(memory_space=pltpu.SMEM), VMEM]
        + [pl.BlockSpec(memory_space=pl.ANY)] * len(after),
        out_specs=VMEM,
        compiler_params=PARAMS,
        cost_estimate=cost(values.size, 4 * values.size),
    )(pattern.reshape(rows // TILE, layers), values, *after)


def put_fixed(ref, at, total):
    rows, columns = total.shape
    top = jnp.maximum(jnp.max(jnp.abs(total), axis=0, keepdims=True), LEAST)
    code = jnp.ceil(jnp.log2(top) * CODE + 0.01)
    fixed = jnp.round(total * (jnp.exp2(code / -CODE) * TOP)).astype(jnp.int32)
    ref[at : at + rows, :] = fixed.astype(jnp.int16)
    codes = jnp.broadcast_to(code.astype(jnp.int32), (SCALE_ROWS, columns))
    ref[at + rows : at + rows + SCALE_ROWS, :] = codes.astype(jnp.int16)


def get_fixed(ref, at, rows):
    code = ref[at + rows : at + rows + SCALE_ROWS, :].astype(jnp.int32)[:1].astype(jnp.float32)
    unit = jnp.exp2(code / CODE) * (1.0 / TOP)
    return ref[at : at + rows, :].astype(jnp.int32).astype(jnp.float32) * unit


def partial_kernel(steps, sources, n_pieces, kept, sent, *refs):
    layer, row, col = (lax.axis_index(a) for a in ("layer", "row", "col"))
    n_cols = lax.axis_size("col")
    n_lefts = sum(len(parts) for parts in sources)
    pieces = refs[n_lefts : n_lefts + n_pieces]
    rows = sum(part[2] for part in sources[0])
    outs = refs[-len(kept) - len(sent) :]
    _, piece_rows, columns = pieces[0].shape

    def right(step, k):
        inner = lax.rem(col + (step + n_cols), n_cols) * TILE
        piece = lax.rem(row - lax.div(inner, piece_rows) + n_pieces, n_pieces)
        start = pl.multiple_of(lax.rem(inner, piece_rows), TILE)
        tile = pieces[0][layer ^ k, pl.ds(start, TILE), :]
        for i in range(1, n_pieces):
            tile = jnp.where(piece == i, pieces[i][layer ^ k, pl.ds(start, TILE), :], tile)
        return tile

    def product(k):
        total = jnp.zeros((rows, columns), jnp.float32)
        for step, parts in zip(steps, sources):
            tile = right(step, k)
            terms = [
                jnp.dot(
                    refs[i][first : first + count, :], tile, preferred_element_type=jnp.float32
                )
                for i, first, count in parts
            ]
            total += terms[0] if len(terms) == 1 else jnp.concatenate(terms, axis=0)
        return total

    for out, ks in zip(outs[len(kept) :], sent):
        for i, k in enumerate(ks):
            put_fixed(out, i * (rows + SCALE_ROWS), product(k))
    for out, k in zip(outs, kept):
        out[...] = product(k)


def partial_products(steps, sources, pieces, after, kept, sent):
    columns = pieces[0].shape[2]
    rows = sum(part[2] for part in sources[0])
    lefts = [array for parts in sources for array, _, _ in parts]
    numbers = iter(range(len(lefts)))
    shapes = tuple(tuple((next(numbers), *part[1:]) for part in parts) for parts in sources)
    n_products = len(kept) + sum(len(ks) for ks in sent)
    outs = [jax.ShapeDtypeStruct((rows, columns), jnp.float32)] * len(kept)
    outs += [
        jax.ShapeDtypeStruct((len(ks) * (rows + SCALE_ROWS), columns), jnp.int16) for ks in sent
    ]
    out = pl.pallas_call(
        functools.partial(
            partial_kernel, tuple(steps), shapes, len(pieces), kept, sent
        ),
        out_shape=outs,
        in_specs=[VMEM] * (len(lefts) + len(pieces))
        + [pl.BlockSpec(memory_space=pl.ANY)] * len(after),
        out_specs=[VMEM] * len(outs),
        compiler_params=PARAMS,
        cost_estimate=cost(
            2 * rows * len(sources) * TILE * columns * n_products,
            2 * len(pieces) * pieces[0].size + 14 * rows * columns,
        ),
    )(*lefts, *pieces, *after)
    return out[: len(kept)], out[len(kept) :]


def pass_on_kernel(kept_ref, received_ref, after_ref, out_ref):
    rows = kept_ref.shape[0]
    total = kept_ref[...] + get_fixed(received_ref, rows + SCALE_ROWS, rows)
    put_fixed(out_ref, 0, total)


def pass_on(kept, received, after):
    rows, columns = kept.shape
    return pl.pallas_call(
        pass_on_kernel,
        out_shape=jax.ShapeDtypeStruct((rows + SCALE_ROWS, columns), jnp.int16),
        in_specs=[VMEM, VMEM, pl.BlockSpec(memory_space=pl.ANY)],
        out_specs=VMEM,
        compiler_params=PARAMS,
        cost_estimate=cost(10 * kept.size, 8 * kept.size),
    )(kept, received, after)


def combine_kernel(n_received, n_before, kept_ref, *refs):
    received, before = refs[:n_received], refs[n_received : n_received + n_before]
    squared_ref, sum_ref = refs[-2:]
    total = kept_ref[...]
    for block in received:
        total += get_fixed(block, 0, total.shape[0])
    squared = total * total
    squared_ref[...] = squared
    column = jnp.sum(squared, axis=0, keepdims=True)
    for ref in before:
        column += ref[...]
    sum_ref[...] = column


def combine(kept, received, before, after):
    return pl.pallas_call(
        functools.partial(combine_kernel, len(received), len(before)),
        out_shape=(
            jax.ShapeDtypeStruct(kept.shape, jnp.float32),
            jax.ShapeDtypeStruct((1, kept.shape[1]), jnp.float32),
        ),
        in_specs=[VMEM] * (1 + len(received) + len(before)) + [pl.BlockSpec(memory_space=pl.ANY)] * len(after),
        out_specs=(VMEM, VMEM),
        compiler_params=PARAMS,
        cost_estimate=cost(8 * kept.size, 14 * kept.size),
    )(kept, *received, *before, *after)


def normalise_kernel(n_columns, rows_total, *refs):
    columns, chunks, out_ref = refs[:n_columns], refs[n_columns:-1], refs[-1]
    colmean = sum(ref[...] for ref in columns) / rows_total
    at = 0
    for chunk in chunks:
        rows = chunk.shape[0]
        out_ref[at : at + rows, :] = (chunk[...] / (colmean + 1e-06)).astype(jnp.bfloat16)
        at += rows


def normalise(sums, chunks, rows_total):
    rows, columns = sum(chunk.shape[0] for chunk in chunks), chunks[0].shape[1]
    return pl.pallas_call(
        functools.partial(normalise_kernel, len(sums), rows_total),
        out_shape=jax.ShapeDtypeStruct((rows, columns), jnp.bfloat16),
        in_specs=[VMEM] * (len(sums) + len(chunks)),
        out_specs=VMEM,
        compiler_params=PARAMS,
        cost_estimate=cost(4 * rows * columns, 6 * rows * columns),
    )(*sums, *chunks)


def shift(x, axis, by):
    n = lax.axis_size(axis)
    return lax.ppermute(x, axis, [(i, (i + by) % n) for i in range(n)])


def swap(x, bits):
    return lax.ppermute(x, "layer", [(i, i ^ bits) for i in range(4)])


def per_device(left_values, left_pattern, right_values, right_pattern):
    n_rows, n_cols = lax.axis_size("row"), lax.axis_size("col")
    rows_local, _, columns_local = left_values.shape
    unit = rows_local // sum(SIXTEENTHS)
    ends = [[unit * sum(cut[: i + 1]) for i in range(len(cut))] for cut in (SIXTEENTHS, MINUS)]
    spans = [list(zip([0] + end, end)) for end in ends]
    chunks = spans[0]

    left = left_values.reshape(rows_local, columns_local)
    pattern = left_pattern.reshape(-1)
    reach = n_cols // 2
    away = list(range(1, reach))
    steps = [0] + [-i for i in away] + away + [reach]
    halves = [[], []]
    for start, end in chunks:
        middle = (start + end) // 2 if end < rows_local else end
        halves[0].append((start, middle))
        halves[1].append((middle, end))

    own = []
    found = [[[] for _ in range(reach)] for _ in (0, 1)]
    kept, received, last = [], [], []
    moving = [[], []]
    arrived = [left, left]

    def within(spans, start, end):
        cut = [(max(a, start), min(b, end)) for a, b in spans]
        return [(a, b) for a, b in cut if a < b]

    def open_slot(slot):
        for d in (0, 1):
            riders = []
            for step, (start, end), first in moving[d]:
                if step < reach:
                    on = [(start, end)] if step < reach - 1 else within(halves[d], start, end)
                    riders += [(step + 1, span, first + span[0] - start) for span in on]
            new = spans[d][slot] if slot < len(spans[d]) else (0, 0)
            if not riders and new == (0, 0):
                continue
            parts = tuple((first, span[1] - span[0]) for _, span, first in riders)
            block = load(left, pattern, new[0], new[1] - new[0], arrived[d], parts, last)
            last[:] = [block]
            arrived[d] = shift(block, "col", 1 - 2 * d)
            moving[d], first = [], 0
            for step, span, _ in riders + [(1, new, 0)] * (new != (0, 0)):
                moving[d].append((step, span, first))
                found[d][step - 1].append((span, arrived[d], first))
                first += span[1] - span[0]
            if d == 0 and new != (0, 0):
                own.append((new, block, first - (new[1] - new[0])))

    def sources(i):
        held = [own] + [found[d][j - 1] for d in (0, 1) for j in away]
        held += [found[0][reach - 1] + found[1][reach - 1]]
        parts = []
        for entries in held:
            met = [
                (rows, array, first + rows[0] - span[0])
                for span, array, first in entries
                for rows in within([span], *chunks[i])
            ]
            met.sort(key=lambda entry: entry[0])
            parts.append([(array, first, rows[1] - rows[0]) for rows, array, first in met])
        return parts

    def sum_chunk(i):
        if i + 1 < len(chunks):
            ks, sent_ks = (0, second(i)), ((3 - second(i), 3),)
        else:
            ks, sent_ks = (0,), ((1,), (2,), (3,))
        mine, sent = partial_products(steps, sources(i), pieces, last, ks, sent_ks)
        kept.append(mine)
        received.append([swap(x, k[0]) for x, k in zip(sent, sent_ks)])
        last[:] = [mine[0]]

    def second(i):
        return 2 - i % 2

    def send_on(i):
        block = pass_on(kept[i][1], received[i][0], last[0])
        received[i].append(swap(block, second(i)))
        last[:] = [block]

    raw = [(right_pattern, right_values)]
    for i in range(1, n_rows):
        raw.append((shift(right_pattern, "row", i), shift(right_values, "row", i)))
    pieces = []

    squares, columns = [], []

    def square(i):
        squared, column = combine(kept[i][0], received[i], columns[-1:], last)
        squares.append(squared)
        columns.append(column)
        last[:] = [column]

    opened = 0
    for i in range(len(chunks)):
        while opened < min(len(chunks) + reach - 1, i + reach + 1):
            open_slot(opened)
            opened += 1
            if opened == 2:
                for tiles, values in raw:
                    pieces.append(mask_right(tiles, values, last))
                    last[:] = pieces[-1:]
        sum_chunk(i)
        if i > 0:
            send_on(i - 1)
        if 1 < i < len(chunks) - 2:
            square(i - 2)
    for i in range(len(squares), len(chunks)):
        square(i)

    sums = columns[-1:] + [shift(columns[-1], "row", i) for i in range(1, n_rows)]
    out = normalise(sums, squares, rows_local * n_rows)
    return out.reshape(rows_local, 1, columns_local)


def solution(mesh):
    return jax.shard_map(
        per_device,
        mesh=mesh,
        in_specs=(
            P("row", "layer", "col"),
            P("row", "layer", "col"),
            P(("layer", "row"), None, "col"),
            P(("layer", "row"), None, "col"),
        ),
        out_specs=P("row", "layer", "col"),
        check_vma=False,
    )
```

```python
import functools
import math

import jax
import jax.numpy as jnp
from jax import lax
from jax.experimental import pallas as pl
from jax.experimental.pallas import tpu as pltpu
from jax.sharding import PartitionSpec as P

TILE = 256
SIXTEENTHS = (3, 4, 4, 3, 2)
SCALE_ROWS = 16
CODE = 64.0
TOP = 32767.0
LEAST = 2.0**-100
VMEM = pl.BlockSpec(memory_space=pltpu.VMEM)
PARAMS = pltpu.CompilerParams(vmem_limit_bytes=16 * 1024 * 1024)


def cost(flops, bytes_accessed):
    return pl.CostEstimate(flops=flops, bytes_accessed=bytes_accessed, transcendentals=0)


def load_kernel(at, size, parts, pattern_ref, left_ref, arrived, *refs):
    out = refs[-1]
    done = 0
    for first, rows in parts:
        out[done : done + rows, :] = arrived[first : first + rows, :]
        done += rows
    step = math.gcd(TILE, math.gcd(at, size))
    for i in range(0, size, step):
        entry = pattern_ref[(at + i) // TILE].astype(jnp.float32).astype(out.dtype)
        out[done + i : done + i + step, :] = left_ref[at + i : at + i + step, :] * entry


def load(left, pattern, at, size, arrived, parts, after):
    columns = left.shape[1]
    total = size + sum(rows for _, rows in parts)
    return pl.pallas_call(
        functools.partial(load_kernel, at, size, parts),
        out_shape=jax.ShapeDtypeStruct((total, columns), left.dtype),
        in_specs=[pl.BlockSpec(memory_space=pltpu.SMEM), VMEM]
        + [VMEM if parts else pl.BlockSpec(memory_space=pl.ANY)]
        + [pl.BlockSpec(memory_space=pl.ANY)] * len(after),
        out_specs=VMEM,
        compiler_params=PARAMS,
        cost_estimate=cost(total * columns, 4 * total * columns),
    )(pattern, left, arrived, *after)


def mask_right_kernel(pattern_ref, values_ref, *refs):
    out = refs[-1]
    layers, rows, _ = out.shape
    for i in range(0, rows, TILE):
        block = jnp.swapaxes(values_ref[i : i + TILE].astype(jnp.float32), 0, 1)
        for j in range(layers):
            entry = pattern_ref[i // TILE, j].astype(jnp.float32)
            out[j, i : i + TILE, :] = (block[j] * entry).astype(out.dtype)


def mask_right(pattern, values, after):
    rows, layers, columns = values.shape
    return pl.pallas_call(
        mask_right_kernel,
        out_shape=jax.ShapeDtypeStruct((layers, rows, columns), values.dtype),
        in_specs=[pl.BlockSpec(memory_space=pltpu.SMEM), VMEM]
        + [pl.BlockSpec(memory_space=pl.ANY)] * len(after),
        out_specs=VMEM,
        compiler_params=PARAMS,
        cost_estimate=cost(values.size, 4 * values.size),
    )(pattern.reshape(rows // TILE, layers), values, *after)


def put_fixed(ref, at, total):
    rows, columns = total.shape
    top = jnp.maximum(jnp.max(jnp.abs(total), axis=0, keepdims=True), LEAST)
    code = jnp.ceil(jnp.log2(top) * CODE + 0.01)
    fixed = jnp.round(total * (jnp.exp2(code / -CODE) * TOP)).astype(jnp.int32)
    ref[at : at + rows, :] = fixed.astype(jnp.int16)
    codes = jnp.broadcast_to(code.astype(jnp.int32), (SCALE_ROWS, columns))
    ref[at + rows : at + rows + SCALE_ROWS, :] = codes.astype(jnp.int16)


def get_fixed(ref, at, rows):
    code = ref[at + rows : at + rows + SCALE_ROWS, :].astype(jnp.int32)[:1].astype(jnp.float32)
    unit = jnp.exp2(code / CODE) * (1.0 / TOP)
    return ref[at : at + rows, :].astype(jnp.int32).astype(jnp.float32) * unit


def partial_kernel(steps, sources, n_pieces, kept, sent, *refs):
    layer, row, col = (lax.axis_index(a) for a in ("layer", "row", "col"))
    n_cols = lax.axis_size("col")
    n_lefts = sum(len(parts) for parts in sources)
    pieces = refs[n_lefts : n_lefts + n_pieces]
    rows = sum(part[2] for part in sources[0])
    outs = refs[-len(kept) - len(sent) :]
    _, piece_rows, columns = pieces[0].shape

    def right(step, k):
        inner = lax.rem(col + (step + n_cols), n_cols) * TILE
        piece = lax.rem(row - lax.div(inner, piece_rows) + n_pieces, n_pieces)
        start = pl.multiple_of(lax.rem(inner, piece_rows), TILE)
        tile = pieces[0][layer ^ k, pl.ds(start, TILE), :]
        for i in range(1, n_pieces):
            tile = jnp.where(piece == i, pieces[i][layer ^ k, pl.ds(start, TILE), :], tile)
        return tile

    def product(k):
        total = jnp.zeros((rows, columns), jnp.float32)
        for step, parts in zip(steps, sources):
            tile = right(step, k)
            terms = [
                jnp.dot(
                    refs[i][first : first + count, :], tile, preferred_element_type=jnp.float32
                )
                for i, first, count in parts
            ]
            total += terms[0] if len(terms) == 1 else jnp.concatenate(terms, axis=0)
        return total

    for out, ks in zip(outs[len(kept) :], sent):
        for i, k in enumerate(ks):
            put_fixed(out, i * (rows + SCALE_ROWS), product(k))
    for out, k in zip(outs, kept):
        out[...] = product(k)


def partial_products(steps, sources, pieces, after, kept, sent):
    columns = pieces[0].shape[2]
    rows = sum(part[2] for part in sources[0])
    lefts = [array for parts in sources for array, _, _ in parts]
    numbers = iter(range(len(lefts)))
    shapes = tuple(tuple((next(numbers), *part[1:]) for part in parts) for parts in sources)
    n_products = len(kept) + sum(len(ks) for ks in sent)
    outs = [jax.ShapeDtypeStruct((rows, columns), jnp.float32)] * len(kept)
    outs += [
        jax.ShapeDtypeStruct((len(ks) * (rows + SCALE_ROWS), columns), jnp.int16) for ks in sent
    ]
    out = pl.pallas_call(
        functools.partial(
            partial_kernel, tuple(steps), shapes, len(pieces), kept, sent
        ),
        out_shape=outs,
        in_specs=[VMEM] * (len(lefts) + len(pieces))
        + [pl.BlockSpec(memory_space=pl.ANY)] * len(after),
        out_specs=[VMEM] * len(outs),
        compiler_params=PARAMS,
        cost_estimate=cost(
            2 * rows * len(sources) * TILE * columns * n_products,
            2 * len(pieces) * pieces[0].size + 14 * rows * columns,
        ),
    )(*lefts, *pieces, *after)
    return out[: len(kept)], out[len(kept) :]


def pass_on_kernel(kept_ref, received_ref, after_ref, out_ref):
    rows = kept_ref.shape[0]
    total = kept_ref[...] + get_fixed(received_ref, rows + SCALE_ROWS, rows)
    put_fixed(out_ref, 0, total)


def pass_on(kept, received, after):
    rows, columns = kept.shape
    return pl.pallas_call(
        pass_on_kernel,
        out_shape=jax.ShapeDtypeStruct((rows + SCALE_ROWS, columns), jnp.int16),
        in_specs=[VMEM, VMEM, pl.BlockSpec(memory_space=pl.ANY)],
        out_specs=VMEM,
        compiler_params=PARAMS,
        cost_estimate=cost(10 * kept.size, 8 * kept.size),
    )(kept, received, after)


def combine_kernel(n_received, n_before, kept_ref, *refs):
    received, before = refs[:n_received], refs[n_received : n_received + n_before]
    squared_ref, sum_ref = refs[-2:]
    total = kept_ref[...]
    for block in received:
        total += get_fixed(block, 0, total.shape[0])
    squared = total * total
    squared_ref[...] = squared
    column = jnp.sum(squared, axis=0, keepdims=True)
    for ref in before:
        column += ref[...]
    sum_ref[...] = column


def combine(kept, received, before, after):
    return pl.pallas_call(
        functools.partial(combine_kernel, len(received), len(before)),
        out_shape=(
            jax.ShapeDtypeStruct(kept.shape, jnp.float32),
            jax.ShapeDtypeStruct((1, kept.shape[1]), jnp.float32),
        ),
        in_specs=[VMEM] * (1 + len(received) + len(before)) + [pl.BlockSpec(memory_space=pl.ANY)] * len(after),
        out_specs=(VMEM, VMEM),
        compiler_params=PARAMS,
        cost_estimate=cost(8 * kept.size, 14 * kept.size),
    )(kept, *received, *before, *after)


def normalise_kernel(n_sums, rows_total, *refs):
    sums, chunks = refs[:n_sums], refs[n_sums:-3]
    out_ref, block, sems = refs[-3:]
    colmean = sum(ref[...] for ref in sums) / rows_total
    at, copies = 0, []
    for i, chunk in enumerate(chunks):
        rows = pl.ds(at, chunk.shape[0])
        block[rows, :] = (chunk[...] / (colmean + 1e-06)).astype(jnp.bfloat16)
        copies.append(pltpu.make_async_copy(block.at[rows], out_ref.at[rows], sems.at[i]))
        copies[-1].start()
        at += chunk.shape[0]
    for copy in copies:
        copy.wait()


def normalise(sums, chunks, rows_total):
    rows, columns = sum(chunk.shape[0] for chunk in chunks), chunks[0].shape[1]
    return pl.pallas_call(
        functools.partial(normalise_kernel, len(sums), rows_total),
        out_shape=jax.ShapeDtypeStruct((rows, columns), jnp.bfloat16),
        in_specs=[VMEM] * (len(sums) + len(chunks)),
        out_specs=pl.BlockSpec(memory_space=pl.ANY),
        scratch_shapes=[
            pltpu.VMEM((rows, columns), jnp.bfloat16),
            pltpu.SemaphoreType.DMA((len(chunks),)),
        ],
        compiler_params=PARAMS,
        cost_estimate=cost(4 * rows * columns, 6 * rows * columns),
    )(*sums, *chunks)


def shift(x, axis, by):
    n = lax.axis_size(axis)
    return lax.ppermute(x, axis, [(i, (i + by) % n) for i in range(n)])


def swap(x, bits):
    return lax.ppermute(x, "layer", [(i, i ^ bits) for i in range(4)])


def per_device(left_values, left_pattern, right_values, right_pattern):
    n_rows, n_cols = lax.axis_size("row"), lax.axis_size("col")
    rows_local, _, columns_local = left_values.shape
    sizes = [rows_local * part // sum(SIXTEENTHS) for part in SIXTEENTHS]

    left = left_values.reshape(rows_local, columns_local)
    pattern = left_pattern.reshape(-1)
    reach = n_cols // 2
    away = list(range(1, reach))
    steps = [0] + [-i for i in away] + away + [reach]

    starts = [sum(sizes[:i]) for i in range(len(sizes))]
    own = []
    found = [([], []) for _ in sizes]
    kept, received, last = [], [], []

    def open_slot(slot):
        at, size = (starts[slot], sizes[slot]) if slot < len(sizes) else (0, 0)
        for d in (0, 1):
            riders = [c for c in range(min(slot, len(sizes))) if len(found[c][d]) < reach]
            parts = []
            for c in riders:
                _, first, rows = found[c][d][-1]
                if len(found[c][d]) == reach - 1:
                    first, rows = first + d * (rows // 2), rows // 2
                parts.append((first, rows))
            arrived = found[riders[0]][d][-1][0] if riders else left
            if slot or d == 0:
                block = load(left, pattern, at, size, arrived, tuple(parts), last)
            last[:] = [block]
            got = shift(block, "col", 1 - 2 * d)
            first = 0
            for c, (_, rows) in zip(riders, parts):
                found[c][d].append((got, first, rows))
                first += rows
            if size:
                found[slot][d].append((got, first, size))
                if d == 0:
                    own.append((block, first, size))

    def sources(i):
        (*below, last_below), (*above, last_above) = found[i]
        return [[part] for part in [own[i]] + below + above] + [[last_below, last_above]]

    def sum_chunk(i):
        if i + 1 < len(sizes):
            ks, sent_ks = (0, second(i)), ((3 - second(i), 3),)
        else:
            ks, sent_ks = (0,), ((3,), (1,), (2,))
        mine, sent = partial_products(steps, sources(i), pieces, last, ks, sent_ks)
        kept.append(mine)
        received.append([swap(x, k[0]) for x, k in zip(sent, sent_ks)])
        last[:] = [mine[0]]

    def second(i):
        return 2 - i % 2

    def send_on(i):
        block = pass_on(kept[i][1], received[i][0], last[0])
        received[i].append(swap(block, second(i)))
        last[:] = [block]

    raw = [(right_pattern, right_values)]
    for i in range(1, n_rows):
        raw.append((shift(right_pattern, "row", i), shift(right_values, "row", i)))
    pieces = []

    squares, columns = [], []

    def square(i):
        squared, column = combine(kept[i][0], received[i], columns[-1:], last)
        squares.append(squared)
        columns.append(column)
        last[:] = [column]

    opened = 0
    for i in range(len(sizes)):
        while opened < min(len(sizes) + reach - 1, i + reach + 1):
            open_slot(opened)
            opened += 1
            if opened == 2:
                for tiles, values in raw:
                    pieces.append(mask_right(tiles, values, last))
                    last[:] = pieces[-1:]
        sum_chunk(i)
        if i > 0:
            send_on(i - 1)
        if 1 < i < len(sizes) - 2:
            square(i - 2)
    for i in range(len(squares), len(sizes)):
        square(i)

    sums = columns[-1:] + [shift(columns[-1], "row", i) for i in range(1, n_rows)]
    out = normalise(sums, squares, rows_local * n_rows)
    return out.reshape(rows_local, 1, columns_local)


def solution(mesh):
    return jax.shard_map(
        per_device,
        mesh=mesh,
        in_specs=(
            P("row", "layer", "col"),
            P("row", "layer", "col"),
            P(("layer", "row"), None, "col"),
            P(("layer", "row"), None, "col"),
        ),
        out_specs=P("row", "layer", "col"),
        check_vma=False,
    )
```

```python
import functools
import math

import jax
import jax.numpy as jnp
from jax import lax
from jax.experimental import pallas as pl
from jax.experimental.pallas import tpu as pltpu
from jax.sharding import PartitionSpec as P

TILE = 256
PARTS = (7, 8, 8, 6, 3)
SCALE_ROWS = 16
CODE = 64.0
TOP = 32767.0
LEAST = 2.0**-100
VMEM = pl.BlockSpec(memory_space=pltpu.VMEM)
PARAMS = pltpu.CompilerParams(vmem_limit_bytes=16 * 1024 * 1024)


def cost(flops, bytes_accessed):
    return pl.CostEstimate(flops=flops, bytes_accessed=bytes_accessed, transcendentals=0)


def load_kernel(at, size, parts, pattern_ref, left_ref, arrived, *refs):
    out = refs[-1]
    done = 0
    for first, rows in parts:
        out[done : done + rows, :] = arrived[first : first + rows, :]
        done += rows
    step = math.gcd(TILE, math.gcd(at, size))
    for i in range(0, size, step):
        entry = pattern_ref[(at + i) // TILE].astype(jnp.float32).astype(out.dtype)
        out[done + i : done + i + step, :] = left_ref[at + i : at + i + step, :] * entry


def load(left, pattern, at, size, arrived, parts, after):
    columns = left.shape[1]
    total = size + sum(rows for _, rows in parts)
    return pl.pallas_call(
        functools.partial(load_kernel, at, size, parts),
        out_shape=jax.ShapeDtypeStruct((total, columns), left.dtype),
        in_specs=[pl.BlockSpec(memory_space=pltpu.SMEM), VMEM]
        + [VMEM if parts else pl.BlockSpec(memory_space=pl.ANY)]
        + [pl.BlockSpec(memory_space=pl.ANY)] * len(after),
        out_specs=VMEM,
        compiler_params=PARAMS,
        cost_estimate=cost(total * columns, 4 * total * columns),
    )(pattern, left, arrived, *after)


def mask_right_kernel(pattern_ref, values_ref, *refs):
    out = refs[-1]
    layers, rows, _ = out.shape
    for i in range(0, rows, TILE):
        block = jnp.swapaxes(values_ref[i : i + TILE].astype(jnp.float32), 0, 1)
        for j in range(layers):
            entry = pattern_ref[i // TILE, j].astype(jnp.float32)
            out[j, i : i + TILE, :] = (block[j] * entry).astype(out.dtype)


def mask_right(pattern, values, after):
    rows, layers, columns = values.shape
    return pl.pallas_call(
        mask_right_kernel,
        out_shape=jax.ShapeDtypeStruct((layers, rows, columns), values.dtype),
        in_specs=[pl.BlockSpec(memory_space=pltpu.SMEM), VMEM]
        + [pl.BlockSpec(memory_space=pl.ANY)] * len(after),
        out_specs=VMEM,
        compiler_params=PARAMS,
        cost_estimate=cost(values.size, 4 * values.size),
    )(pattern.reshape(rows // TILE, layers), values, *after)


def put_fixed(ref, at, total):
    rows, columns = total.shape
    top = jnp.maximum(jnp.max(jnp.abs(total), axis=0, keepdims=True), LEAST)
    code = jnp.ceil(jnp.log2(top) * CODE + 0.01)
    fixed = jnp.round(total * (jnp.exp2(code / -CODE) * TOP)).astype(jnp.int32)
    ref[at : at + rows, :] = fixed.astype(jnp.int16)
    codes = jnp.broadcast_to(code.astype(jnp.int32), (SCALE_ROWS, columns))
    ref[at + rows : at + rows + SCALE_ROWS, :] = codes.astype(jnp.int16)


def get_fixed(ref, at, rows):
    code = ref[at + rows : at + rows + SCALE_ROWS, :].astype(jnp.int32)[:1].astype(jnp.float32)
    unit = jnp.exp2(code / CODE) * (1.0 / TOP)
    return ref[at : at + rows, :].astype(jnp.int32).astype(jnp.float32) * unit


def partial_kernel(steps, sources, n_pieces, kept, sent, *refs):
    layer, row, col = (lax.axis_index(a) for a in ("layer", "row", "col"))
    n_cols = lax.axis_size("col")
    n_lefts = sum(len(parts) for parts in sources)
    pieces = refs[n_lefts : n_lefts + n_pieces]
    rows = sum(part[2] for part in sources[0])
    outs = refs[-len(kept) - len(sent) :]
    _, piece_rows, columns = pieces[0].shape

    def right(step, k):
        inner = lax.rem(col + (step + n_cols), n_cols) * TILE
        piece = lax.rem(row - lax.div(inner, piece_rows) + n_pieces, n_pieces)
        start = pl.multiple_of(lax.rem(inner, piece_rows), TILE)
        tile = pieces[0][layer ^ k, pl.ds(start, TILE), :]
        for i in range(1, n_pieces):
            tile = jnp.where(piece == i, pieces[i][layer ^ k, pl.ds(start, TILE), :], tile)
        return tile

    def product(k):
        total = jnp.zeros((rows, columns), jnp.float32)
        for step, parts in zip(steps, sources):
            tile = right(step, k)
            terms = [
                jnp.dot(
                    refs[i][first : first + count, :], tile, preferred_element_type=jnp.float32
                )
                for i, first, count in parts
            ]
            total += terms[0] if len(terms) == 1 else jnp.concatenate(terms, axis=0)
        return total

    for out, ks in zip(outs[len(kept) :], sent):
        for i, k in enumerate(ks):
            put_fixed(out, i * (rows + SCALE_ROWS), product(k))
    for out, k in zip(outs, kept):
        out[...] = product(k)


def partial_products(steps, sources, pieces, after, kept, sent):
    columns = pieces[0].shape[2]
    rows = sum(part[2] for part in sources[0])
    lefts = [array for parts in sources for array, _, _ in parts]
    numbers = iter(range(len(lefts)))
    shapes = tuple(tuple((next(numbers), *part[1:]) for part in parts) for parts in sources)
    n_products = len(kept) + sum(len(ks) for ks in sent)
    outs = [jax.ShapeDtypeStruct((rows, columns), jnp.float32)] * len(kept)
    outs += [
        jax.ShapeDtypeStruct((len(ks) * (rows + SCALE_ROWS), columns), jnp.int16) for ks in sent
    ]
    out = pl.pallas_call(
        functools.partial(
            partial_kernel, tuple(steps), shapes, len(pieces), kept, sent
        ),
        out_shape=outs,
        in_specs=[VMEM] * (len(lefts) + len(pieces))
        + [pl.BlockSpec(memory_space=pl.ANY)] * len(after),
        out_specs=[VMEM] * len(outs),
        compiler_params=PARAMS,
        cost_estimate=cost(
            2 * rows * len(sources) * TILE * columns * n_products,
            2 * len(pieces) * pieces[0].size + 14 * rows * columns,
        ),
    )(*lefts, *pieces, *after)
    return out[: len(kept)], out[len(kept) :]


def pass_on_kernel(kept_ref, received_ref, after_ref, out_ref):
    rows = kept_ref.shape[0]
    total = kept_ref[...] + get_fixed(received_ref, rows + SCALE_ROWS, rows)
    put_fixed(out_ref, 0, total)


def pass_on(kept, received, after):
    rows, columns = kept.shape
    return pl.pallas_call(
        pass_on_kernel,
        out_shape=jax.ShapeDtypeStruct((rows + SCALE_ROWS, columns), jnp.int16),
        in_specs=[VMEM, VMEM, pl.BlockSpec(memory_space=pl.ANY)],
        out_specs=VMEM,
        compiler_params=PARAMS,
        cost_estimate=cost(10 * kept.size, 8 * kept.size),
    )(kept, received, after)


def combine_kernel(n_received, n_before, kept_ref, *refs):
    received, before = refs[:n_received], refs[n_received : n_received + n_before]
    squared_ref, sum_ref = refs[-2:]
    total = kept_ref[...]
    for block in received:
        total += get_fixed(block, 0, total.shape[0])
    squared = total * total
    squared_ref[...] = squared
    column = jnp.sum(squared, axis=0, keepdims=True)
    for ref in before:
        column += ref[...]
    sum_ref[...] = column


def combine(kept, received, before, after):
    return pl.pallas_call(
        functools.partial(combine_kernel, len(received), len(before)),
        out_shape=(
            jax.ShapeDtypeStruct(kept.shape, jnp.float32),
            jax.ShapeDtypeStruct((1, kept.shape[1]), jnp.float32),
        ),
        in_specs=[VMEM] * (1 + len(received) + len(before)) + [pl.BlockSpec(memory_space=pl.ANY)] * len(after),
        out_specs=(VMEM, VMEM),
        compiler_params=PARAMS,
        cost_estimate=cost(8 * kept.size, 14 * kept.size),
    )(kept, *received, *before, *after)


def normalise_kernel(n_sums, rows_total, *refs):
    sums, chunks = refs[:n_sums], refs[n_sums:-3]
    out_ref, block, sems = refs[-3:]
    colmean = sum(ref[...] for ref in sums) / rows_total
    scale = 1.0 / (colmean + 1e-06)
    at, copies = 0, []
    for i, chunk in enumerate(chunks):
        rows = pl.ds(at, chunk.shape[0])
        block[rows, :] = (chunk[...] * scale).astype(jnp.bfloat16)
        copies.append(pltpu.make_async_copy(block.at[rows], out_ref.at[rows], sems.at[i]))
        copies[-1].start()
        at += chunk.shape[0]
    for copy in copies:
        copy.wait()


def normalise(sums, chunks, rows_total):
    rows, columns = sum(chunk.shape[0] for chunk in chunks), chunks[0].shape[1]
    return pl.pallas_call(
        functools.partial(normalise_kernel, len(sums), rows_total),
        out_shape=jax.ShapeDtypeStruct((rows, columns), jnp.bfloat16),
        in_specs=[VMEM] * (len(sums) + len(chunks)),
        out_specs=pl.BlockSpec(memory_space=pl.ANY),
        scratch_shapes=[
            pltpu.VMEM((rows, columns), jnp.bfloat16),
            pltpu.SemaphoreType.DMA((len(chunks),)),
        ],
        compiler_params=PARAMS,
        cost_estimate=cost(4 * rows * columns, 6 * rows * columns),
    )(*sums, *chunks)


def shift(x, axis, by):
    n = lax.axis_size(axis)
    return lax.ppermute(x, axis, [(i, (i + by) % n) for i in range(n)])


def swap(x, bits):
    return lax.ppermute(x, "layer", [(i, i ^ bits) for i in range(4)])


def per_device(left_values, left_pattern, right_values, right_pattern):
    n_rows, n_cols = lax.axis_size("row"), lax.axis_size("col")
    rows_local, _, columns_local = left_values.shape
    sizes = [rows_local * part // sum(PARTS) for part in PARTS]

    left = left_values.reshape(rows_local, columns_local)
    pattern = left_pattern.reshape(-1)
    reach = n_cols // 2
    away = list(range(1, reach))
    steps = [0] + [-i for i in away] + away + [reach]

    starts = [sum(sizes[:i]) for i in range(len(sizes))]
    own = []
    found = [([], []) for _ in sizes]
    kept, received, last = [], [], []

    def open_slot(slot):
        at, size = (starts[slot], sizes[slot]) if slot < len(sizes) else (0, 0)
        for d in (0, 1):
            riders = [c for c in range(min(slot, len(sizes))) if len(found[c][d]) < reach]
            parts = []
            for c in riders:
                _, first, rows = found[c][d][-1]
                if len(found[c][d]) == reach - 1:
                    first, rows = first + d * (rows // 2), rows // 2
                parts.append((first, rows))
            arrived = found[riders[0]][d][-1][0] if riders else left
            if slot or d == 0:
                block = load(left, pattern, at, size, arrived, tuple(parts), last)
            last[:] = [block]
            got = shift(block, "col", 1 - 2 * d)
            first = 0
            for c, (_, rows) in zip(riders, parts):
                found[c][d].append((got, first, rows))
                first += rows
            if size:
                found[slot][d].append((got, first, size))
                if d == 0:
                    own.append((block, first, size))

    def sources(i):
        (*below, last_below), (*above, last_above) = found[i]
        return [[part] for part in [own[i]] + below + above] + [[last_below, last_above]]

    def sum_chunk(i):
        if i + 1 < len(sizes):
            ks, sent_ks = (0, second(i)), ((3 - second(i), 3),)
        else:
            ks, sent_ks = (0,), ((3,), (1,), (2,))
        mine, sent = partial_products(steps, sources(i), pieces, last, ks, sent_ks)
        kept.append(mine)
        received.append([swap(x, k[0]) for x, k in zip(sent, sent_ks)])
        last[:] = [mine[0]]

    def second(i):
        return 2 - i % 2

    def send_on(i):
        block = pass_on(kept[i][1], received[i][0], last[0])
        received[i].append(swap(block, second(i)))
        last[:] = [block]

    raw = [(right_pattern, right_values)]
    for i in range(1, n_rows):
        raw.append((shift(right_pattern, "row", i), shift(right_values, "row", i)))
    pieces = []

    squares, columns = [], []

    def square(i):
        squared, column = combine(kept[i][0], received[i], columns[-1:], last)
        squares.append(squared)
        columns.append(column)
        last[:] = [column]

    opened = 0
    for i in range(len(sizes)):
        while opened < min(len(sizes) + reach - 1, i + reach + 1):
            open_slot(opened)
            opened += 1
            if opened == 2:
                for tiles, values in raw:
                    pieces.append(mask_right(tiles, values, last))
                    last[:] = pieces[-1:]
        sum_chunk(i)
        if i > 0:
            send_on(i - 1)
        if 1 < i < len(sizes) - 2:
            square(i - 2)
    for i in range(len(squares), len(sizes)):
        square(i)

    sums = columns[-1:] + [shift(columns[-1], "row", i) for i in range(1, n_rows)]
    out = normalise(sums, squares, rows_local * n_rows)
    return out.reshape(rows_local, 1, columns_local)


def solution(mesh):
    return jax.shard_map(
        per_device,
        mesh=mesh,
        in_specs=(
            P("row", "layer", "col"),
            P("row", "layer", "col"),
            P(("layer", "row"), None, "col"),
            P(("layer", "row"), None, "col"),
        ),
        out_specs=P("row", "layer", "col"),
        check_vma=False,
    )
```

```python
import functools
import math

import jax
import jax.numpy as jnp
from jax import lax
from jax.experimental import pallas as pl
from jax.experimental.pallas import tpu as pltpu
from jax.sharding import PartitionSpec as P

TILE = 256
SIXTEENTHS = (3, 4, 4, 3, 2)
SCALE_ROWS = 16
CODE = 64.0
TOP = 32767.0
LEAST = 2.0**-100
VMEM = pl.BlockSpec(memory_space=pltpu.VMEM)
PARAMS = pltpu.CompilerParams(vmem_limit_bytes=16 * 1024 * 1024)


def cost(flops, bytes_accessed):
    return pl.CostEstimate(flops=flops, bytes_accessed=bytes_accessed, transcendentals=0)


def load_kernel(at, size, parts, pattern_ref, left_ref, arrived, *refs):
    out = refs[-1]
    done = 0
    for first, rows in parts:
        out[done : done + rows, :] = arrived[first : first + rows, :]
        done += rows
    step = math.gcd(TILE, math.gcd(at, size))
    for i in range(0, size, step):
        entry = pattern_ref[(at + i) // TILE].astype(jnp.float32).astype(out.dtype)
        out[done + i : done + i + step, :] = left_ref[at + i : at + i + step, :] * entry


def load(left, pattern, at, size, arrived, parts, after):
    columns = left.shape[1]
    total = size + sum(rows for _, rows in parts)
    return pl.pallas_call(
        functools.partial(load_kernel, at, size, parts),
        out_shape=jax.ShapeDtypeStruct((total, columns), left.dtype),
        in_specs=[pl.BlockSpec(memory_space=pltpu.SMEM), VMEM]
        + [VMEM if parts else pl.BlockSpec(memory_space=pl.ANY)]
        + [pl.BlockSpec(memory_space=pl.ANY)] * len(after),
        out_specs=VMEM,
        compiler_params=PARAMS,
        cost_estimate=cost(total * columns, 4 * total * columns),
    )(pattern, left, arrived, *after)


def mask_right_kernel(pattern_ref, values_ref, *refs):
    out = refs[-1]
    layers, rows, _ = out.shape
    for i in range(0, rows, TILE):
        block = jnp.swapaxes(values_ref[i : i + TILE].astype(jnp.float32), 0, 1)
        for j in range(layers):
            entry = pattern_ref[i // TILE, j].astype(jnp.float32)
            out[j, i : i + TILE, :] = (block[j] * entry).astype(out.dtype)


def mask_right(pattern, values, after):
    rows, layers, columns = values.shape
    return pl.pallas_call(
        mask_right_kernel,
        out_shape=jax.ShapeDtypeStruct((layers, rows, columns), values.dtype),
        in_specs=[pl.BlockSpec(memory_space=pltpu.SMEM), VMEM]
        + [pl.BlockSpec(memory_space=pl.ANY)] * len(after),
        out_specs=VMEM,
        compiler_params=PARAMS,
        cost_estimate=cost(values.size, 4 * values.size),
    )(pattern.reshape(rows // TILE, layers), values, *after)


def put_fixed(ref, at, total):
    rows, columns = total.shape
    top = jnp.maximum(jnp.max(jnp.abs(total), axis=0, keepdims=True), LEAST)
    code = jnp.ceil(jnp.log2(top) * CODE + 0.01)
    fixed = jnp.round(total * (jnp.exp2(code / -CODE) * TOP)).astype(jnp.int32)
    ref[at : at + rows, :] = fixed.astype(jnp.int16)
    codes = jnp.broadcast_to(code.astype(jnp.int32), (SCALE_ROWS, columns))
    ref[at + rows : at + rows + SCALE_ROWS, :] = codes.astype(jnp.int16)


def get_fixed(ref, at, rows):
    code = ref[at + rows : at + rows + SCALE_ROWS, :].astype(jnp.int32)[:1].astype(jnp.float32)
    unit = jnp.exp2(code / CODE) * (1.0 / TOP)
    return ref[at : at + rows, :].astype(jnp.int32).astype(jnp.float32) * unit


def partial_kernel(steps, sources, n_pieces, kept, sent, *refs):
    layer, row, col = (lax.axis_index(a) for a in ("layer", "row", "col"))
    n_cols = lax.axis_size("col")
    n_lefts = sum(len(parts) for parts in sources)
    pieces = refs[n_lefts : n_lefts + n_pieces]
    rows = sum(part[2] for part in sources[0])
    outs = refs[-len(kept) - len(sent) :]
    _, piece_rows, columns = pieces[0].shape

    def right(step, k):
        inner = lax.rem(col + (step + n_cols), n_cols) * TILE
        piece = lax.rem(row - lax.div(inner, piece_rows) + n_pieces, n_pieces)
        start = pl.multiple_of(lax.rem(inner, piece_rows), TILE)
        tile = pieces[0][layer ^ k, pl.ds(start, TILE), :]
        for i in range(1, n_pieces):
            tile = jnp.where(piece == i, pieces[i][layer ^ k, pl.ds(start, TILE), :], tile)
        return tile

    def product(k):
        total = jnp.zeros((rows, columns), jnp.float32)
        for step, parts in zip(steps, sources):
            tile = right(step, k)
            terms = [
                jnp.dot(
                    refs[i][first : first + count, :], tile, preferred_element_type=jnp.float32
                )
                for i, first, count in parts
            ]
            total += terms[0] if len(terms) == 1 else jnp.concatenate(terms, axis=0)
        return total

    for out, ks in zip(outs[len(kept) :], sent):
        for i, k in enumerate(ks):
            put_fixed(out, i * (rows + SCALE_ROWS), product(k))
    for out, k in zip(outs, kept):
        out[...] = product(k)


def partial_products(steps, sources, pieces, after, kept, sent):
    columns = pieces[0].shape[2]
    rows = sum(part[2] for part in sources[0])
    lefts = [array for parts in sources for array, _, _ in parts]
    numbers = iter(range(len(lefts)))
    shapes = tuple(tuple((next(numbers), *part[1:]) for part in parts) for parts in sources)
    n_products = len(kept) + sum(len(ks) for ks in sent)
    outs = [jax.ShapeDtypeStruct((rows, columns), jnp.float32)] * len(kept)
    outs += [
        jax.ShapeDtypeStruct((len(ks) * (rows + SCALE_ROWS), columns), jnp.int16) for ks in sent
    ]
    out = pl.pallas_call(
        functools.partial(
            partial_kernel, tuple(steps), shapes, len(pieces), kept, sent
        ),
        out_shape=outs,
        in_specs=[VMEM] * (len(lefts) + len(pieces))
        + [pl.BlockSpec(memory_space=pl.ANY)] * len(after),
        out_specs=[VMEM] * len(outs),
        compiler_params=PARAMS,
        cost_estimate=cost(
            2 * rows * len(sources) * TILE * columns * n_products,
            2 * len(pieces) * pieces[0].size + 14 * rows * columns,
        ),
    )(*lefts, *pieces, *after)
    return out[: len(kept)], out[len(kept) :]


def pass_on_kernel(kept_ref, received_ref, after_ref, out_ref):
    rows = kept_ref.shape[0]
    total = kept_ref[...] + get_fixed(received_ref, rows + SCALE_ROWS, rows)
    put_fixed(out_ref, 0, total)


def pass_on(kept, received, after):
    rows, columns = kept.shape
    return pl.pallas_call(
        pass_on_kernel,
        out_shape=jax.ShapeDtypeStruct((rows + SCALE_ROWS, columns), jnp.int16),
        in_specs=[VMEM, VMEM, pl.BlockSpec(memory_space=pl.ANY)],
        out_specs=VMEM,
        compiler_params=PARAMS,
        cost_estimate=cost(10 * kept.size, 8 * kept.size),
    )(kept, received, after)


def combine_kernel(n_received, n_before, kept_ref, *refs):
    received, before = refs[:n_received], refs[n_received : n_received + n_before]
    squared_ref, sum_ref = refs[-2:]
    total = kept_ref[...]
    for block in received:
        total += get_fixed(block, 0, total.shape[0])
    squared = total * total
    squared_ref[...] = squared
    column = jnp.sum(squared, axis=0, keepdims=True)
    for ref in before:
        column += ref[...]
    sum_ref[...] = column


def combine(kept, received, before, after):
    return pl.pallas_call(
        functools.partial(combine_kernel, len(received), len(before)),
        out_shape=(
            jax.ShapeDtypeStruct(kept.shape, jnp.float32),
            jax.ShapeDtypeStruct((1, kept.shape[1]), jnp.float32),
        ),
        in_specs=[VMEM] * (1 + len(received) + len(before)) + [pl.BlockSpec(memory_space=pl.ANY)] * len(after),
        out_specs=(VMEM, VMEM),
        compiler_params=PARAMS,
        cost_estimate=cost(8 * kept.size, 14 * kept.size),
    )(kept, *received, *before, *after)


def normalise_kernel(n_sums, rows_total, *refs):
    sums, chunks = refs[:n_sums], refs[n_sums:-3]
    out_ref, block, sems = refs[-3:]
    colmean = sum(ref[...] for ref in sums) / rows_total
    at, copies = 0, []
    for i, chunk in enumerate(chunks):
        rows = pl.ds(at, chunk.shape[0])
        block[rows, :] = (chunk[...] / (colmean + 1e-06)).astype(jnp.bfloat16)
        copies.append(pltpu.make_async_copy(block.at[rows], out_ref.at[rows], sems.at[i]))
        copies[-1].start()
        at += chunk.shape[0]
    for copy in copies:
        copy.wait()


def normalise(sums, chunks, rows_total):
    rows, columns = sum(chunk.shape[0] for chunk in chunks), chunks[0].shape[1]
    return pl.pallas_call(
        functools.partial(normalise_kernel, len(sums), rows_total),
        out_shape=jax.ShapeDtypeStruct((rows, columns), jnp.bfloat16),
        in_specs=[VMEM] * (len(sums) + len(chunks)),
        out_specs=pl.BlockSpec(memory_space=pl.ANY),
        scratch_shapes=[
            pltpu.VMEM((rows, columns), jnp.bfloat16),
            pltpu.SemaphoreType.DMA((len(chunks),)),
        ],
        compiler_params=PARAMS,
        cost_estimate=cost(4 * rows * columns, 6 * rows * columns),
    )(*sums, *chunks)


def shift(x, axis, by):
    n = lax.axis_size(axis)
    return lax.ppermute(x, axis, [(i, (i + by) % n) for i in range(n)])


def swap(x, bits):
    return lax.ppermute(x, "layer", [(i, i ^ bits) for i in range(4)])


def per_device(left_values, left_pattern, right_values, right_pattern):
    n_rows, n_cols = lax.axis_size("row"), lax.axis_size("col")
    rows_local, _, columns_local = left_values.shape
    sizes = [rows_local * part // sum(SIXTEENTHS) for part in SIXTEENTHS]

    left = left_values.reshape(rows_local, columns_local)
    pattern = left_pattern.reshape(-1)
    reach = n_cols // 2
    away = list(range(1, reach))
    steps = [0] + [-i for i in away] + away + [reach]

    starts = [sum(sizes[:i]) for i in range(len(sizes))]
    own = []
    found = [([], []) for _ in sizes]
    kept, received, last = [], [], []

    def is_last(c):
        return c + 1 == len(sizes)

    def open_slot(slot):
        at, size = (starts[slot], sizes[slot]) if slot < len(sizes) else (0, 0)
        for d in (0, 1):
            riders = [
                c for c in range(min(slot, len(sizes))) if len(found[c][d]) < reach - d * is_last(c)
            ]
            if not size and not riders:
                continue
            parts = []
            for c in riders:
                _, first, rows = found[c][d][-1]
                if len(found[c][d]) == reach - 1 and not is_last(c):
                    first, rows = first + d * (rows // 2), rows // 2
                parts.append((first, rows))
            arrived = found[riders[0]][d][-1][0] if riders else left
            if slot or d == 0:
                block = load(left, pattern, at, size, arrived, tuple(parts), last)
            last[:] = [block]
            got = shift(block, "col", 1 - 2 * d)
            first = 0
            for c, (_, rows) in zip(riders, parts):
                found[c][d].append((got, first, rows))
                first += rows
            if size:
                found[slot][d].append((got, first, size))
                if d == 0:
                    own.append((block, first, size))

    def sources(i):
        below, above = (found[i][d][: reach - 1] for d in (0, 1))
        farthest = [part for d in (0, 1) for part in found[i][d][reach - 1 :]]
        return [[part] for part in [own[i]] + below + above] + [farthest]

    def sum_chunk(i):
        if i + 1 < len(sizes):
            ks, sent_ks = (0, second(i)), ((3 - second(i), 3),)
        else:
            ks, sent_ks = (0,), ((3,), (1,), (2,))
        mine, sent = partial_products(steps, sources(i), pieces, last, ks, sent_ks)
        kept.append(mine)
        received.append([swap(x, k[0]) for x, k in zip(sent, sent_ks)])
        last[:] = [mine[0]]

    def second(i):
        return 2 - i % 2

    def send_on(i):
        block = pass_on(kept[i][1], received[i][0], last[0])
        received[i].append(swap(block, second(i)))
        last[:] = [block]

    raw = [(right_pattern, right_values)]
    for i in range(1, n_rows):
        raw.append((shift(right_pattern, "row", i), shift(right_values, "row", i)))
    pieces = []

    squares, columns = [], []

    def square(i):
        squared, column = combine(kept[i][0], received[i], columns[-1:], last)
        squares.append(squared)
        columns.append(column)
        last[:] = [column]

    opened = 0
    for i in range(len(sizes)):
        while opened < min(len(sizes) + reach - 1, i + reach + 1):
            open_slot(opened)
            opened += 1
            if opened == 2:
                for tiles, values in raw:
                    pieces.append(mask_right(tiles, values, last))
                    last[:] = pieces[-1:]
        sum_chunk(i)
        if i > 0:
            send_on(i - 1)
        if 1 < i < len(sizes) - 2:
            square(i - 2)
    for i in range(len(squares), len(sizes)):
        square(i)

    sums = columns[-1:] + [shift(columns[-1], "row", i) for i in range(1, n_rows)]
    out = normalise(sums, squares, rows_local * n_rows)
    return out.reshape(rows_local, 1, columns_local)


def solution(mesh):
    return jax.shard_map(
        per_device,
        mesh=mesh,
        in_specs=(
            P("row", "layer", "col"),
            P("row", "layer", "col"),
            P(("layer", "row"), None, "col"),
            P(("layer", "row"), None, "col"),
        ),
        out_specs=P("row", "layer", "col"),
        check_vma=False,
    )
```

```python
import functools
import math

import jax
import jax.numpy as jnp
from jax import lax
from jax.experimental import pallas as pl
from jax.experimental.pallas import tpu as pltpu
from jax.sharding import PartitionSpec as P

TILE = 256
SIXTEENTHS = (3, 4, 4, 3, 2)
SCALE_ROWS = 16
CODE = 64.0
TOP = 32767.0
LEAST = 2.0**-100
VMEM = pl.BlockSpec(memory_space=pltpu.VMEM)
PARAMS = pltpu.CompilerParams(vmem_limit_bytes=16 * 1024 * 1024)


def cost(flops, bytes_accessed):
    return pl.CostEstimate(flops=flops, bytes_accessed=bytes_accessed, transcendentals=0)


def load_kernel(at, size, parts, pattern_ref, left_ref, arrived, *refs):
    out = refs[-1]
    done = 0
    for first, rows in parts:
        out[done : done + rows, :] = arrived[first : first + rows, :]
        done += rows
    step = math.gcd(TILE, math.gcd(at, size))
    for i in range(0, size, step):
        entry = pattern_ref[(at + i) // TILE].astype(jnp.float32).astype(out.dtype)
        out[done + i : done + i + step, :] = left_ref[at + i : at + i + step, :] * entry


def load(left, pattern, at, size, arrived, parts, after):
    columns = left.shape[1]
    total = size + sum(rows for _, rows in parts)
    return pl.pallas_call(
        functools.partial(load_kernel, at, size, parts),
        out_shape=jax.ShapeDtypeStruct((total, columns), left.dtype),
        in_specs=[pl.BlockSpec(memory_space=pltpu.SMEM), VMEM]
        + [VMEM if parts else pl.BlockSpec(memory_space=pl.ANY)]
        + [pl.BlockSpec(memory_space=pl.ANY)] * len(after),
        out_specs=VMEM,
        compiler_params=PARAMS,
        cost_estimate=cost(total * columns, 4 * total * columns),
    )(pattern, left, arrived, *after)


def mask_right_kernel(pattern_ref, values_ref, *refs):
    out = refs[-1]
    layers, rows, _ = out.shape
    for i in range(0, rows, TILE):
        block = jnp.swapaxes(values_ref[i : i + TILE].astype(jnp.float32), 0, 1)
        for j in range(layers):
            entry = pattern_ref[i // TILE, j].astype(jnp.float32)
            out[j, i : i + TILE, :] = (block[j] * entry).astype(out.dtype)


def mask_right(pattern, values, after):
    rows, layers, columns = values.shape
    return pl.pallas_call(
        mask_right_kernel,
        out_shape=jax.ShapeDtypeStruct((layers, rows, columns), values.dtype),
        in_specs=[pl.BlockSpec(memory_space=pltpu.SMEM), VMEM]
        + [pl.BlockSpec(memory_space=pl.ANY)] * len(after),
        out_specs=VMEM,
        compiler_params=PARAMS,
        cost_estimate=cost(values.size, 4 * values.size),
    )(pattern.reshape(rows // TILE, layers), values, *after)


def put_fixed(ref, at, total):
    rows, columns = total.shape
    top = jnp.maximum(jnp.max(jnp.abs(total), axis=0, keepdims=True), LEAST)
    code = jnp.ceil(jnp.log2(top) * CODE + 0.01)
    fixed = jnp.round(total * (jnp.exp2(code / -CODE) * TOP)).astype(jnp.int32)
    ref[at : at + rows, :] = fixed.astype(jnp.int16)
    codes = jnp.broadcast_to(code.astype(jnp.int32), (SCALE_ROWS, columns))
    ref[at + rows : at + rows + SCALE_ROWS, :] = codes.astype(jnp.int16)


def get_fixed(ref, at, rows):
    code = ref[at + rows : at + rows + SCALE_ROWS, :].astype(jnp.int32)[:1].astype(jnp.float32)
    unit = jnp.exp2(code / CODE) * (1.0 / TOP)
    return ref[at : at + rows, :].astype(jnp.int32).astype(jnp.float32) * unit


def partial_kernel(steps, sources, n_pieces, kept, sent, *refs):
    layer, row, col = (lax.axis_index(a) for a in ("layer", "row", "col"))
    n_cols = lax.axis_size("col")
    n_lefts = sum(len(parts) for parts in sources)
    pieces = refs[n_lefts : n_lefts + n_pieces]
    rows = sum(part[2] for part in sources[0])
    outs = refs[-len(kept) - len(sent) :]
    _, piece_rows, columns = pieces[0].shape

    def right(step, k):
        up = jnp.where(lax.rem(row, 2) == 0, step, -step)
        inner = lax.rem(col + up + n_cols, n_cols) * TILE
        piece = lax.rem(row - lax.div(inner, piece_rows) + n_pieces, n_pieces)
        start = pl.multiple_of(lax.rem(inner, piece_rows), TILE)
        tile = pieces[0][layer ^ k, pl.ds(start, TILE), :]
        for i in range(1, n_pieces):
            tile = jnp.where(piece == i, pieces[i][layer ^ k, pl.ds(start, TILE), :], tile)
        return tile

    def product(k):
        total = jnp.zeros((rows, columns), jnp.float32)
        for step, parts in zip(steps, sources):
            tile = right(step, k)
            terms = [
                jnp.dot(
                    refs[i][first : first + count, :], tile, preferred_element_type=jnp.float32
                )
                for i, first, count in parts
            ]
            total += terms[0] if len(terms) == 1 else jnp.concatenate(terms, axis=0)
        return total

    for out, ks in zip(outs[len(kept) :], sent):
        for i, k in enumerate(ks):
            put_fixed(out, i * (rows + SCALE_ROWS), product(k))
    for out, k in zip(outs, kept):
        out[...] = product(k)


def partial_products(steps, sources, pieces, after, kept, sent):
    columns = pieces[0].shape[2]
    rows = sum(part[2] for part in sources[0])
    lefts = [array for parts in sources for array, _, _ in parts]
    numbers = iter(range(len(lefts)))
    shapes = tuple(tuple((next(numbers), *part[1:]) for part in parts) for parts in sources)
    n_products = len(kept) + sum(len(ks) for ks in sent)
    outs = [jax.ShapeDtypeStruct((rows, columns), jnp.float32)] * len(kept)
    outs += [
        jax.ShapeDtypeStruct((len(ks) * (rows + SCALE_ROWS), columns), jnp.int16) for ks in sent
    ]
    out = pl.pallas_call(
        functools.partial(
            partial_kernel, tuple(steps), shapes, len(pieces), kept, sent
        ),
        out_shape=outs,
        in_specs=[VMEM] * (len(lefts) + len(pieces))
        + [pl.BlockSpec(memory_space=pl.ANY)] * len(after),
        out_specs=[VMEM] * len(outs),
        compiler_params=PARAMS,
        cost_estimate=cost(
            2 * rows * len(sources) * TILE * columns * n_products,
            2 * len(pieces) * pieces[0].size + 14 * rows * columns,
        ),
    )(*lefts, *pieces, *after)
    return out[: len(kept)], out[len(kept) :]


def pass_on_kernel(kept_ref, received_ref, after_ref, out_ref):
    rows = kept_ref.shape[0]
    total = kept_ref[...] + get_fixed(received_ref, rows + SCALE_ROWS, rows)
    put_fixed(out_ref, 0, total)


def pass_on(kept, received, after):
    rows, columns = kept.shape
    return pl.pallas_call(
        pass_on_kernel,
        out_shape=jax.ShapeDtypeStruct((rows + SCALE_ROWS, columns), jnp.int16),
        in_specs=[VMEM, VMEM, pl.BlockSpec(memory_space=pl.ANY)],
        out_specs=VMEM,
        compiler_params=PARAMS,
        cost_estimate=cost(10 * kept.size, 8 * kept.size),
    )(kept, received, after)


def combine_kernel(n_received, n_before, kept_ref, *refs):
    received, before = refs[:n_received], refs[n_received : n_received + n_before]
    squared_ref, sum_ref = refs[-2:]
    total = kept_ref[...]
    for block in received:
        total += get_fixed(block, 0, total.shape[0])
    squared = total * total
    squared_ref[...] = squared
    column = jnp.sum(squared, axis=0, keepdims=True)
    for ref in before:
        column += ref[...]
    sum_ref[...] = column


def combine(kept, received, before, after):
    return pl.pallas_call(
        functools.partial(combine_kernel, len(received), len(before)),
        out_shape=(
            jax.ShapeDtypeStruct(kept.shape, jnp.float32),
            jax.ShapeDtypeStruct((1, kept.shape[1]), jnp.float32),
        ),
        in_specs=[VMEM] * (1 + len(received) + len(before)) + [pl.BlockSpec(memory_space=pl.ANY)] * len(after),
        out_specs=(VMEM, VMEM),
        compiler_params=PARAMS,
        cost_estimate=cost(8 * kept.size, 14 * kept.size),
    )(kept, *received, *before, *after)


def normalise_kernel(n_sums, rows_total, *refs):
    sums, chunks = refs[:n_sums], refs[n_sums:-3]
    out_ref, block, sems = refs[-3:]
    colmean = sum(ref[...] for ref in sums) / rows_total
    at, copies = 0, []
    for i, chunk in enumerate(chunks):
        rows = pl.ds(at, chunk.shape[0])
        block[rows, :] = (chunk[...] / (colmean + 1e-06)).astype(jnp.bfloat16)
        copies.append(pltpu.make_async_copy(block.at[rows], out_ref.at[rows], sems.at[i]))
        copies[-1].start()
        at += chunk.shape[0]
    for copy in copies:
        copy.wait()


def normalise(sums, chunks, rows_total):
    rows, columns = sum(chunk.shape[0] for chunk in chunks), chunks[0].shape[1]
    return pl.pallas_call(
        functools.partial(normalise_kernel, len(sums), rows_total),
        out_shape=jax.ShapeDtypeStruct((rows, columns), jnp.bfloat16),
        in_specs=[VMEM] * (len(sums) + len(chunks)),
        out_specs=pl.BlockSpec(memory_space=pl.ANY),
        scratch_shapes=[
            pltpu.VMEM((rows, columns), jnp.bfloat16),
            pltpu.SemaphoreType.DMA((len(chunks),)),
        ],
        compiler_params=PARAMS,
        cost_estimate=cost(4 * rows * columns, 6 * rows * columns),
    )(*sums, *chunks)


def shift(x, axis, by):
    n = lax.axis_size(axis)
    return lax.ppermute(x, axis, [(i, (i + by) % n) for i in range(n)])


def turn(x, by):
    n_rows, n_cols = lax.axis_size("row"), lax.axis_size("col")
    pairs = [
        (r * n_cols + c, r * n_cols + (c + by * (1 - 2 * (r % 2))) % n_cols)
        for r in range(n_rows)
        for c in range(n_cols)
    ]
    return lax.ppermute(x, ("row", "col"), pairs)


def swap(x, bits):
    return lax.ppermute(x, "layer", [(i, i ^ bits) for i in range(4)])


def per_device(left_values, left_pattern, right_values, right_pattern):
    n_rows, n_cols = lax.axis_size("row"), lax.axis_size("col")
    rows_local, _, columns_local = left_values.shape
    sizes = [rows_local * part // sum(SIXTEENTHS) for part in SIXTEENTHS]

    left = left_values.reshape(rows_local, columns_local)
    pattern = left_pattern.reshape(-1)
    reach = n_cols // 2
    away = list(range(1, reach))
    steps = [0] + [-i for i in away] + away + [reach]

    starts = [sum(sizes[:i]) for i in range(len(sizes))]
    own = []
    found = [([], []) for _ in sizes]
    kept, received, last = [], [], []

    def open_slot(slot):
        at, size = (starts[slot], sizes[slot]) if slot < len(sizes) else (0, 0)
        for d in (0, 1):
            riders = [c for c in range(min(slot, len(sizes))) if len(found[c][d]) < reach]
            parts = []
            for c in riders:
                _, first, rows = found[c][d][-1]
                if len(found[c][d]) == reach - 1:
                    first, rows = first + d * (rows // 2), rows // 2
                parts.append((first, rows))
            arrived = found[riders[0]][d][-1][0] if riders else left
            if slot or d == 0:
                block = load(left, pattern, at, size, arrived, tuple(parts), last)
            last[:] = [block]
            got = turn(block, 1 - 2 * d)
            first = 0
            for c, (_, rows) in zip(riders, parts):
                found[c][d].append((got, first, rows))
                first += rows
            if size:
                found[slot][d].append((got, first, size))
                if d == 0:
                    own.append((block, first, size))

    def sources(i):
        (*below, last_below), (*above, last_above) = found[i]
        return [[part] for part in [own[i]] + below + above] + [[last_below, last_above]]

    def sum_chunk(i):
        if i + 1 < len(sizes):
            ks, sent_ks = (0, second(i)), ((3 - second(i), 3),)
        else:
            ks, sent_ks = (0,), ((3,), (1,), (2,))
        mine, sent = partial_products(steps, sources(i), pieces, last, ks, sent_ks)
        kept.append(mine)
        received.append([swap(x, k[0]) for x, k in zip(sent, sent_ks)])
        last[:] = [mine[0]]

    def second(i):
        return 2 - i % 2

    def send_on(i):
        block = pass_on(kept[i][1], received[i][0], last[0])
        received[i].append(swap(block, second(i)))
        last[:] = [block]

    raw = [(right_pattern, right_values)]
    for i in range(1, n_rows):
        raw.append((shift(right_pattern, "row", i), shift(right_values, "row", i)))
    pieces = []

    squares, columns = [], []

    def square(i):
        squared, column = combine(kept[i][0], received[i], columns[-1:], last)
        squares.append(squared)
        columns.append(column)
        last[:] = [column]

    opened = 0
    for i in range(len(sizes)):
        while opened < min(len(sizes) + reach - 1, i + reach + 1):
            open_slot(opened)
            opened += 1
            if opened == 2:
                for tiles, values in raw:
                    pieces.append(mask_right(tiles, values, last))
                    last[:] = pieces[-1:]
        sum_chunk(i)
        if i > 0:
            send_on(i - 1)
        if 1 < i < len(sizes) - 2:
            square(i - 2)
    for i in range(len(squares), len(sizes)):
        square(i)

    sums = columns[-1:] + [shift(columns[-1], "row", i) for i in range(1, n_rows)]
    out = normalise(sums, squares, rows_local * n_rows)
    return out.reshape(rows_local, 1, columns_local)


def solution(mesh):
    return jax.shard_map(
        per_device,
        mesh=mesh,
        in_specs=(
            P("row", "layer", "col"),
            P("row", "layer", "col"),
            P(("layer", "row"), None, "col"),
            P(("layer", "row"), None, "col"),
        ),
        out_specs=P("row", "layer", "col"),
        check_vma=False,
    )
```

```python
import functools
import math

import jax
import jax.numpy as jnp
from jax import lax
from jax.experimental import pallas as pl
from jax.experimental.pallas import tpu as pltpu
from jax.sharding import PartitionSpec as P

TILE = 256
SIXTEENTHS = (3, 4, 4, 3, 2)
SCALE_ROWS = 16
CODE = 64.0
TOP = 32767.0
LEAST = 2.0**-100
VMEM = pl.BlockSpec(memory_space=pltpu.VMEM)
PARAMS = pltpu.CompilerParams(vmem_limit_bytes=16 * 1024 * 1024)


def cost(flops, bytes_accessed):
    return pl.CostEstimate(flops=flops, bytes_accessed=bytes_accessed, transcendentals=0)


def load_kernel(at, size, parts, pattern_ref, left_ref, arrived, *refs):
    out = refs[-1]
    done = 0
    for first, rows in parts:
        out[done : done + rows, :] = arrived[first : first + rows, :]
        done += rows
    step = math.gcd(TILE, math.gcd(at, size))
    for i in range(0, size, step):
        entry = pattern_ref[(at + i) // TILE].astype(jnp.float32).astype(out.dtype)
        out[done + i : done + i + step, :] = left_ref[at + i : at + i + step, :] * entry


def load(left, pattern, at, size, arrived, parts, after):
    columns = left.shape[1]
    total = size + sum(rows for _, rows in parts)
    return pl.pallas_call(
        functools.partial(load_kernel, at, size, parts),
        out_shape=jax.ShapeDtypeStruct((total, columns), left.dtype),
        in_specs=[pl.BlockSpec(memory_space=pltpu.SMEM), VMEM]
        + [VMEM if parts else pl.BlockSpec(memory_space=pl.ANY)]
        + [pl.BlockSpec(memory_space=pl.ANY)] * len(after),
        out_specs=VMEM,
        compiler_params=PARAMS,
        cost_estimate=cost(total * columns, 4 * total * columns),
    )(pattern, left, arrived, *after)


def mask_right_kernel(pattern_ref, values_ref, *refs):
    out = refs[-1]
    layers, rows, _ = out.shape
    for i in range(0, rows, TILE):
        block = jnp.swapaxes(values_ref[i : i + TILE].astype(jnp.float32), 0, 1)
        for j in range(layers):
            entry = pattern_ref[i // TILE, j].astype(jnp.float32)
            out[j, i : i + TILE, :] = (block[j] * entry).astype(out.dtype)


def mask_right(pattern, values, after):
    rows, layers, columns = values.shape
    return pl.pallas_call(
        mask_right_kernel,
        out_shape=jax.ShapeDtypeStruct((layers, rows, columns), values.dtype),
        in_specs=[pl.BlockSpec(memory_space=pltpu.SMEM), VMEM]
        + [pl.BlockSpec(memory_space=pl.ANY)] * len(after),
        out_specs=VMEM,
        compiler_params=PARAMS,
        cost_estimate=cost(values.size, 4 * values.size),
    )(pattern.reshape(rows // TILE, layers), values, *after)


def put_fixed(ref, at, total):
    rows, columns = total.shape
    top = jnp.maximum(jnp.max(jnp.abs(total), axis=0, keepdims=True), LEAST)
    code = jnp.ceil(jnp.log2(top) * CODE + 0.01)
    fixed = jnp.round(total * (jnp.exp2(code / -CODE) * TOP)).astype(jnp.int32)
    ref[at : at + rows, :] = fixed.astype(jnp.int16)
    codes = jnp.broadcast_to(code.astype(jnp.int32), (SCALE_ROWS, columns))
    ref[at + rows : at + rows + SCALE_ROWS, :] = codes.astype(jnp.int16)


def get_fixed(ref, at, rows):
    code = ref[at + rows : at + rows + SCALE_ROWS, :].astype(jnp.int32)[:1].astype(jnp.float32)
    unit = jnp.exp2(code / CODE) * (1.0 / TOP)
    return ref[at : at + rows, :].astype(jnp.int32).astype(jnp.float32) * unit


def partial_kernel(steps, sources, n_pieces, kept, sent, *refs):
    layer, row, col = (lax.axis_index(a) for a in ("layer", "row", "col"))
    n_cols = lax.axis_size("col")
    n_lefts = sum(len(parts) for parts in sources)
    pieces = refs[n_lefts : n_lefts + n_pieces]
    rows = sum(part[2] for part in sources[0])
    outs = refs[-len(kept) - len(sent) :]
    _, piece_rows, columns = pieces[0].shape

    def right(step, k):
        inner = lax.rem(col + (step + n_cols), n_cols) * TILE
        piece = lax.rem(row - lax.div(inner, piece_rows) + n_pieces, n_pieces)
        start = pl.multiple_of(lax.rem(inner, piece_rows), TILE)
        tile = pieces[0][layer ^ k, pl.ds(start, TILE), :]
        for i in range(1, n_pieces):
            tile = jnp.where(piece == i, pieces[i][layer ^ k, pl.ds(start, TILE), :], tile)
        return tile

    def product(k):
        total = jnp.zeros((rows, columns), jnp.float32)
        for step, parts in zip(steps, sources):
            tile = right(step, k)
            terms = [
                jnp.dot(
                    refs[i][first : first + count, :], tile, preferred_element_type=jnp.float32
                )
                for i, first, count in parts
            ]
            total += terms[0] if len(terms) == 1 else jnp.concatenate(terms, axis=0)
        return total

    for out, ks in zip(outs[len(kept) :], sent):
        for i, k in enumerate(ks):
            put_fixed(out, i * (rows + SCALE_ROWS), product(k))
    for out, k in zip(outs, kept):
        out[...] = product(k)


def partial_products(steps, sources, pieces, after, kept, sent):
    columns = pieces[0].shape[2]
    rows = sum(part[2] for part in sources[0])
    lefts = [array for parts in sources for array, _, _ in parts]
    numbers = iter(range(len(lefts)))
    shapes = tuple(tuple((next(numbers), *part[1:]) for part in parts) for parts in sources)
    n_products = len(kept) + sum(len(ks) for ks in sent)
    outs = [jax.ShapeDtypeStruct((rows, columns), jnp.float32)] * len(kept)
    outs += [
        jax.ShapeDtypeStruct((len(ks) * (rows + SCALE_ROWS), columns), jnp.int16) for ks in sent
    ]
    out = pl.pallas_call(
        functools.partial(
            partial_kernel, tuple(steps), shapes, len(pieces), kept, sent
        ),
        out_shape=outs,
        in_specs=[VMEM] * (len(lefts) + len(pieces))
        + [pl.BlockSpec(memory_space=pl.ANY)] * len(after),
        out_specs=[VMEM] * len(outs),
        compiler_params=PARAMS,
        cost_estimate=cost(
            2 * rows * len(sources) * TILE * columns * n_products,
            2 * len(pieces) * pieces[0].size + 14 * rows * columns,
        ),
    )(*lefts, *pieces, *after)
    return out[: len(kept)], out[len(kept) :]


def pass_on_kernel(kept_ref, received_ref, after_ref, out_ref):
    rows = kept_ref.shape[0]
    total = kept_ref[...] + get_fixed(received_ref, rows + SCALE_ROWS, rows)
    put_fixed(out_ref, 0, total)


def pass_on(kept, received, after):
    rows, columns = kept.shape
    return pl.pallas_call(
        pass_on_kernel,
        out_shape=jax.ShapeDtypeStruct((rows + SCALE_ROWS, columns), jnp.int16),
        in_specs=[VMEM, VMEM, pl.BlockSpec(memory_space=pl.ANY)],
        out_specs=VMEM,
        compiler_params=PARAMS,
        cost_estimate=cost(10 * kept.size, 8 * kept.size),
    )(kept, received, after)


def combine_kernel(n_received, n_before, kept_ref, *refs):
    received, before = refs[:n_received], refs[n_received : n_received + n_before]
    squared_ref, sum_ref = refs[-2:]
    total = kept_ref[...]
    for block in received:
        total += get_fixed(block, 0, total.shape[0])
    squared = total * total
    squared_ref[...] = squared
    column = jnp.sum(squared, axis=0, keepdims=True)
    for ref in before:
        column += ref[...]
    sum_ref[...] = column


def combine(kept, received, before, after):
    return pl.pallas_call(
        functools.partial(combine_kernel, len(received), len(before)),
        out_shape=(
            jax.ShapeDtypeStruct(kept.shape, jnp.float32),
            jax.ShapeDtypeStruct((1, kept.shape[1]), jnp.float32),
        ),
        in_specs=[VMEM] * (1 + len(received) + len(before)) + [pl.BlockSpec(memory_space=pl.ANY)] * len(after),
        out_specs=(VMEM, VMEM),
        compiler_params=PARAMS,
        cost_estimate=cost(8 * kept.size, 14 * kept.size),
    )(kept, *received, *before, *after)


def normalise_kernel(n_sums, rows_total, *refs):
    sums, chunks = refs[:n_sums], refs[n_sums:-3]
    out_ref, block, sems = refs[-3:]
    colmean = sum(ref[...] for ref in sums) / rows_total
    at, copies = 0, []
    for i, chunk in enumerate(chunks):
        rows = pl.ds(at, chunk.shape[0])
        block[rows, :] = (chunk[...] / (colmean + 1e-06)).astype(jnp.bfloat16)
        copies.append(pltpu.make_async_copy(block.at[rows], out_ref.at[rows], sems.at[i]))
        copies[-1].start()
        at += chunk.shape[0]
    for copy in copies:
        copy.wait()


def normalise(sums, chunks, rows_total):
    rows, columns = sum(chunk.shape[0] for chunk in chunks), chunks[0].shape[1]
    return pl.pallas_call(
        functools.partial(normalise_kernel, len(sums), rows_total),
        out_shape=jax.ShapeDtypeStruct((rows, columns), jnp.bfloat16),
        in_specs=[VMEM] * (len(sums) + len(chunks)),
        out_specs=pl.BlockSpec(memory_space=pl.ANY),
        scratch_shapes=[
            pltpu.VMEM((rows, columns), jnp.bfloat16),
            pltpu.SemaphoreType.DMA((len(chunks),)),
        ],
        compiler_params=PARAMS,
        cost_estimate=cost(4 * rows * columns, 6 * rows * columns),
    )(*sums, *chunks)


def shift(x, axis, by):
    n = lax.axis_size(axis)
    return lax.ppermute(x, axis, [(i, (i + by) % n) for i in range(n)])


def swap(x, bits):
    return lax.ppermute(x, "layer", [(i, i ^ bits) for i in range(4)])


def per_device(left_values, left_pattern, right_values, right_pattern):
    n_rows, n_cols = lax.axis_size("row"), lax.axis_size("col")
    rows_local, _, columns_local = left_values.shape
    sizes = [rows_local * part // sum(SIXTEENTHS) for part in SIXTEENTHS]

    left = left_values.reshape(rows_local, columns_local)
    pattern = left_pattern.reshape(-1)
    reach = n_cols // 2
    away = list(range(1, reach))
    steps = [0] + [-i for i in away] + away + [reach]

    starts = [sum(sizes[:i]) for i in range(len(sizes))]
    own = []
    found = [([], []) for _ in sizes]
    kept, received, last = [], [], []

    def open_slot(slot):
        at, size = (starts[slot], sizes[slot]) if slot < len(sizes) else (0, 0)
        for d in (0, 1):
            riders = [c for c in range(min(slot, len(sizes))) if len(found[c][d]) < reach]
            parts = []
            for c in riders:
                _, first, rows = found[c][d][-1]
                if len(found[c][d]) == reach - 1:
                    first, rows = first + d * (rows // 2), rows // 2
                parts.append((first, rows))
            arrived = found[riders[0]][d][-1][0] if riders else left
            if slot or d == 0:
                block = load(left, pattern, at, size, arrived, tuple(parts), last)
            last[:] = [block]
            got = shift(block, "col", 1 - 2 * d)
            first = 0
            for c, (_, rows) in zip(riders, parts):
                found[c][d].append((got, first, rows))
                first += rows
            if size:
                found[slot][d].append((got, first, size))
                if d == 0:
                    own.append((block, first, size))

    def sources(i):
        (*below, last_below), (*above, last_above) = found[i]
        return [[part] for part in [own[i]] + below + above] + [[last_below, last_above]]

    def direct(i):
        return i in (0, len(sizes) - 1)

    def sum_chunk(i):
        if not direct(i):
            ks, sent_ks = (0, second(i)), ((3 - second(i), 3),)
        else:
            ks, sent_ks = (0,), ((3,), (1,), (2,))
        mine, sent = partial_products(steps, sources(i), pieces, last, ks, sent_ks)
        kept.append(mine)
        received.append([swap(x, k[0]) for x, k in zip(sent, sent_ks)])
        last[:] = [mine[0]]

    def second(i):
        return 2 - i % 2

    def send_on(i):
        block = pass_on(kept[i][1], received[i][0], last[0])
        received[i].append(swap(block, second(i)))
        last[:] = [block]

    raw = [(right_pattern, right_values)]
    for i in range(1, n_rows):
        raw.append((shift(right_pattern, "row", i), shift(right_values, "row", i)))
    pieces = []

    squares, columns = [], []

    def square(i):
        squared, column = combine(kept[i][0], received[i], columns[-1:], last)
        squares.append(squared)
        columns.append(column)
        last[:] = [column]

    opened = 0
    for i in range(len(sizes)):
        while opened < min(len(sizes) + reach - 1, i + reach + 1):
            open_slot(opened)
            opened += 1
            if opened == 2:
                for tiles, values in raw:
                    pieces.append(mask_right(tiles, values, last))
                    last[:] = pieces[-1:]
        if i == 1:
            square(0)
        sum_chunk(i)
        if i > 0 and not direct(i - 1):
            send_on(i - 1)
    for i in range(len(squares), len(sizes)):
        square(i)

    sums = columns[-1:] + [shift(columns[-1], "row", i) for i in range(1, n_rows)]
    out = normalise(sums, squares, rows_local * n_rows)
    return out.reshape(rows_local, 1, columns_local)


def solution(mesh):
    return jax.shard_map(
        per_device,
        mesh=mesh,
        in_specs=(
            P("row", "layer", "col"),
            P("row", "layer", "col"),
            P(("layer", "row"), None, "col"),
            P(("layer", "row"), None, "col"),
        ),
        out_specs=P("row", "layer", "col"),
        check_vma=False,
    )
```

```python
import functools
import math

import jax
import jax.numpy as jnp
from jax import lax
from jax.experimental import pallas as pl
from jax.experimental.pallas import tpu as pltpu
from jax.sharding import PartitionSpec as P

TILE = 256
SIXTEENTHS = (3, 4, 4, 3, 2)
SCALE_ROWS = 16
CODE = 64.0
TOP = 32767.0
LEAST = 2.0**-100
VMEM = pl.BlockSpec(memory_space=pltpu.VMEM)
PARAMS = pltpu.CompilerParams(vmem_limit_bytes=16 * 1024 * 1024)


def cost(flops, bytes_accessed):
    return pl.CostEstimate(flops=flops, bytes_accessed=bytes_accessed, transcendentals=0)


def load_kernel(at, size, parts, pattern_ref, left_ref, arrived, *refs):
    out = refs[-1]
    done = 0
    for first, rows in parts:
        out[done : done + rows, :] = arrived[first : first + rows, :]
        done += rows
    step = math.gcd(TILE, math.gcd(at, size))
    for i in range(0, size, step):
        entry = pattern_ref[(at + i) // TILE].astype(jnp.float32).astype(out.dtype)
        out[done + i : done + i + step, :] = left_ref[at + i : at + i + step, :] * entry


def load(left, pattern, at, size, arrived, parts, after):
    columns = left.shape[1]
    total = size + sum(rows for _, rows in parts)
    return pl.pallas_call(
        functools.partial(load_kernel, at, size, parts),
        out_shape=jax.ShapeDtypeStruct((total, columns), left.dtype),
        in_specs=[pl.BlockSpec(memory_space=pltpu.SMEM), VMEM]
        + [VMEM if parts else pl.BlockSpec(memory_space=pl.ANY)]
        + [pl.BlockSpec(memory_space=pl.ANY)] * len(after),
        out_specs=VMEM,
        compiler_params=PARAMS,
        cost_estimate=cost(total * columns, 4 * total * columns),
    )(pattern, left, arrived, *after)


def mask_right_kernel(pattern_ref, values_ref, *refs):
    out = refs[-1]
    layers, rows, _ = out.shape
    for i in range(0, rows, TILE):
        block = jnp.swapaxes(values_ref[i : i + TILE].astype(jnp.float32), 0, 1)
        for j in range(layers):
            entry = pattern_ref[i // TILE, j].astype(jnp.float32)
            out[j, i : i + TILE, :] = (block[j] * entry).astype(out.dtype)


def mask_right(pattern, values, after):
    rows, layers, columns = values.shape
    return pl.pallas_call(
        mask_right_kernel,
        out_shape=jax.ShapeDtypeStruct((layers, rows, columns), values.dtype),
        in_specs=[pl.BlockSpec(memory_space=pltpu.SMEM), VMEM]
        + [pl.BlockSpec(memory_space=pl.ANY)] * len(after),
        out_specs=VMEM,
        compiler_params=PARAMS,
        cost_estimate=cost(values.size, 4 * values.size),
    )(pattern.reshape(rows // TILE, layers), values, *after)


def put_fixed(ref, at, total):
    rows, columns = total.shape
    top = jnp.maximum(jnp.max(jnp.abs(total), axis=0, keepdims=True), LEAST)
    code = jnp.ceil(jnp.log2(top) * CODE + 0.01)
    fixed = jnp.round(total * (jnp.exp2(code / -CODE) * TOP)).astype(jnp.int32)
    ref[at : at + rows, :] = fixed.astype(jnp.int16)
    codes = jnp.broadcast_to(code.astype(jnp.int32), (SCALE_ROWS, columns))
    ref[at + rows : at + rows + SCALE_ROWS, :] = codes.astype(jnp.int16)


def get_fixed(ref, at, rows):
    code = ref[at + rows : at + rows + SCALE_ROWS, :].astype(jnp.int32)[:1].astype(jnp.float32)
    unit = jnp.exp2(code / CODE) * (1.0 / TOP)
    return ref[at : at + rows, :].astype(jnp.int32).astype(jnp.float32) * unit


def partial_kernel(steps, sources, n_pieces, kept, sent, *refs):
    layer, row, col = (lax.axis_index(a) for a in ("layer", "row", "col"))
    n_cols = lax.axis_size("col")
    n_lefts = sum(len(parts) for parts in sources)
    pieces = refs[n_lefts : n_lefts + n_pieces]
    rows = sum(part[2] for part in sources[0])
    outs = refs[-len(kept) - len(sent) :]
    _, piece_rows, columns = pieces[0].shape

    def right(step, k):
        inner = lax.rem(col + (step + n_cols), n_cols) * TILE
        piece = lax.rem(row - lax.div(inner, piece_rows) + n_pieces, n_pieces)
        start = pl.multiple_of(lax.rem(inner, piece_rows), TILE)
        tile = pieces[0][layer ^ k, pl.ds(start, TILE), :]
        for i in range(1, n_pieces):
            tile = jnp.where(piece == i, pieces[i][layer ^ k, pl.ds(start, TILE), :], tile)
        return tile

    def product(k):
        total = jnp.zeros((rows, columns), jnp.float32)
        for step, parts in zip(steps, sources):
            tile = right(step, k)
            terms = [
                jnp.dot(
                    refs[i][first : first + count, :], tile, preferred_element_type=jnp.float32
                )
                for i, first, count in parts
            ]
            total += terms[0] if len(terms) == 1 else jnp.concatenate(terms, axis=0)
        return total

    for out, ks in zip(outs[len(kept) :], sent):
        for i, k in enumerate(ks):
            put_fixed(out, i * (rows + SCALE_ROWS), product(k))
    for out, k in zip(outs, kept):
        out[...] = product(k)


def partial_products(steps, sources, pieces, after, kept, sent):
    columns = pieces[0].shape[2]
    rows = sum(part[2] for part in sources[0])
    lefts = [array for parts in sources for array, _, _ in parts]
    numbers = iter(range(len(lefts)))
    shapes = tuple(tuple((next(numbers), *part[1:]) for part in parts) for parts in sources)
    n_products = len(kept) + sum(len(ks) for ks in sent)
    outs = [jax.ShapeDtypeStruct((rows, columns), jnp.float32)] * len(kept)
    outs += [
        jax.ShapeDtypeStruct((len(ks) * (rows + SCALE_ROWS), columns), jnp.int16) for ks in sent
    ]
    out = pl.pallas_call(
        functools.partial(
            partial_kernel, tuple(steps), shapes, len(pieces), kept, sent
        ),
        out_shape=outs,
        in_specs=[VMEM] * (len(lefts) + len(pieces))
        + [pl.BlockSpec(memory_space=pl.ANY)] * len(after),
        out_specs=[VMEM] * len(outs),
        compiler_params=PARAMS,
        cost_estimate=cost(
            2 * rows * len(sources) * TILE * columns * n_products,
            2 * len(pieces) * pieces[0].size + 14 * rows * columns,
        ),
    )(*lefts, *pieces, *after)
    return out[: len(kept)], out[len(kept) :]


def pass_on_kernel(kept_ref, received_ref, after_ref, out_ref):
    rows = kept_ref.shape[0]
    total = kept_ref[...] + get_fixed(received_ref, rows + SCALE_ROWS, rows)
    put_fixed(out_ref, 0, total)


def pass_on(kept, received, after):
    rows, columns = kept.shape
    return pl.pallas_call(
        pass_on_kernel,
        out_shape=jax.ShapeDtypeStruct((rows + SCALE_ROWS, columns), jnp.int16),
        in_specs=[VMEM, VMEM, pl.BlockSpec(memory_space=pl.ANY)],
        out_specs=VMEM,
        compiler_params=PARAMS,
        cost_estimate=cost(10 * kept.size, 8 * kept.size),
    )(kept, received, after)


def combine_kernel(n_received, n_before, kept_ref, *refs):
    received, before = refs[:n_received], refs[n_received : n_received + n_before]
    squared_ref, sum_ref = refs[-2:]
    total = kept_ref[...]
    for block in received:
        total += get_fixed(block, 0, total.shape[0])
    squared = total * total
    squared_ref[...] = squared
    column = jnp.sum(squared, axis=0, keepdims=True)
    for ref in before:
        column += ref[...]
    sum_ref[...] = column


def combine(kept, received, before, after):
    return pl.pallas_call(
        functools.partial(combine_kernel, len(received), len(before)),
        out_shape=(
            jax.ShapeDtypeStruct(kept.shape, jnp.float32),
            jax.ShapeDtypeStruct((1, kept.shape[1]), jnp.float32),
        ),
        in_specs=[VMEM] * (1 + len(received) + len(before)) + [pl.BlockSpec(memory_space=pl.ANY)] * len(after),
        out_specs=(VMEM, VMEM),
        compiler_params=PARAMS,
        cost_estimate=cost(8 * kept.size, 14 * kept.size),
    )(kept, *received, *before, *after)


def normalise_kernel(n_sums, rows_total, *refs):
    sums, chunks = refs[:n_sums], refs[n_sums:-3]
    out_ref, block, sems = refs[-3:]
    colmean = sum(ref[...] for ref in sums) / rows_total
    at, copies = 0, []
    for i, chunk in enumerate(chunks):
        rows = pl.ds(at, chunk.shape[0])
        block[rows, :] = (chunk[...] / (colmean + 1e-06)).astype(jnp.bfloat16)
        copies.append(pltpu.make_async_copy(block.at[rows], out_ref.at[rows], sems.at[i]))
        copies[-1].start()
        at += chunk.shape[0]
    for copy in copies:
        copy.wait()


def normalise(sums, chunks, rows_total):
    rows, columns = sum(chunk.shape[0] for chunk in chunks), chunks[0].shape[1]
    return pl.pallas_call(
        functools.partial(normalise_kernel, len(sums), rows_total),
        out_shape=jax.ShapeDtypeStruct((rows, columns), jnp.bfloat16),
        in_specs=[VMEM] * (len(sums) + len(chunks)),
        out_specs=pl.BlockSpec(memory_space=pl.ANY),
        scratch_shapes=[
            pltpu.VMEM((rows, columns), jnp.bfloat16),
            pltpu.SemaphoreType.DMA((len(chunks),)),
        ],
        compiler_params=PARAMS,
        cost_estimate=cost(4 * rows * columns, 6 * rows * columns),
    )(*sums, *chunks)


def shift(x, axis, by):
    n = lax.axis_size(axis)
    return lax.ppermute(x, axis, [(i, (i + by) % n) for i in range(n)])


def swap(x, bits):
    return lax.ppermute(x, "layer", [(i, i ^ bits) for i in range(4)])


def per_device(left_values, left_pattern, right_values, right_pattern):
    n_rows, n_cols = lax.axis_size("row"), lax.axis_size("col")
    rows_local, _, columns_local = left_values.shape
    sizes = [rows_local * part // sum(SIXTEENTHS) for part in SIXTEENTHS]

    left = left_values.reshape(rows_local, columns_local)
    pattern = left_pattern.reshape(-1)
    reach = n_cols // 2
    away = list(range(1, reach))
    steps = [0] + [-i for i in away] + away + [reach]

    starts = [sum(sizes[:i]) for i in range(len(sizes))]
    own = []
    found = [([], []) for _ in sizes]
    kept, received, last = [], [], []

    def open_slot(slot):
        at, size = (starts[slot], sizes[slot]) if slot < len(sizes) else (0, 0)
        for d in (0, 1):
            riders = [c for c in range(min(slot, len(sizes))) if len(found[c][d]) < reach]
            parts = []
            for c in riders:
                _, first, rows = found[c][d][-1]
                if len(found[c][d]) == reach - 1:
                    first, rows = first + d * (rows // 2), rows // 2
                parts.append((first, rows))
            arrived = found[riders[0]][d][-1][0] if riders else left
            if slot or d == 0:
                block = load(left, pattern, at, size, arrived, tuple(parts), last)
            last[:] = [block]
            got = shift(block, "col", 1 - 2 * d)
            first = 0
            for c, (_, rows) in zip(riders, parts):
                found[c][d].append((got, first, rows))
                first += rows
            if size:
                found[slot][d].append((got, first, size))
                if d == 0:
                    own.append((block, first, size))

    def sources(i):
        (*below, last_below), (*above, last_above) = found[i]
        return [[part] for part in [own[i]] + below + above] + [[last_below, last_above]]

    def direct(i):
        return i in (0, 1, len(sizes) - 1)

    def sum_chunk(i):
        if not direct(i):
            ks, sent_ks = (0, second(i)), ((3 - second(i), 3),)
        else:
            ks, sent_ks = (0,), ((3,), (1,), (2,))
        mine, sent = partial_products(steps, sources(i), pieces, last, ks, sent_ks)
        kept.append(mine)
        received.append([swap(x, k[0]) for x, k in zip(sent, sent_ks)])
        last[:] = [mine[0]]

    def second(i):
        return 2 - i % 2

    def send_on(i):
        block = pass_on(kept[i][1], received[i][0], last[0])
        received[i].append(swap(block, second(i)))
        last[:] = [block]

    raw = [(right_pattern, right_values)]
    for i in range(1, n_rows):
        raw.append((shift(right_pattern, "row", i), shift(right_values, "row", i)))
    pieces = []

    squares, columns = [], []

    def square(i):
        squared, column = combine(kept[i][0], received[i], columns[-1:], last)
        squares.append(squared)
        columns.append(column)
        last[:] = [column]

    opened = 0
    for i in range(len(sizes)):
        while opened < min(len(sizes) + reach - 1, i + reach + 1):
            open_slot(opened)
            opened += 1
            if opened == 2:
                for tiles, values in raw:
                    pieces.append(mask_right(tiles, values, last))
                    last[:] = pieces[-1:]
        if i in (1, 2):
            square(i - 1)
        sum_chunk(i)
        if i > 0 and not direct(i - 1):
            send_on(i - 1)
    for i in range(len(squares), len(sizes)):
        square(i)

    sums = columns[-1:] + [shift(columns[-1], "row", i) for i in range(1, n_rows)]
    out = normalise(sums, squares, rows_local * n_rows)
    return out.reshape(rows_local, 1, columns_local)


def solution(mesh):
    return jax.shard_map(
        per_device,
        mesh=mesh,
        in_specs=(
            P("row", "layer", "col"),
            P("row", "layer", "col"),
            P(("layer", "row"), None, "col"),
            P(("layer", "row"), None, "col"),
        ),
        out_specs=P("row", "layer", "col"),
        check_vma=False,
    )
```

```python
import functools
import math

import jax
import jax.numpy as jnp
from jax import lax
from jax.experimental import pallas as pl
from jax.experimental.pallas import tpu as pltpu
from jax.sharding import PartitionSpec as P

TILE = 256
SIXTEENTHS = (3, 4, 4, 3, 2)
SCALE_ROWS = 16
CODE = 64.0
TOP = 32767.0
LEAST = 2.0**-100
VMEM = pl.BlockSpec(memory_space=pltpu.VMEM)
PARAMS = pltpu.CompilerParams(vmem_limit_bytes=16 * 1024 * 1024)


def cost(flops, bytes_accessed):
    return pl.CostEstimate(flops=flops, bytes_accessed=bytes_accessed, transcendentals=0)


def load_kernel(at, size, parts, pattern_ref, left_ref, arrived, *refs):
    out = refs[-1]
    done = 0
    for first, rows in parts:
        out[done : done + rows, :] = arrived[first : first + rows, :]
        done += rows
    step = math.gcd(TILE, math.gcd(at, size))
    for i in range(0, size, step):
        entry = pattern_ref[(at + i) // TILE].astype(jnp.float32).astype(out.dtype)
        out[done + i : done + i + step, :] = left_ref[at + i : at + i + step, :] * entry


def load(left, pattern, at, size, arrived, parts, after):
    columns = left.shape[1]
    total = size + sum(rows for _, rows in parts)
    return pl.pallas_call(
        functools.partial(load_kernel, at, size, parts),
        out_shape=jax.ShapeDtypeStruct((total, columns), left.dtype),
        in_specs=[pl.BlockSpec(memory_space=pltpu.SMEM), VMEM]
        + [VMEM if parts else pl.BlockSpec(memory_space=pl.ANY)]
        + [pl.BlockSpec(memory_space=pl.ANY)] * len(after),
        out_specs=VMEM,
        compiler_params=PARAMS,
        cost_estimate=cost(total * columns, 4 * total * columns),
    )(pattern, left, arrived, *after)


def mask_right_kernel(pattern_ref, values_ref, *refs):
    out = refs[-1]
    layers, rows, _ = out.shape
    for i in range(0, rows, TILE):
        block = jnp.swapaxes(values_ref[i : i + TILE].astype(jnp.float32), 0, 1)
        for j in range(layers):
            entry = pattern_ref[i // TILE, j].astype(jnp.float32)
            out[j, i : i + TILE, :] = (block[j] * entry).astype(out.dtype)


def mask_right(pattern, values, after):
    rows, layers, columns = values.shape
    return pl.pallas_call(
        mask_right_kernel,
        out_shape=jax.ShapeDtypeStruct((layers, rows, columns), values.dtype),
        in_specs=[pl.BlockSpec(memory_space=pltpu.SMEM), VMEM]
        + [pl.BlockSpec(memory_space=pl.ANY)] * len(after),
        out_specs=VMEM,
        compiler_params=PARAMS,
        cost_estimate=cost(values.size, 4 * values.size),
    )(pattern.reshape(rows // TILE, layers), values, *after)


def put_fixed(ref, at, total):
    rows, columns = total.shape
    top = jnp.maximum(jnp.max(jnp.abs(total), axis=0, keepdims=True), LEAST)
    code = jnp.ceil(jnp.log2(top) * CODE + 0.01)
    fixed = jnp.round(total * (jnp.exp2(code / -CODE) * TOP)).astype(jnp.int32)
    ref[at : at + rows, :] = fixed.astype(jnp.int16)
    codes = jnp.broadcast_to(code.astype(jnp.int32), (SCALE_ROWS, columns))
    ref[at + rows : at + rows + SCALE_ROWS, :] = codes.astype(jnp.int16)


def get_fixed(ref, at, rows):
    code = ref[at + rows : at + rows + SCALE_ROWS, :].astype(jnp.int32)[:1].astype(jnp.float32)
    unit = jnp.exp2(code / CODE) * (1.0 / TOP)
    return ref[at : at + rows, :].astype(jnp.int32).astype(jnp.float32) * unit


def partial_kernel(steps, sources, n_pieces, kept, sent, *refs):
    layer, row, col = (lax.axis_index(a) for a in ("layer", "row", "col"))
    n_cols = lax.axis_size("col")
    n_lefts = sum(len(parts) for parts in sources)
    pieces = refs[n_lefts : n_lefts + n_pieces]
    rows = sum(part[2] for part in sources[0])
    outs = refs[-len(kept) - len(sent) :]
    _, piece_rows, columns = pieces[0].shape

    def right(step, k):
        inner = lax.rem(col + (step + n_cols), n_cols) * TILE
        piece = lax.rem(row - lax.div(inner, piece_rows) + n_pieces, n_pieces)
        start = pl.multiple_of(lax.rem(inner, piece_rows), TILE)
        tile = pieces[0][layer ^ k, pl.ds(start, TILE), :]
        for i in range(1, n_pieces):
            tile = jnp.where(piece == i, pieces[i][layer ^ k, pl.ds(start, TILE), :], tile)
        return tile

    def product(k):
        total = jnp.zeros((rows, columns), jnp.float32)
        for step, parts in zip(steps, sources):
            tile = right(step, k)
            terms = [
                jnp.dot(
                    refs[i][first : first + count, :], tile, preferred_element_type=jnp.float32
                )
                for i, first, count in parts
            ]
            total += terms[0] if len(terms) == 1 else jnp.concatenate(terms, axis=0)
        return total

    for out, ks in zip(outs[len(kept) :], sent):
        for i, k in enumerate(ks):
            put_fixed(out, i * (rows + SCALE_ROWS), product(k))
    for out, k in zip(outs, kept):
        out[...] = product(k)


def partial_products(steps, sources, pieces, after, kept, sent):
    columns = pieces[0].shape[2]
    rows = sum(part[2] for part in sources[0])
    lefts = [array for parts in sources for array, _, _ in parts]
    numbers = iter(range(len(lefts)))
    shapes = tuple(tuple((next(numbers), *part[1:]) for part in parts) for parts in sources)
    n_products = len(kept) + sum(len(ks) for ks in sent)
    outs = [jax.ShapeDtypeStruct((rows, columns), jnp.float32)] * len(kept)
    outs += [
        jax.ShapeDtypeStruct((len(ks) * (rows + SCALE_ROWS), columns), jnp.int16) for ks in sent
    ]
    out = pl.pallas_call(
        functools.partial(
            partial_kernel, tuple(steps), shapes, len(pieces), kept, sent
        ),
        out_shape=outs,
        in_specs=[VMEM] * (len(lefts) + len(pieces))
        + [pl.BlockSpec(memory_space=pl.ANY)] * len(after),
        out_specs=[VMEM] * len(outs),
        compiler_params=PARAMS,
        cost_estimate=cost(
            2 * rows * len(sources) * TILE * columns * n_products,
            2 * len(pieces) * pieces[0].size + 14 * rows * columns,
        ),
    )(*lefts, *pieces, *after)
    return out[: len(kept)], out[len(kept) :]


def pass_on_kernel(kept_ref, received_ref, after_ref, out_ref):
    rows = kept_ref.shape[0]
    total = kept_ref[...] + get_fixed(received_ref, rows + SCALE_ROWS, rows)
    put_fixed(out_ref, 0, total)


def pass_on(kept, received, after):
    rows, columns = kept.shape
    return pl.pallas_call(
        pass_on_kernel,
        out_shape=jax.ShapeDtypeStruct((rows + SCALE_ROWS, columns), jnp.int16),
        in_specs=[VMEM, VMEM, pl.BlockSpec(memory_space=pl.ANY)],
        out_specs=VMEM,
        compiler_params=PARAMS,
        cost_estimate=cost(10 * kept.size, 8 * kept.size),
    )(kept, received, after)


def combine_kernel(n_received, n_before, kept_ref, *refs):
    received, before = refs[:n_received], refs[n_received : n_received + n_before]
    squared_ref, sum_ref = refs[-2:]
    total = kept_ref[...]
    for block in received:
        total += get_fixed(block, 0, total.shape[0])
    squared = total * total
    squared_ref[...] = squared
    column = jnp.sum(squared, axis=0, keepdims=True)
    for ref in before:
        column += ref[...]
    sum_ref[...] = column


def combine(kept, received, before, after):
    return pl.pallas_call(
        functools.partial(combine_kernel, len(received), len(before)),
        out_shape=(
            jax.ShapeDtypeStruct(kept.shape, jnp.float32),
            jax.ShapeDtypeStruct((1, kept.shape[1]), jnp.float32),
        ),
        in_specs=[VMEM] * (1 + len(received) + len(before)) + [pl.BlockSpec(memory_space=pl.ANY)] * len(after),
        out_specs=(VMEM, VMEM),
        compiler_params=PARAMS,
        cost_estimate=cost(8 * kept.size, 14 * kept.size),
    )(kept, *received, *before, *after)


def normalise_kernel(n_sums, rows_total, *refs):
    sums, chunks = refs[:n_sums], refs[n_sums:-3]
    out_ref, block, sems = refs[-3:]
    colmean = sum(ref[...] for ref in sums) / rows_total
    at, copies = 0, []
    for i, chunk in enumerate(chunks):
        rows = pl.ds(at, chunk.shape[0])
        block[rows, :] = (chunk[...] / (colmean + 1e-06)).astype(jnp.bfloat16)
        copies.append(pltpu.make_async_copy(block.at[rows], out_ref.at[rows], sems.at[i]))
        copies[-1].start()
        at += chunk.shape[0]
    for copy in copies:
        copy.wait()


def normalise(sums, chunks, rows_total):
    rows, columns = sum(chunk.shape[0] for chunk in chunks), chunks[0].shape[1]
    return pl.pallas_call(
        functools.partial(normalise_kernel, len(sums), rows_total),
        out_shape=jax.ShapeDtypeStruct((rows, columns), jnp.bfloat16),
        in_specs=[VMEM] * (len(sums) + len(chunks)),
        out_specs=pl.BlockSpec(memory_space=pl.ANY),
        scratch_shapes=[
            pltpu.VMEM((rows, columns), jnp.bfloat16),
            pltpu.SemaphoreType.DMA((len(chunks),)),
        ],
        compiler_params=PARAMS,
        cost_estimate=cost(4 * rows * columns, 6 * rows * columns),
    )(*sums, *chunks)


def shift(x, axis, by):
    n = lax.axis_size(axis)
    return lax.ppermute(x, axis, [(i, (i + by) % n) for i in range(n)])


def swap(x, bits):
    return lax.ppermute(x, "layer", [(i, i ^ bits) for i in range(4)])


def per_device(left_values, left_pattern, right_values, right_pattern):
    n_rows, n_cols = lax.axis_size("row"), lax.axis_size("col")
    rows_local, _, columns_local = left_values.shape
    sizes = [rows_local * part // sum(SIXTEENTHS) for part in SIXTEENTHS]

    left = left_values.reshape(rows_local, columns_local)
    pattern = left_pattern.reshape(-1)
    reach = n_cols // 2
    away = list(range(1, reach))
    steps = [0] + [-i for i in away] + away + [reach]

    starts = [sum(sizes[:i]) for i in range(len(sizes))]
    own = []
    found = [([], []) for _ in sizes]
    kept, received, last = [], [], []

    def open_slot(slot):
        at, size = (starts[slot], sizes[slot]) if slot < len(sizes) else (0, 0)
        for d in (0, 1):
            riders = [c for c in range(min(slot, len(sizes))) if len(found[c][d]) < reach]
            parts = []
            for c in riders:
                _, first, rows = found[c][d][-1]
                if len(found[c][d]) == reach - 1:
                    first, rows = first + d * (rows // 2), rows // 2
                parts.append((first, rows))
            arrived = found[riders[0]][d][-1][0] if riders else left
            if slot or d == 0:
                block = load(left, pattern, at, size, arrived, tuple(parts), last)
            last[:] = [block]
            got = shift(block, "col", 1 - 2 * d)
            first = 0
            for c, (_, rows) in zip(riders, parts):
                found[c][d].append((got, first, rows))
                first += rows
            if size:
                found[slot][d].append((got, first, size))
                if d == 0:
                    own.append((block, first, size))

    def sources(i):
        (*below, last_below), (*above, last_above) = found[i]
        return [[part] for part in [own[i]] + below + above] + [[last_below, last_above]]

    def direct(i):
        return i in (0, 1, len(sizes) - 1)

    def sum_chunk(i):
        if not direct(i):
            ks, sent_ks = (0, second(i)), ((3 - second(i), 3),)
        else:
            ks, sent_ks = (0,), ((3,), (1,), (2,))
        mine, sent = partial_products(steps, sources(i), pieces, last, ks, sent_ks)
        kept.append(mine)
        received.append([swap(x, k[0]) for x, k in zip(sent, sent_ks)])
        last[:] = [mine[0]]

    def second(i):
        return 2 - i % 2

    def send_on(i):
        block = pass_on(kept[i][1], received[i][0], last[0])
        received[i].append(swap(block, second(i)))
        last[:] = [block]

    raw = [(right_pattern, right_values)]
    for i in range(1, n_rows):
        raw.append((shift(right_pattern, "row", i), shift(right_values, "row", i)))
    pieces = []

    squares, columns = [], []

    def square(i):
        squared, column = combine(kept[i][0], received[i], columns[-1:], last)
        squares.append(squared)
        columns.append(column)
        last[:] = [column]

    opened = 0
    for i in range(len(sizes)):
        while opened < min(len(sizes) + reach - 1, i + reach + 1):
            open_slot(opened)
            opened += 1
            if opened == 2:
                for tiles, values in raw:
                    pieces.append(mask_right(tiles, values, last))
                    last[:] = pieces[-1:]
        if i in (1, 2):
            square(i - 1)
        sum_chunk(i)
        if i + 1 == len(sizes):
            for j in range(len(sizes)):
                if not direct(j):
                    send_on(j)
    for i in range(len(squares), len(sizes)):
        square(i)

    sums = columns[-1:] + [shift(columns[-1], "row", i) for i in range(1, n_rows)]
    out = normalise(sums, squares, rows_local * n_rows)
    return out.reshape(rows_local, 1, columns_local)


def solution(mesh):
    return jax.shard_map(
        per_device,
        mesh=mesh,
        in_specs=(
            P("row", "layer", "col"),
            P("row", "layer", "col"),
            P(("layer", "row"), None, "col"),
            P(("layer", "row"), None, "col"),
        ),
        out_specs=P("row", "layer", "col"),
        check_vma=False,
    )
```
